32 devices in a mesh: dp: 8 (over z, y), row: 2 (over x), col: 2 (over core).
Axes of the slice: x: 2, y: 2, z: 4, core: 2. Of those that a mesh axis runs over, the one named last changes fastest.
Arguments:
- tokens: bfloat16 [10240, 1536], P(('dp', 'row', 'col')), may hold values from -6 to 6
- attn_gain: float32 [1536], replicated, may hold values from 0.1 to 1.9
- query_weight: bfloat16 [1536, 1536], P(None, ('row', 'col')), may hold values from -0.15625 to 0.15625
- key_weight: bfloat16 [1536, 512], P(None, ('row', 'col')), may hold values from -0.15625 to 0.15625
- value_weight: bfloat16 [1536, 512], P(None, ('row', 'col')), may hold values from -0.15625 to 0.15625
- out_weight: bfloat16 [1536, 1536], P(('row', 'col')), may hold values from -2.5 to 2.5
- mlp_gain: float32 [1536], replicated, may hold values from 0.1 to 1.9
- router_weight: bfloat16 [1536, 16], replicated, may hold values from -0.078125 to 0.078125
- gate_weight: bfloat16 [16, 1536, 512], P('dp', None, ('row', 'col')), may hold values from -0.15625 to 0.15625
- up_weight: bfloat16 [16, 1536, 512], P('dp', None, ('row', 'col')), may hold values from -0.15625 to 0.15625
- down_weight: bfloat16 [16, 512, 1536], P('dp', ('row', 'col')), may hold values from -0.75 to 0.75
- output_grad: bfloat16 [10240, 1536], P(('dp', 'row', 'col')), may hold values from -6 to 6
- expert_ids: int32 [10240, 8], P(('dp', 'row', 'col')), may hold values from 0 to 15, all different within a row
- slot_rank: int32 [10240, 8], P(('dp', 'row', 'col')), may hold values from 0 to 2559, as said below
- segment_ids: int32 [10240], P(('dp', 'row', 'col')), may hold values from 0 to 12, as said below
- parent_ids: int32 [10240], P(('dp', 'row', 'col')), may hold values from 0 to 4, as said below
Outputs:
- output: bfloat16 [10240, 1536], P(('dp', 'row', 'col'))
- input_grad: float32 [10240, 1536], P(('dp', 'row', 'col'))
- attn_gain_grad: float32 [1536], replicated
- query_grad: float32 [1536, 1536], P(None, ('row', 'col'))
- key_grad: float32 [1536, 512], P(None, ('row', 'col'))
- value_grad: float32 [1536, 512], P(None, ('row', 'col'))
- out_grad: float32 [1536, 1536], P(('row', 'col'))
- mlp_gain_grad: float32 [1536], replicated
- router_grad: float32 [1536, 16], replicated
- gate_grad: float32 [16, 1536, 512], P('dp', None, ('row', 'col'))
- up_grad: float32 [16, 1536, 512], P('dp', None, ('row', 'col'))
- down_grad: float32 [16, 512, 1536], P('dp', ('row', 'col'))
The draws below stay inside these ranges and needn't reach their ends.
Inputs may be any that keep to these rules, and one draw needn't show every extreme that they name: `segment_ids`: within each aligned block of 1280 tokens (one tree), segment 0 (the trunk) holds the first 512 tokens; segments 1 to 4 (branches) and 5 to 12 (leaves) hold 64 consecutive tokens each, in an order that varies. `parent_ids`: each token's segment's parent: 0 for the trunk and the branches, a branch for a leaf; each branch is the parent of two leaves; equal for all tokens of a segment. `slot_rank`: over the 320 rows of one device, a permutation of 0 to 2559.
All inputs are finite; a program needn't handle non-finite values.
Results may differ from the reference program's by a relative error of at most 0.019.
Values may be sent and summed in bfloat16 or wider, within the bound.
No kernel may reach another device: no remote copies, remote signals or barrier semaphores. Data moves between devices by JAX's collectives and lax.ppermute only.
A program may use at most 256 MiB of HBM per device.

```python
import math
import jax
import jax.numpy as jnp
from jax import lax

D = 1536
HQ = 24
HK = 8
HD = 64
FE = 512
TOPK = 8
TOK_DEV = 320
EXPERTS = 16
TREE = 1280
SEG = 64
TRUNK = 512
TOKENS = 10240
CAP = 200


def tree_layout(key):
    tree_count = TOKENS // TREE
    key_list = jax.random.split(key, tree_count)

    def one_tree(tree_key):
        order_key, leaf_key = jax.random.split(tree_key)
        labels = jnp.concatenate([jnp.zeros((1,), jnp.int32), 1 + jax.random.permutation(order_key, 12).astype(jnp.int32)])
        leaf_owner = 1 + jax.random.permutation(leaf_key, 8).astype(jnp.int32) // 2
        parent_table = jnp.concatenate([jnp.zeros((5,), jnp.int32), leaf_owner])
        position = jnp.arange(TREE, dtype=jnp.int32)
        block_number = jnp.where(position < TRUNK, 0, 1 + (position - TRUNK) // SEG)
        segment = labels[block_number]
        return (segment, parent_table[segment])
    segment, parent = jax.vmap(one_tree)(key_list)
    return (segment.reshape(-1), parent.reshape(-1))


def draw_segment_ids(key, part):
    return tree_layout(key)[0]


def draw_parent_ids(key, part):
    return tree_layout(key)[1]


def draw_slot_rank(key, part):
    key = jax.random.fold_in(key, 7)
    key_list = jax.random.split(key, TOKENS // TOK_DEV)

    def one_device(device_key):
        return jax.random.permutation(device_key, TOK_DEV * TOPK).astype(jnp.int32)
    ranking = jax.vmap(one_device)(key_list)
    return ranking.reshape(TOKENS, TOPK)


def block_scale(stream_key, extent, cuts, smallest, high):
    def one(dim, shards_of):
        draws = jax.random.uniform(jax.random.fold_in(jax.random.fold_in(stream_key, 6), dim), (shards_of,), jnp.float32, smallest / len(cuts), high / len(cuts))
        return jnp.repeat(jnp.exp(draws), extent[dim] // shards_of).reshape((-1,) + (1,) * (len(extent) - dim - 1))

    gain = one(*cuts[0])
    for cut in cuts[1:]:
        gain = gain * one(*cut)
    return gain


def picks_of(own_key, rows, amount, top, lift):
    sequence = jax.random.permutation(jax.random.fold_in(own_key, 1), amount)
    boost = sequence
    for power in range(3):
        boost = boost * boost // amount
    boost = boost * lift // amount
    chance = jax.random.randint(jax.random.fold_in(own_key, 2), (rows, amount), 0, 4096) + boost
    holders = jax.random.permutation(jax.random.fold_in(own_key, 3), rows)[jnp.arange(amount) % rows]
    chance = jnp.where(jnp.arange(rows)[:, None] == holders[None, :], 1 << 14, chance)
    priority = chance * amount + jnp.arange(amount)
    return lax.top_k(priority.astype(jnp.int32), top)[1].astype(jnp.int32)


def bell_draw(stream_key, shape, width, limit, shards=(), held_as=jnp.bfloat16):
    values = jax.random.normal(stream_key, shape, jnp.float32) * width
    if len(shards) > 0:
        values = block_scale(stream_key, shape, shards, -0.22, 0.18) * values
    return jnp.clip(values, min=-limit, max=limit).astype(held_as)


def setup_inputs(seed: int = 0) -> dict:
    streams_of = jax.random.split(jax.random.key(seed), 17)
    tokens = bell_draw(streams_of[0], (TOKENS, D), 1.0, 6.0, ((0, 32),))
    attn_gain = jnp.clip(1.0 + 0.18 * jax.random.normal(streams_of[1], (D,), jnp.float32), 0.1, 1.9)
    query_weight = bell_draw(streams_of[2], (D, HQ * HD), D ** -0.5, 0.15625, ((1, 4),))
    key_weight = bell_draw(streams_of[3], (D, HK * HD), D ** -0.5, 0.15625, ((1, 4),))
    value_weight = bell_draw(streams_of[4], (D, HK * HD), D ** -0.5, 0.15625, ((1, 4),))
    out_weight = bell_draw(streams_of[5], (HQ * HD, D), (max(HQ * HD // 256, 1)) ** -0.5, 2.5, ((0, 4),))
    mlp_gain = jnp.clip(1.0 + 0.18 * jax.random.normal(streams_of[6], (D,), jnp.float32), 0.1, 1.9)
    router_weight = bell_draw(streams_of[7], (D, EXPERTS), (4 * D) ** -0.5, 0.078125)
    gate_weight = bell_draw(streams_of[8], (EXPERTS, D, FE), D ** -0.5, 0.15625, ((0, 8), (2, 4)))
    up_weight = bell_draw(streams_of[9], (EXPERTS, D, FE), D ** -0.5, 0.15625, ((0, 8), (2, 4)))
    down_weight = bell_draw(streams_of[10], (EXPERTS, FE, D), (FE // 8) ** -0.5, 0.75, ((0, 8), (1, 4)))
    output_grad = bell_draw(streams_of[11], (TOKENS, D), 1.0, 6.0, ((0, 32),))
    expert_ids = picks_of(streams_of[12], TOKENS, EXPERTS, TOPK, 4096)
    slot_rank = draw_slot_rank(jax.random.fold_in(streams_of[16], 71), 0)
    segment_ids = draw_segment_ids(jax.random.fold_in(streams_of[16], 71), 0)
    parent_ids = draw_parent_ids(jax.random.fold_in(streams_of[16], 71), 0)
    return dict(tokens=tokens, attn_gain=attn_gain, query_weight=query_weight, key_weight=key_weight, value_weight=value_weight, out_weight=out_weight, mlp_gain=mlp_gain, router_weight=router_weight, gate_weight=gate_weight, up_weight=up_weight, down_weight=down_weight, output_grad=output_grad, expert_ids=expert_ids, slot_rank=slot_rank, segment_ids=segment_ids, parent_ids=parent_ids)


EPS = 1e-05
HIGHEST = lax.Precision.HIGHEST
segment_count = 13

@jax.custom_vjp
def low(v):
    return lax.optimization_barrier(v.astype(jnp.bfloat16)).astype(jnp.float32)

@jax.custom_vjp
def low_back(v):
    return v

def low_keep(v):
    return (low(v), None)

def low_pass(kept, grad):
    return (grad,)

def back_keep(v):
    return (v, None)

def back_low(kept, grad):
    return (low(grad),)
low.defvjp(low_keep, low_pass)
low_back.defvjp(back_keep, back_low)

def product(left, right):
    return jnp.dot(left, right, precision=HIGHEST, preferred_element_type=jnp.float32)

def grand_parents(segment, parent):
    labels = jnp.arange(segment_count, dtype=jnp.int32)
    parent_table = lax.optimization_barrier(jnp.max(jnp.where(segment[None, :] == labels[:, None], parent[None, :], 0), axis=1))
    return lax.optimization_barrier(jnp.sum(jnp.where(parent[:, None] == labels[None, :], parent_table[None, :], 0), axis=1))

def visible_pairs(query_segment, query_parent, query_grand, query_position, segment, position):
    key_segment = segment[None, :]
    same_segment = (key_segment == query_segment[:, None]) & (position[None, :] <= query_position[:, None])
    from_parent = (key_segment == query_parent[:, None]) & (key_segment != query_segment[:, None])
    from_grand = (key_segment == query_grand[:, None]) & (key_segment != query_segment[:, None]) & (key_segment != query_parent[:, None])
    return same_segment | from_parent | from_grand

def slot_tables(operands):
    tree_experts, tree_ranks = operands
    blocks = TREE // TOK_DEV
    flat_expert = tree_experts.reshape(blocks, TOK_DEV * TOPK)
    flat_rank = tree_ranks.reshape(blocks, TOK_DEV * TOPK)
    earlier = (flat_expert[:, None, :] == flat_expert[:, :, None]) & (flat_rank[:, None, :] < flat_rank[:, :, None])
    slot_number = lax.optimization_barrier(jnp.sum(earlier.astype(jnp.int32), axis=2))
    block_number = jnp.arange(blocks, dtype=jnp.int32)[:, None]
    row_span = blocks * CAP
    target = jnp.where(slot_number < CAP, flat_expert * row_span + block_number * CAP + slot_number, EXPERTS * row_span)
    pair_index = jnp.arange(blocks * TOK_DEV * TOPK, dtype=jnp.int32)
    slot_table = jnp.full((EXPERTS * row_span,), TREE * TOPK, jnp.int32).at[target.reshape(-1)].set(pair_index, mode='drop')
    is_valid = (slot_table < TREE * TOPK).astype(jnp.float32)
    slot_table = jnp.minimum(slot_table, TREE * TOPK - 1)
    return ((slot_table // TOPK).reshape(EXPERTS, row_span), (slot_table % TOPK).reshape(EXPERTS, row_span), is_valid.reshape(EXPERTS, row_span))

def tree_forward(params, tokens, segment, parent, token_table, choice_table, valid_table, tree_experts):
    attn_gain, query_weight, key_weight, value_weight, out_weight, mlp_gain, router_weight, gate_weight, up_weight, down_weight = params
    score_scale = 1.0 / math.sqrt(HD)
    scale_attn = lax.rsqrt(lax.optimization_barrier(jnp.mean(tokens * tokens, axis=-1, keepdims=True)) + EPS)
    normed = low(tokens * scale_attn * attn_gain)
    queries = low(low_back(product(normed, query_weight)))
    key_rows = low(low_back(product(normed, key_weight)))
    value_rows = low(low_back(product(normed, value_weight)))
    position = jnp.arange(TREE, dtype=jnp.int32)
    grand = grand_parents(segment, parent)
    visible = visible_pairs(segment, parent, grand, position, segment, position)
    per_group = HQ // HK
    query_heads = jnp.transpose(queries.reshape(TREE, HK, per_group, HD), (1, 0, 2, 3))
    key_heads = jnp.transpose(key_rows.reshape(TREE, HK, HD), (1, 0, 2))
    value_heads = jnp.transpose(value_rows.reshape(TREE, HK, HD), (1, 0, 2))

    def group_attention(operands):
        query_group, key_group, value_group = operands
        scores = low_back(jnp.einsum('qrd,kd->rqk', query_group, key_group, precision=HIGHEST) * score_scale)
        masked = jnp.where(visible[None], scores, -jnp.inf)
        row_max = lax.optimization_barrier(jnp.max(masked, axis=-1, keepdims=True))
        weights = jnp.exp(masked - row_max)
        probs = low(weights / lax.optimization_barrier(jnp.sum(weights, axis=-1, keepdims=True)))
        return jnp.einsum('rqk,kd->qrd', probs, value_group, precision=HIGHEST)
    heads = lax.map(jax.checkpoint(group_attention), (query_heads, key_heads, value_heads))
    heads = low(low_back(jnp.transpose(heads, (1, 0, 2, 3)).reshape(TREE, HQ * HD)))
    attn_result = low_back(product(heads, out_weight))
    hidden = tokens + attn_result
    scale_mlp = lax.rsqrt(lax.optimization_barrier(jnp.mean(hidden * hidden, axis=-1, keepdims=True)) + EPS)
    mlp_in = low(hidden * scale_mlp * mlp_gain)
    logits = low_back(product(mlp_in, router_weight))
    chosen = jnp.take_along_axis(logits, tree_experts, axis=1)
    chosen_max = lax.optimization_barrier(jnp.max(chosen, axis=1, keepdims=True))
    chosen_exp = jnp.exp(chosen - chosen_max)
    gates = chosen_exp / lax.optimization_barrier(jnp.sum(chosen_exp, axis=1, keepdims=True))
    expert_rows = low_back(mlp_in[token_table] * valid_table[..., None])
    gate_pre = low_back(jnp.einsum('erd,edf->erf', expert_rows, gate_weight, precision=HIGHEST))
    up_pre = low_back(jnp.einsum('erd,edf->erf', expert_rows, up_weight, precision=HIGHEST))
    activated = low(jax.nn.silu(gate_pre) * up_pre)
    expert_out = low(low_back(jnp.einsum('erf,efd->erd', activated, down_weight, precision=HIGHEST)))
    slot_weight = gates[token_table, choice_table] * valid_table
    mixture = jnp.zeros((TREE, D), jnp.float32).at[token_table.reshape(-1)].add((slot_weight[..., None] * expert_out).reshape(-1, D))
    return hidden + mixture

def reference(tokens, attn_gain, query_weight, key_weight, value_weight, out_weight, mlp_gain, router_weight, gate_weight, up_weight, down_weight, output_grad, expert_ids, slot_rank, segment_ids, parent_ids):
    tree_count = TOKENS // TREE
    tree_experts = expert_ids.reshape(tree_count, TREE, TOPK)
    token_table, choice_table, valid_table = lax.map(slot_tables, (tree_experts, slot_rank.reshape(tree_count, TREE, TOPK)))
    params = tuple((weight.astype(jnp.float32) for weight in (attn_gain, query_weight, key_weight, value_weight, out_weight, mlp_gain, router_weight, gate_weight, up_weight, down_weight)))
    tree_inputs = (segment_ids.reshape(tree_count, TREE), parent_ids.reshape(tree_count, TREE), token_table, choice_table, valid_table, tree_experts)

    def whole(weights, token_values):

        def step(running, operands):
            tree_tokens, segment, parent, tokens_of_slots, choices_of_slots, valid_slots, experts_of_tree = operands
            return (running, tree_forward(weights, tree_tokens, segment, parent, tokens_of_slots, choices_of_slots, valid_slots, experts_of_tree))
        final_state, outputs = lax.scan(jax.checkpoint(step), jnp.zeros((), jnp.float32), (token_values.reshape(tree_count, TREE, D),) + tree_inputs)
        return outputs.reshape(TOKENS, D)
    result, pullback = jax.vjp(whole, params, tokens.astype(jnp.float32))
    weight_grads, input_grad = pullback(output_grad.astype(jnp.float32))
    return (result.astype(jnp.bfloat16), input_grad, weight_grads[0], weight_grads[1], weight_grads[2], weight_grads[3], weight_grads[4], weight_grads[5], weight_grads[6], weight_grads[7], weight_grads[8], weight_grads[9])
```

```python
import functools
import math

import jax
import jax.numpy as jnp
from jax import lax
from jax.experimental import pallas as pl
from jax.experimental.pallas import tpu as pltpu
from jax.sharding import PartitionSpec as P

HD = 64
TOPK = 8
QT = 128
EPS = 1e-05
NEG = -1e30
MIB = 2**20
BF = jnp.bfloat16
F32 = jnp.float32
VMEM = pl.BlockSpec(memory_space=pltpu.VMEM)
SMEM = pl.BlockSpec(memory_space=pltpu.SMEM)


def dot(a, b, ca, cb):
    return lax.dot_general(a, b, (((ca,), (cb,)), ((), ())), preferred_element_type=F32)


def after(value, *earlier):
    return lax.optimization_barrier((value,) + earlier)[0]


def stack_heads(block, count):
    return jnp.concatenate([block[:, h * HD : (h + 1) * HD] for h in range(count)], axis=0)


def causal_mask(per_group):
    key = lax.broadcasted_iota(jnp.int32, (QT, QT), 0)
    query = lax.broadcasted_iota(jnp.int32, (QT, QT), 1)
    return jnp.concatenate([key <= query] * per_group, axis=1)


def tile_masks(seg, parents, per_group):
    key = lax.broadcasted_iota(jnp.int32, (QT, QT), 0)
    query = lax.broadcasted_iota(jnp.int32, (QT, QT), 1)
    own = (key <= query) & (key // seg == query // seg)
    par = None
    for j, parent in enumerate(parents):
        hit = (key // seg == j) & (query // seg == j) & (parent > 0)
        par = hit if par is None else par | hit
    return (
        jnp.concatenate([own] * per_group, axis=1),
        jnp.concatenate([par] * per_group, axis=1),
    )


def softmax_parts(keys, masks, q):
    parts = []
    top = None
    for k, mask in zip(keys, masks):
        s = dot(k, q, 1, 1)
        if mask is not None:
            s = jnp.where(mask, s, NEG)
        parts.append(s)
        m = jnp.max(s, axis=0, keepdims=True)
        top = m if top is None else jnp.maximum(top, m)
    probs = []
    total = None
    for s in parts:
        e = jnp.exp(s - top)
        t = jnp.sum(e, axis=0, keepdims=True)
        total = t if total is None else total + t
        probs.append(e)
    inverse = 1.0 / total
    return [e * inverse for e in probs]


def each_tile(qkv_ref, parent_ref, kv, per_group, seg, work):
    rows = qkv_ref.shape[0]
    trunk = 8 * seg
    segs = QT // seg
    q_width = kv * per_group * HD
    causal = causal_mask(per_group)

    def columns(g):
        return q_width + g * HD, q_width + kv * HD + g * HD

    for i in range(trunk // QT):
        for g in range(kv):
            kc, vc = columns(g)
            spans = ([(0, i * QT)] if i > 0 else []) + [(i * QT, QT)]
            keys = [qkv_ref[a : a + n, kc : kc + HD] for a, n in spans]
            values = [qkv_ref[a : a + n, vc : vc + HD] for a, n in spans]
            masks = ([None] if i > 0 else []) + [causal]
            work(i * QT, g, keys, values, masks, [[s] for s in spans])

    def body(i, carry):
        first = pl.multiple_of(trunk + i * QT, QT)
        parents = [parent_ref[8 + i * segs + j] for j in range(segs)]
        starts = [pl.multiple_of(p * seg, seg) for p in parents]
        own, par = tile_masks(seg, parents, per_group)

        def take(c):
            blocks = [qkv_ref[pl.ds(s, seg), c : c + HD] for s in starts]
            return [
                qkv_ref[0:trunk, c : c + HD],
                qkv_ref[pl.ds(first, QT), c : c + HD],
                jnp.concatenate(blocks, axis=0) if segs > 1 else blocks[0],
            ]

        for g in range(kv):
            kc, vc = columns(g)
            places = [[(0, trunk)], [(first, QT)], [(s, seg) for s in starts]]
            work(first, g, take(kc), take(vc), [None, own, par], places)
        return carry

    lax.fori_loop(0, (rows - trunk) // QT, body, 0)


def attend_forward_kernel(kv, per_group, seg, blocks, shard_ref, parent_ref, *refs):
    ins, (qkv_ref, out_ref, full_ref) = refs[:blocks], refs[blocks:]
    local = ins[0].shape[0]
    scale = BF(1.0 / math.sqrt(HD))
    for j in range(blocks):
        at = pl.multiple_of(shard_ref[j] * local, 64)
        qkv_ref[pl.ds(at, local), :] = ins[j][...]

    def work(first, g, keys, values, masks, places):
        block = qkv_ref[pl.ds(first, QT), g * per_group * HD : (g + 1) * per_group * HD]
        probs = softmax_parts(keys, masks, stack_heads(block, per_group) * scale)
        total = None
        for p, v in zip(probs, values):
            o = dot(v, p.astype(BF), 0, 0)
            total = o if total is None else total + o
        for h in range(per_group):
            c = (g * per_group + h) * HD
            full_ref[pl.ds(first, QT), c : c + HD] = total[:, h * QT : (h + 1) * QT].T.astype(BF)

    each_tile(qkv_ref, parent_ref, kv, per_group, seg, work)
    for j in range(blocks):
        at = pl.multiple_of(shard_ref[j] * local, 64)
        out_ref[j * local : (j + 1) * local, :] = full_ref[pl.ds(at, local), :]


def attend_forward(shards, parent_block, qkv_blocks, kv, per_group, seg):
    blocks = len(qkv_blocks)
    local, wide = qkv_blocks[0].shape
    rows = blocks * local
    width = kv * per_group * HD
    cells = rows * 12 * seg * kv * per_group
    return pl.pallas_call(
        functools.partial(attend_forward_kernel, kv, per_group, seg, blocks),
        out_shape=[jax.ShapeDtypeStruct((rows, wide), BF), jax.ShapeDtypeStruct((rows, width), BF)],
        in_specs=[SMEM, SMEM] + [VMEM] * blocks,
        out_specs=[VMEM, VMEM],
        scratch_shapes=[pltpu.VMEM((rows, width), BF)],
        compiler_params=pltpu.CompilerParams(vmem_limit_bytes=40 * MIB),
        cost_estimate=pl.CostEstimate(
            flops=16 * HD * cells, bytes_accessed=4 * rows * wide, transcendentals=cells
        ),
        name="attend_forward",
    )(shards, parent_block, *qkv_blocks)


def attend_backward_kernel(kv, per_group, seg, blocks, shard_ref, parent_ref, qkv_ref, *refs):
    ins, (out_ref, do_ref, full_ref, dk_ref, dv_ref) = refs[:blocks], refs[blocks:]
    local = ins[0].shape[0]
    q_width = kv * per_group * HD
    scale = 1.0 / math.sqrt(HD)
    for j in range(blocks):
        at = pl.multiple_of(shard_ref[j] * local, 64)
        do_ref[pl.ds(at, local), :] = ins[j][...]
    dk_ref[...] = jnp.zeros_like(dk_ref)
    dv_ref[...] = jnp.zeros_like(dv_ref)

    def work(first, g, keys, values, masks, places):
        span = slice(g * per_group * HD, (g + 1) * per_group * HD)
        q = stack_heads(qkv_ref[pl.ds(first, QT), span], per_group) * BF(scale)
        d = stack_heads(do_ref[pl.ds(first, QT), span], per_group)
        probs = softmax_parts(keys, masks, q)
        grads = [dot(v, d, 1, 1) for v in values]
        delta = None
        for p, grad in zip(probs, grads):
            t = jnp.sum(grad * p, axis=0, keepdims=True)
            delta = t if delta is None else delta + t
        dq = None
        for p, grad, k, place in zip(probs, grads, keys, places):
            ds = (p * (grad - delta)).astype(BF)
            dk = dot(ds, q, 1, 0)
            dv = dot(p.astype(BF), d, 1, 0)
            o = dot(k, ds, 0, 0)
            dq = o if dq is None else dq + o
            at = 0
            for start, size in place:
                dk_ref[pl.ds(start, size), g * HD : (g + 1) * HD] += dk[at : at + size]
                dv_ref[pl.ds(start, size), g * HD : (g + 1) * HD] += dv[at : at + size]
                at += size
        dq = dq * scale
        for h in range(per_group):
            c = (g * per_group + h) * HD
            full_ref[pl.ds(first, QT), c : c + HD] = dq[:, h * QT : (h + 1) * QT].T.astype(BF)

    each_tile(qkv_ref, parent_ref, kv, per_group, seg, work)
    full_ref[:, q_width : q_width + kv * HD] = dk_ref[...].astype(BF)
    full_ref[:, q_width + kv * HD : q_width + 2 * kv * HD] = dv_ref[...].astype(BF)
    for j in range(blocks):
        at = pl.multiple_of(shard_ref[j] * local, 64)
        out_ref[j * local : (j + 1) * local, :] = full_ref[pl.ds(at, local), :]


def attend_backward(shards, parent_block, qkv, grad_blocks, kv, per_group, seg):
    blocks = len(grad_blocks)
    rows, wide = qkv.shape
    width = kv * per_group * HD
    cells = rows * 12 * seg * kv * per_group
    return pl.pallas_call(
        functools.partial(attend_backward_kernel, kv, per_group, seg, blocks),
        out_shape=jax.ShapeDtypeStruct((rows, wide), BF),
        in_specs=[SMEM, SMEM, VMEM] + [VMEM] * blocks,
        out_specs=VMEM,
        scratch_shapes=[
            pltpu.VMEM((rows, width), BF),
            pltpu.VMEM((rows, wide), BF),
            pltpu.VMEM((rows, kv * HD), F32),
            pltpu.VMEM((rows, kv * HD), F32),
        ],
        compiler_params=pltpu.CompilerParams(vmem_limit_bytes=40 * MIB),
        cost_estimate=pl.CostEstimate(
            flops=40 * HD * cells, bytes_accessed=6 * rows * wide, transcendentals=cells
        ),
        name="attend_backward",
    )(shards, parent_block, qkv, *grad_blocks)


def expert_kernel(
    at_ref, xa_ref, xb_ref, ga_ref, gb_ref, code_ref, router_ref, gate_ref, up_ref, down_ref,
    mix_a_ref, mix_b_ref, back_a_ref, back_b_ref, dot_ref, act_ref, dgate_ref, dup_ref,
):
    half = xa_ref.shape[0]
    x = jnp.concatenate([xa_ref[...], xb_ref[...]], axis=0)
    g = jnp.concatenate([ga_ref[...], gb_ref[...]], axis=0)
    code_a = code_ref[at_ref[1]]
    code_b = code_ref[at_ref[2]]
    token = lax.broadcasted_iota(jnp.int32, code_a.shape, 1)
    code = jnp.where(token < half, code_a, code_b).T
    logits = dot(x, router_ref[...], 1, 0)
    logits = jnp.where(code > 0.5, logits, NEG)
    top = jnp.max(logits, axis=1, keepdims=True)
    e = jnp.exp(logits - top)
    kept = jnp.where(code > 1.5, 1.0, 0.0)
    gates = kept * e / jnp.sum(e, axis=1, keepdims=True)
    lane = lax.broadcasted_iota(jnp.int32, gates.shape, 1)
    count = gate_ref.shape[0]
    mix = None
    back = None
    for n in range(count):
        mine = lane == at_ref[0] + n
        weight = jnp.sum(jnp.where(mine, gates, 0.0), axis=1, keepdims=True)
        keep = jnp.sum(jnp.where(mine, kept, 0.0), axis=1, keepdims=True)
        gate_pre = dot(x, gate_ref[n], 1, 0)
        up_pre = dot(x, up_ref[n], 1, 0)
        grad = dot(g, down_ref[n], 1, 1)
        sig = 1.0 / (1.0 + jnp.exp(-gate_pre))
        silu = gate_pre * sig
        act = (silu * up_pre).astype(BF).astype(F32)
        pair_dot = jnp.sum(act * grad, axis=1, keepdims=True) * keep
        dot_ref[n : n + 1, :] = pair_dot.T
        weighted = (act * weight).astype(BF)
        grad = grad * weight
        dgate = (grad * up_pre * sig * (1.0 + gate_pre * (1.0 - sig))).astype(BF)
        dup = (grad * silu).astype(BF)
        act_ref[n] = weighted
        dgate_ref[n] = dgate
        dup_ref[n] = dup
        m = dot(weighted, down_ref[n], 1, 0)
        mix = m if mix is None else mix + m
        b = dot(dgate, gate_ref[n], 1, 1) + dot(dup, up_ref[n], 1, 1)
        back = b if back is None else back + b
    mix = mix.astype(BF)
    back = back.astype(BF)
    mix_a_ref[...] = mix[:half]
    mix_b_ref[...] = mix[half:]
    back_a_ref[...] = back[:half]
    back_b_ref[...] = back[half:]


def expert_step(at, x, g, codes, router, gate, up, down):
    half, width = x[0].shape
    count, _, hidden = gate.shape
    rows = 2 * half
    half_shape = jax.ShapeDtypeStruct((half, width), BF)
    kept_shape = jax.ShapeDtypeStruct((count, rows, hidden), BF)
    return pl.pallas_call(
        expert_kernel,
        out_shape=[half_shape] * 4
        + [jax.ShapeDtypeStruct((count, rows), F32)]
        + [kept_shape] * 3,
        in_specs=[SMEM] + [VMEM] * 9,
        out_specs=[VMEM] * 8,
        compiler_params=pltpu.CompilerParams(vmem_limit_bytes=56 * MIB),
        cost_estimate=pl.CostEstimate(
            flops=2 * rows * width * hidden * count * 6 * 2,
            bytes_accessed=6 * width * hidden * count + 10 * rows * width,
            transcendentals=rows * hidden * count,
        ),
        name="expert_step",
    )(at, x[0], x[1], g[0], g[1], codes, router, gate, up, down)


def tree_moves():
    rows, cols = lax.axis_size("row"), lax.axis_size("col")
    both = ("row", "col")
    if rows == 2 and cols == 2:
        swap = [(0, 1), (1, 0)]
        cross = [(0, 3), (3, 0), (1, 2), (2, 1)]
        me = lax.axis_index("row") * 2 + lax.axis_index("col")
        shards = [me, me ^ 1, me ^ 2, me ^ 3]

        def gather(x):
            across = lax.ppermute(x, "row", swap)
            beside = lax.ppermute(x, "col", swap)
            return [x, beside, across, lax.ppermute(across, "col", swap)]

        def exchange(blocks):
            return [
                blocks[0],
                lax.ppermute(blocks[1], "col", swap),
                lax.ppermute(blocks[2], "row", swap),
                lax.ppermute(blocks[3], both, cross),
            ]

        def reduce(blocks):
            far = blocks[2].astype(F32) + lax.ppermute(blocks[3], "col", swap).astype(F32)
            far = lax.ppermute(far.astype(BF), "row", swap).astype(F32)
            near = blocks[0].astype(F32) + lax.ppermute(blocks[1], "col", swap).astype(F32)
            return near + far

        return shards, gather, exchange, reduce

    count = rows * cols

    def gather(x):
        whole = lax.all_gather(x, both, axis=0)
        return [whole[i] for i in range(count)]

    def exchange(blocks):
        whole = lax.all_to_all(jnp.stack(blocks), both, 0, 0)
        return [whole[i] for i in range(count)]

    def reduce(blocks):
        return lax.psum_scatter(jnp.stack(blocks), both, scatter_dimension=0).astype(F32)

    return [jnp.int32(i) for i in range(count)], gather, exchange, reduce


def ring_order(count):
    depth = 4 if count % 4 == 0 else 1
    ys = count // depth
    order = []
    for y in range(ys):
        zs = range(depth) if y % 2 == 0 else reversed(range(depth))
        order += [z * ys + y for z in zs]
    return order


def ring_steps(order):
    n = len(order)
    onward = [(order[i], order[(i + 1) % n]) for i in range(n)]
    return onward, [(b, a) for a, b in onward]


def ring_gather(a, b, order):
    onward, backward = ring_steps(order)
    held = [(a, b)]
    for _ in range(len(order) - 1):
        a = lax.ppermute(a, "dp", onward)
        b = lax.ppermute(b, "dp", backward)
        held.append((a, b))
    return held


def ring_reduce(parts, order):
    onward, backward = ring_steps(order)
    a, b = parts[1]
    for k in range(1, len(order)):
        a = lax.ppermute(a, "dp", onward)
        b = lax.ppermute(b, "dp", backward)
        more = parts[(k + 1) % len(order)]
        a = a.astype(F32) + more[0].astype(F32)
        b = b.astype(F32) + more[1].astype(F32)
        if k < len(order) - 1:
            a, b = a.astype(BF), b.astype(BF)
    return jnp.concatenate([a, b], axis=0)


def rms_scale(values):
    return lax.rsqrt(jnp.mean(values * values, axis=-1, keepdims=True) + EPS)


def norm_back(grad_normed, values, scale_rows, gain):
    weighted = grad_normed * gain
    grad_gain = jnp.sum(grad_normed * values * scale_rows, axis=0)
    inner = jnp.mean(weighted * values, axis=-1, keepdims=True)
    return (
        scale_rows * weighted - values * scale_rows * scale_rows * scale_rows * inner,
        grad_gain,
    )


def shards_program(
    tokens, attn_gain, query_weight, key_weight, value_weight, out_weight, mlp_gain, router_weight,
    gate_weight, up_weight, down_weight, output_grad, expert_ids, slot_rank, segment_ids, parent_ids,
):
    local_rows, width = tokens.shape
    half = local_rows // 2
    ring = lax.axis_size("dp")
    order = ring_order(ring)
    places = [order.index(i) for i in range(ring)]
    shards, tree_gather, tree_exchange, tree_reduce = tree_moves()
    count = len(shards)
    shard_ids = jnp.stack(shards).astype(jnp.int32)
    kv = key_weight.shape[1] // HD
    per_group = query_weight.shape[1] // key_weight.shape[1]
    q_width = query_weight.shape[1]
    k_width = key_weight.shape[1]
    experts_local = gate_weight.shape[0]
    experts = experts_local * ring
    capacity = 5 * local_rows * TOPK // (4 * experts)
    seg = local_rows * count // 20
    dp_index = lax.axis_index("dp")
    place = jnp.array(places, jnp.int32)[dp_index]

    token_values = tokens.astype(F32)
    scale_attn = rms_scale(token_values)
    normed = (token_values * scale_attn * attn_gain).astype(BF)
    tree_normed = tree_gather(normed)
    step = math.gcd(seg, local_rows)
    labels = jnp.stack([segment_ids[::step], parent_ids[::step]]).astype(jnp.int32)
    tree_labels = lax.all_gather(labels, ("row", "col"), axis=1, tiled=True)[:, :: seg // step]
    spot = jnp.arange(20, dtype=jnp.int32)
    parent_block = jnp.sum(
        jnp.where(
            (tree_labels[0][None, :] == tree_labels[1][:, None]) & (tree_labels[1][:, None] > 0),
            spot[None, :],
            0,
        ),
        axis=1,
    )

    flat_expert = expert_ids.reshape(-1)
    flat_rank = slot_rank.reshape(-1)
    earlier = (flat_expert[None, :] == flat_expert[:, None]) & (
        flat_rank[None, :] < flat_rank[:, None]
    )
    kept = (jnp.sum(earlier.astype(jnp.int32), axis=1) < capacity).reshape(local_rows, TOPK)
    marks = 1.0 + kept.T.astype(F32)
    columns = jnp.arange(experts, dtype=jnp.int32)
    code = jnp.sum(
        jnp.where(expert_ids.T[:, None, :] == columns[None, :, None], marks[:, None, :], 0.0), axis=0
    )
    codes = lax.all_gather(code, "dp", axis=0)

    grads = ring_gather(output_grad[:half], output_grad[half:], order)

    qkv_weight = jnp.concatenate([query_weight, key_weight, value_weight], axis=1)
    qkv_blocks = [
        jnp.dot(block, qkv_weight, preferred_element_type=F32).astype(BF) for block in tree_normed
    ]
    out_blocks = tree_gather(after(out_weight, tree_normed[2]))
    qkv, heads = attend_forward(shard_ids, parent_block, qkv_blocks, kv, per_group, seg)
    head_blocks = tree_exchange(
        [heads[j * local_rows : (j + 1) * local_rows] for j in range(count)]
    )
    gate_blocks = tree_gather(after(gate_weight, out_blocks[2]))
    up_blocks = tree_gather(after(up_weight, out_blocks[2]))
    down_blocks = tree_gather(after(down_weight, out_blocks[2]))
    full_gate = jnp.concatenate(gate_blocks, axis=2)
    full_up = jnp.concatenate(up_blocks, axis=2)
    full_down = jnp.concatenate(down_blocks, axis=1)

    hidden = token_values + jnp.dot(
        jnp.concatenate(head_blocks, axis=1),
        jnp.concatenate(out_blocks, axis=0),
        preferred_element_type=F32,
    )
    scale_mlp = rms_scale(hidden)
    mlp_in = (hidden * scale_mlp * mlp_gain).astype(BF)

    rows_held = ring_gather(mlp_in[:half], mlp_in[half:], order)
    mixes, backs, dots, acts, dgates, dups = [], [], [], [], [], []
    order_array = jnp.array(order, jnp.int32)
    for k in range(ring):
        at = jnp.stack(
            [
                dp_index * experts_local,
                order_array[(place - k) % ring],
                order_array[(place + k) % ring],
            ]
        ).astype(jnp.int32)
        mix_a, mix_b, back_a, back_b, pair_dot, act, dgate, dup = expert_step(
            at, rows_held[k], grads[k], codes, router_weight, full_gate, full_up, full_down
        )
        mixes.append((mix_a, mix_b))
        backs.append((back_a, back_b))
        dots.append(pair_dot)
        acts.append(act)
        dgates.append(dgate)
        dups.append(dup)
    grad_rows = ring_reduce(backs, order)
    mixes[1] = tuple(after(m, grad_rows) for m in mixes[1])
    output = (hidden + ring_reduce(mixes, order)).astype(BF)

    steps = jnp.arange(ring, dtype=jnp.int32)
    place_of = jnp.array(places, jnp.int32)
    all_dots = jnp.stack(dots)
    first_half = jnp.arange(local_rows) < half

    def pick(index):
        return jnp.sum(
            jnp.where((index[:, None] == steps[None, :])[:, :, None, None], all_dots[None], 0.0),
            axis=1,
        )

    send = jnp.where(first_half, pick((place - place_of) % ring), pick((place_of - place) % ring))
    grad_gates = lax.all_to_all(send, "dp", 0, 0, tiled=True).reshape(experts, local_rows).T

    code_here = code.T
    logits = jnp.dot(mlp_in, router_weight, preferred_element_type=F32)
    logits = jnp.where(code_here > 0.5, logits, NEG)
    chosen_exp = jnp.exp(logits - jnp.max(logits, axis=1, keepdims=True))
    gates = chosen_exp / jnp.sum(chosen_exp, axis=1, keepdims=True)
    weighted_sum = jnp.sum(gates * grad_gates, axis=1, keepdims=True)
    grad_logits = (gates * (grad_gates - weighted_sum)).astype(BF)
    router_part = jnp.dot(mlp_in.T, grad_logits, preferred_element_type=F32)
    grad_mlp_in = grad_rows + jnp.dot(grad_logits, router_weight.T, preferred_element_type=F32)
    grad_hidden_norm, mlp_gain_part = norm_back(grad_mlp_in, hidden, scale_mlp, mlp_gain)
    grad_hidden = output_grad.astype(F32) + grad_hidden_norm
    grad_attn = grad_hidden.astype(BF)

    grad_blocks = tree_gather(grad_attn)
    grad_head_blocks = [
        jnp.dot(block, out_weight.T, preferred_element_type=F32).astype(BF) for block in grad_blocks
    ]
    dqkv = attend_backward(shard_ids, parent_block, qkv, grad_head_blocks, kv, per_group, seg)
    normed_rows = jnp.concatenate(tree_normed, axis=0)
    out_part = jnp.dot(
        heads.T, jnp.concatenate(grad_blocks, axis=0), preferred_element_type=F32
    ).astype(BF)
    qkv_part = jnp.dot(normed_rows.T, dqkv, preferred_element_type=F32).astype(BF)
    summed = jnp.dot(dqkv, qkv_weight.T, preferred_element_type=F32).astype(BF)
    grad_normed = tree_reduce(
        [summed[j * local_rows : (j + 1) * local_rows] for j in range(count)]
    )
    grad_token_norm, attn_gain_part = norm_back(grad_normed, token_values, scale_attn, attn_gain)
    input_grad = grad_hidden + grad_token_norm

    all_rows = jnp.concatenate([r for pair in rows_held for r in pair], axis=0)
    all_grads = jnp.concatenate([r for pair in grads for r in pair], axis=0)

    def expert_grad(parts, rows, pattern):
        return jnp.einsum(
            pattern, rows, jnp.concatenate(parts, axis=1), preferred_element_type=F32
        ).astype(BF)

    unit = gate_weight.shape[2]
    gate_full = expert_grad(dgates, all_rows, "td,etf->edf")
    up_full = expert_grad(dups, all_rows, "td,etf->edf")
    down_full = expert_grad(acts, all_grads, "td,etf->efd")
    gate_grad = tree_reduce([gate_full[:, :, j * unit : (j + 1) * unit] for j in range(count)])
    up_grad = tree_reduce([up_full[:, :, j * unit : (j + 1) * unit] for j in range(count)])
    down_grad = tree_reduce([down_full[:, j * unit : (j + 1) * unit] for j in range(count)])
    out_grad = lax.psum(out_part, "dp").astype(F32)
    qkv_grad = lax.psum(qkv_part, "dp").astype(F32)
    attn_gain_grad, mlp_gain_grad, router_grad = lax.psum(
        (attn_gain_part, mlp_gain_part, router_part), ("dp", "row", "col")
    )
    return (
        output,
        input_grad,
        attn_gain_grad,
        qkv_grad[:, :q_width],
        qkv_grad[:, q_width : q_width + k_width],
        qkv_grad[:, q_width + k_width :],
        out_grad,
        mlp_gain_grad,
        router_grad,
        gate_grad,
        up_grad,
        down_grad,
    )


def solution(mesh):
    every = ("dp", "row", "col")
    tree = ("row", "col")
    return jax.shard_map(
        shards_program,
        mesh=mesh,
        in_specs=(
            P(every, None),
            P(),
            P(None, tree),
            P(None, tree),
            P(None, tree),
            P(tree, None),
            P(),
            P(),
            P("dp", None, tree),
            P("dp", None, tree),
            P("dp", tree, None),
            P(every, None),
            P(every, None),
            P(every, None),
            P(every),
            P(every),
        ),
        out_specs=(
            P(every, None),
            P(every, None),
            P(),
            P(None, tree),
            P(None, tree),
            P(None, tree),
            P(tree, None),
            P(),
            P(),
            P("dp", None, tree),
            P("dp", None, tree),
            P("dp", tree, None),
        ),
        check_vma=False,
    )
```

```python
import functools
import math

import jax
import jax.numpy as jnp
from jax import lax
from jax.experimental import pallas as pl
from jax.experimental.pallas import tpu as pltpu
from jax.sharding import PartitionSpec as P

HD = 64
TOPK = 8
QT = 128
EPS = 1e-05
NEG = -1e30
MIB = 2**20
BF = jnp.bfloat16
F32 = jnp.float32
VMEM = pl.BlockSpec(memory_space=pltpu.VMEM)
SMEM = pl.BlockSpec(memory_space=pltpu.SMEM)
ANY = pl.BlockSpec(memory_space=pl.ANY)


def dot(a, b, ca, cb):
    return lax.dot_general(a, b, (((ca,), (cb,)), ((), ())), preferred_element_type=F32)


def tie(*values):
    return lax.optimization_barrier(values)


def stack_heads(block, count):
    return jnp.concatenate([block[:, h * HD : (h + 1) * HD] for h in range(count)], axis=0)


def causal_mask(per_group):
    key = lax.broadcasted_iota(jnp.int32, (QT, QT), 0)
    query = lax.broadcasted_iota(jnp.int32, (QT, QT), 1)
    return jnp.concatenate([key <= query] * per_group, axis=1)


def tile_masks(seg, parents, per_group):
    key = lax.broadcasted_iota(jnp.int32, (QT, QT), 0)
    query = lax.broadcasted_iota(jnp.int32, (QT, QT), 1)
    own = (key <= query) & (key // seg == query // seg)
    par = None
    for j, parent in enumerate(parents):
        hit = (key // seg == j) & (query // seg == j) & (parent > 0)
        par = hit if par is None else par | hit
    return (
        jnp.concatenate([own] * per_group, axis=1),
        jnp.concatenate([par] * per_group, axis=1),
    )


def softmax_parts(keys, masks, q):
    parts = []
    top = None
    for k, mask in zip(keys, masks):
        s = dot(k, q, 1, 1)
        if mask is not None:
            s = jnp.where(mask, s, NEG)
        parts.append(s)
        m = jnp.max(s, axis=0, keepdims=True)
        top = m if top is None else jnp.maximum(top, m)
    probs = []
    total = None
    for s in parts:
        e = jnp.exp(s - top)
        t = jnp.sum(e, axis=0, keepdims=True)
        total = t if total is None else total + t
        probs.append(e)
    inverse = 1.0 / total
    return [e * inverse for e in probs]


def each_tile(qkv_ref, parent_ref, kv, per_group, seg, work):
    rows = qkv_ref.shape[0]
    trunk = 8 * seg
    segs = QT // seg
    q_width = kv * per_group * HD
    causal = causal_mask(per_group)

    def columns(g):
        return q_width + g * HD, q_width + kv * HD + g * HD

    for i in range(trunk // QT):
        for g in range(kv):
            kc, vc = columns(g)
            spans = ([(0, i * QT)] if i > 0 else []) + [(i * QT, QT)]
            keys = [qkv_ref[a : a + n, kc : kc + HD] for a, n in spans]
            values = [qkv_ref[a : a + n, vc : vc + HD] for a, n in spans]
            masks = ([None] if i > 0 else []) + [causal]
            work(i * QT, g, keys, values, masks, [[s] for s in spans])

    def body(i, carry):
        first = pl.multiple_of(trunk + i * QT, QT)
        parents = [parent_ref[8 + i * segs + j] for j in range(segs)]
        starts = [pl.multiple_of(p * seg, seg) for p in parents]
        own, par = tile_masks(seg, parents, per_group)

        def take(c):
            blocks = [qkv_ref[pl.ds(s, seg), c : c + HD] for s in starts]
            return [
                qkv_ref[0:trunk, c : c + HD],
                qkv_ref[pl.ds(first, QT), c : c + HD],
                jnp.concatenate(blocks, axis=0) if segs > 1 else blocks[0],
            ]

        for g in range(kv):
            kc, vc = columns(g)
            places = [[(0, trunk)], [(first, QT)], [(s, seg) for s in starts]]
            work(first, g, take(kc), take(vc), [None, own, par], places)
        return carry

    lax.fori_loop(0, (rows - trunk) // QT, body, 0)


def attend_forward_kernel(kv, per_group, seg, blocks, shard_ref, parent_ref, *refs):
    ins, (qkv_ref, out_ref, full_ref) = refs[:blocks], refs[blocks:]
    local = out_ref.shape[0] // blocks
    scale = BF(1.0 / math.sqrt(HD))
    for j in range(blocks):
        at = pl.multiple_of(shard_ref[j] * local, 64)
        qkv_ref[pl.ds(at, local), :] = ins[j][0:local, :]

    def work(first, g, keys, values, masks, places):
        block = qkv_ref[pl.ds(first, QT), g * per_group * HD : (g + 1) * per_group * HD]
        probs = softmax_parts(keys, masks, stack_heads(block, per_group) * scale)
        total = None
        for p, v in zip(probs, values):
            o = dot(v, p.astype(BF), 0, 0)
            total = o if total is None else total + o
        for h in range(per_group):
            c = (g * per_group + h) * HD
            full_ref[pl.ds(first, QT), c : c + HD] = total[:, h * QT : (h + 1) * QT].T.astype(BF)

    each_tile(qkv_ref, parent_ref, kv, per_group, seg, work)
    for j in range(blocks):
        at = pl.multiple_of(shard_ref[j] * local, 64)
        out_ref[j * local : (j + 1) * local, :] = full_ref[pl.ds(at, local), :]


def attend_forward(shards, parent_block, qkv_blocks, kv, per_group, seg):
    blocks = len(qkv_blocks)
    wide = qkv_blocks[0].shape[1]
    rows = 20 * seg
    width = kv * per_group * HD
    cells = rows * 12 * seg * kv * per_group
    return pl.pallas_call(
        functools.partial(attend_forward_kernel, kv, per_group, seg, blocks),
        out_shape=[jax.ShapeDtypeStruct((rows, wide), BF), jax.ShapeDtypeStruct((rows, width), BF)],
        in_specs=[SMEM, SMEM] + [VMEM] * blocks,
        out_specs=[VMEM, VMEM],
        scratch_shapes=[pltpu.VMEM((rows, width), BF)],
        compiler_params=pltpu.CompilerParams(vmem_limit_bytes=40 * MIB),
        cost_estimate=pl.CostEstimate(
            flops=16 * HD * cells, bytes_accessed=4 * rows * wide, transcendentals=cells
        ),
        name="attend_forward",
    )(shards, parent_block, *qkv_blocks)


def attend_backward_kernel(kv, per_group, seg, blocks, shard_ref, parent_ref, qkv_ref, *refs):
    ins, (out_ref, do_ref, full_ref, dk_ref, dv_ref) = refs[:blocks], refs[blocks:]
    local = ins[0].shape[0]
    q_width = kv * per_group * HD
    scale = 1.0 / math.sqrt(HD)
    for j in range(blocks):
        at = pl.multiple_of(shard_ref[j] * local, 64)
        do_ref[pl.ds(at, local), :] = ins[j][...]
    dk_ref[...] = jnp.zeros_like(dk_ref)
    dv_ref[...] = jnp.zeros_like(dv_ref)

    def work(first, g, keys, values, masks, places):
        span = slice(g * per_group * HD, (g + 1) * per_group * HD)
        q = stack_heads(qkv_ref[pl.ds(first, QT), span], per_group) * BF(scale)
        d = stack_heads(do_ref[pl.ds(first, QT), span], per_group)
        probs = softmax_parts(keys, masks, q)
        grads = [dot(v, d, 1, 1) for v in values]
        delta = None
        for p, grad in zip(probs, grads):
            t = jnp.sum(grad * p, axis=0, keepdims=True)
            delta = t if delta is None else delta + t
        dq = None
        for p, grad, k, place in zip(probs, grads, keys, places):
            ds = (p * (grad - delta)).astype(BF)
            dk = dot(ds, q, 1, 0)
            dv = dot(p.astype(BF), d, 1, 0)
            o = dot(k, ds, 0, 0)
            dq = o if dq is None else dq + o
            at = 0
            for start, size in place:
                dk_ref[pl.ds(start, size), g * HD : (g + 1) * HD] += dk[at : at + size]
                dv_ref[pl.ds(start, size), g * HD : (g + 1) * HD] += dv[at : at + size]
                at += size
        dq = dq * scale
        for h in range(per_group):
            c = (g * per_group + h) * HD
            full_ref[pl.ds(first, QT), c : c + HD] = dq[:, h * QT : (h + 1) * QT].T.astype(BF)

    each_tile(qkv_ref, parent_ref, kv, per_group, seg, work)
    full_ref[:, q_width : q_width + kv * HD] = dk_ref[...].astype(BF)
    full_ref[:, q_width + kv * HD : q_width + 2 * kv * HD] = dv_ref[...].astype(BF)
    for j in range(blocks):
        at = pl.multiple_of(shard_ref[j] * local, 64)
        out_ref[j * local : (j + 1) * local, :] = full_ref[pl.ds(at, local), :]


def attend_backward(shards, parent_block, qkv, grad_blocks, kv, per_group, seg):
    blocks = len(grad_blocks)
    rows, wide = qkv.shape
    width = kv * per_group * HD
    cells = rows * 12 * seg * kv * per_group
    return pl.pallas_call(
        functools.partial(attend_backward_kernel, kv, per_group, seg, blocks),
        out_shape=jax.ShapeDtypeStruct((rows, wide), BF),
        in_specs=[SMEM, SMEM, VMEM] + [VMEM] * blocks,
        out_specs=VMEM,
        scratch_shapes=[
            pltpu.VMEM((rows, width), BF),
            pltpu.VMEM((rows, wide), BF),
            pltpu.VMEM((rows, kv * HD), F32),
            pltpu.VMEM((rows, kv * HD), F32),
        ],
        compiler_params=pltpu.CompilerParams(vmem_limit_bytes=40 * MIB),
        cost_estimate=pl.CostEstimate(
            flops=40 * HD * cells, bytes_accessed=6 * rows * wide, transcendentals=cells
        ),
        name="attend_backward",
    )(shards, parent_block, qkv, *grad_blocks)


def expert_kernel(first, blocks, fresh, at_ref, xa_ref, xb_ref, grads_ref, router_ref, *refs):
    count = len(blocks)
    weight_refs, refs = refs[: sum(blocks)], refs[sum(blocks) :]
    if not fresh:
        refs = refs[6:]
    back_a_ref, back_b_ref, dot_ref, mix_ref, rows_ref, grad_rows_ref, *kept_refs = refs[:9]
    weights, held, g_held, mix_held, weight_sem, held_sem, row_sem, g_sem, mix_sem = refs[9:]
    half = back_a_ref.shape[0]
    rows = 2 * half
    experts = router_ref.shape[1]
    spots = [pl.multiple_of(at_ref[1 + i] * rows + i * half, 16) for i in range(2)]
    arrived = []
    for i in range(2):
        copy = pltpu.make_async_copy(
            grads_ref.at[pl.ds(spots[i], half)], g_held.at[pl.ds(i * half, half)], g_sem.at[i]
        )
        copy.start()
        arrived.append(copy)
    loads = []
    for i in (2, 0, 1):
        for n in range(count):
            at = sum(blocks[:n])
            for j in range(blocks[n]):
                source = weight_refs[at + j].at[i]
                unit = source.shape[1]
                copy = pltpu.make_async_copy(
                    source,
                    weights[i].at[n, :, pl.ds(j * unit, unit)],
                    weight_sem.at[i * sum(blocks) + at + j],
                )
                loads.append((n, i, copy))
    for n in range(count):
        for m, _, copy in loads:
            if m == n:
                copy.start()

    def loaded(n, i):
        for m, k, copy in loads:
            if (m, k) == (n, i):
                copy.wait()

    stores = []
    for i, ref in enumerate((xa_ref, xb_ref)):
        stores.append(
            pltpu.make_async_copy(
                ref.at[pl.ds(0, half)], rows_ref.at[pl.ds(first + i * half, half)], row_sem.at[i]
            )
        )
        stores[-1].start()
    x = jnp.concatenate([xa_ref[0:half], xb_ref[0:half]], axis=0)
    code = jnp.concatenate(
        [ref[half : half + experts, 0:half].astype(F32).T for ref in (xa_ref, xb_ref)], axis=0
    )
    logits = dot(x, router_ref[...], 1, 0)
    logits = jnp.where(code > 0.5, logits, NEG)
    top = jnp.max(logits, axis=1, keepdims=True)
    e = jnp.exp(logits - top)
    kept = jnp.where(code > 1.5, 1.0, 0.0)
    gates = kept * e / jnp.sum(e, axis=1, keepdims=True)
    lane = lax.broadcasted_iota(jnp.int32, gates.shape, 1)
    for copy in arrived:
        copy.wait()
    copy = pltpu.make_async_copy(g_held, grad_rows_ref.at[pl.ds(first, rows)], row_sem.at[2])
    copy.start()
    stores.append(copy)
    g = g_held[...]
    mix = None
    back = None
    for n in range(count):
        mine = lane == at_ref[0] + n
        weight = jnp.sum(jnp.where(mine, gates, 0.0), axis=1, keepdims=True)
        keep = jnp.sum(jnp.where(mine, kept, 0.0), axis=1, keepdims=True)
        loaded(n, 2)
        grad = dot(g, weights[2][n], 1, 0)
        loaded(n, 0)
        gate_pre = dot(x, weights[0][n], 1, 0)
        loaded(n, 1)
        up_pre = dot(x, weights[1][n], 1, 0)
        sig = 1.0 / (1.0 + jnp.exp(-gate_pre))
        silu = gate_pre * sig
        act = (silu * up_pre).astype(BF).astype(F32)
        pair_dot = jnp.sum(act * grad, axis=1, keepdims=True) * keep
        dot_ref[n : n + 1, :] = pair_dot.T
        weighted = (act * weight).astype(BF)
        grad = grad * weight
        dgate = (grad * up_pre * sig * (1.0 + gate_pre * (1.0 - sig))).astype(BF)
        dup = (grad * silu).astype(BF)
        for i, value in enumerate((weighted, dgate, dup)):
            held[i][n] = value
            copy = pltpu.make_async_copy(
                held[i].at[n], kept_refs[i].at[n, pl.ds(first, rows)], held_sem.at[n * 3 + i]
            )
            copy.start()
            stores.append(copy)
        m = dot(weighted, weights[2][n], 1, 1)
        mix = m if mix is None else mix + m
        b = dot(dgate, weights[0][n], 1, 1) + dot(dup, weights[1][n], 1, 1)
        back = b if back is None else back + b
    mix_held[...] = mix.astype(BF)
    for i in range(2):
        copy = pltpu.make_async_copy(
            mix_held.at[pl.ds(i * half, half)], mix_ref.at[pl.ds(spots[i], half)], mix_sem.at[i]
        )
        copy.start()
        stores.append(copy)
    back = back.astype(BF)
    back_a_ref[...] = back[:half]
    back_b_ref[...] = back[half:]
    for copy in stores:
        copy.wait()


def expert_step(k, steps, at, x, grads, router, weights, buffers):
    width = x[0].shape[1]
    half = grads.shape[0] // steps // 2
    rows = 2 * half
    count = len(weights)
    hidden = sum(w.shape[2] for w in weights[0])
    half_shape = jax.ShapeDtypeStruct((half, width), BF)
    big_shapes = [jax.ShapeDtypeStruct((steps * rows, width), BF)] * 3
    big_shapes += [jax.ShapeDtypeStruct((count, steps * rows, hidden), BF)] * 3
    operands = [at, *x, grads, router, *[b for w in weights for b in w]]
    specs = [SMEM, VMEM, VMEM, ANY, VMEM] + [ANY] * (len(operands) - 5)
    aliases = {}
    if buffers is not None:
        aliases = {len(operands) + i: 3 + i for i in range(6)}
        operands += buffers
        specs += [ANY] * 6
    blocks = [len(w) for w in weights]
    out = pl.pallas_call(
        functools.partial(expert_kernel, k * rows, blocks, buffers is None),
        out_shape=[half_shape] * 2 + [jax.ShapeDtypeStruct((count, rows), F32)] + big_shapes,
        in_specs=specs,
        out_specs=[VMEM] * 3 + [ANY] * 6,
        input_output_aliases=aliases,
        scratch_shapes=[
            [pltpu.VMEM((count, width, hidden), BF)] * 3,
            [pltpu.VMEM((count, rows, hidden), BF)] * 3,
            pltpu.VMEM((rows, width), BF),
            pltpu.VMEM((rows, width), BF),
            pltpu.SemaphoreType.DMA((3 * sum(blocks),)),
            pltpu.SemaphoreType.DMA((count * 3,)),
            pltpu.SemaphoreType.DMA((3,)),
            pltpu.SemaphoreType.DMA((2,)),
            pltpu.SemaphoreType.DMA((2,)),
        ],
        compiler_params=pltpu.CompilerParams(vmem_limit_bytes=40 * MIB),
        cost_estimate=pl.CostEstimate(
            flops=2 * rows * width * hidden * count * 6,
            bytes_accessed=6 * width * hidden * count + 10 * rows * width,
            transcendentals=rows * hidden * count,
        ),
        name="expert_step",
    )(*operands)
    return out[:2], out[2], out[3:]


def expert_grad_kernel(act_ref, dgate_ref, dup_ref, x_ref, g_ref, *outs):
    half, _, _, unit = outs[0].shape
    for i, (rows, ref) in enumerate(((x_ref, dgate_ref), (x_ref, dup_ref), (g_ref, act_ref))):
        grad = dot(rows[...], ref[0], 0, 0).astype(BF)
        for j in range(2 * half):
            outs[j // half][j % half, i] = grad[:, j * unit : (j + 1) * unit]


def expert_grads(kept, x, g, parts, expert):
    _, rows, hidden = kept[0].shape
    width = x.shape[1]
    unit = hidden // parts
    tile = 512 if width % 512 == 0 else width
    half = parts // 2
    return list(pl.pallas_call(
        expert_grad_kernel,
        grid=(width // tile,),
        out_shape=[jax.ShapeDtypeStruct((half, 3, width, unit), BF)] * 2,
        in_specs=[pl.BlockSpec((1, rows, hidden), lambda i: (expert, 0, 0))] * 3
        + [pl.BlockSpec((rows, tile), lambda i: (0, i))] * 2,
        out_specs=[pl.BlockSpec((half, 3, tile, unit), lambda i: (0, 0, i, 0))] * 2,
        compiler_params=pltpu.CompilerParams(vmem_limit_bytes=56 * MIB),
        cost_estimate=pl.CostEstimate(
            flops=6 * rows * width * hidden,
            bytes_accessed=12 * width * hidden,
            transcendentals=0,
        ),
        name="expert_grads",
    )(*kept, x, g))


def tree_moves():
    rows, cols = lax.axis_size("row"), lax.axis_size("col")
    if rows == 2 and cols == 2:
        swap = [(0, 1), (1, 0)]
        me = lax.axis_index("row") * 2 + lax.axis_index("col")

        def gather(x):
            across = lax.ppermute(x, "row", swap)
            beside = lax.ppermute(x, "col", swap)
            return [x, across, beside, lax.ppermute(across, "col", swap)]

        def reduce(mine, other):
            came = lax.ppermute(other, "col", swap)
            far = (mine[1].astype(F32) + came[1].astype(F32)).astype(BF)
            near = mine[0].astype(F32) + came[0].astype(F32)
            return near, lax.ppermute(far, "row", swap)

        return [me, me ^ 2, me ^ 1, me ^ 3], gather, reduce

    count = rows * cols
    both = ("row", "col")

    def gather(x):
        whole = lax.all_gather(x, both, axis=0)
        return [whole[i] for i in range(count)]

    def reduce(mine, other):
        blocks = jnp.concatenate([mine, other], axis=0)
        total = lax.psum_scatter(blocks, both, scatter_dimension=0)
        return total.astype(F32), jnp.zeros_like(total)

    return [jnp.int32(i) for i in range(count)], gather, reduce


def half_orders(count):
    ys = count // 4
    near = [y for y in range(ys)] + [ys + y for y in reversed(range(ys))]
    return [near, [partner_of(i, count) for i in near]]


def partner_of(index, count):
    ys = count // 4
    return (3 - index // ys) * ys + index % ys


def ring_order(count):
    ys = count // 4
    order = []
    for y in range(ys):
        zs = range(4) if y % 2 == 0 else reversed(range(4))
        order += [z * ys + y for z in zs]
    return order


def ring_move(x, order, by):
    n = len(order)
    return lax.ppermute(x, "dp", [(order[i], order[(i + by) % n]) for i in range(n)])


class Ring:
    def __init__(self, count, dp_index):
        self.orders = half_orders(count)
        self.steps = len(self.orders[0])
        at = [[o.index(i) for o in self.orders if i in o][0] for i in range(count)]
        self.place = jnp.array(at, jnp.int32)[dp_index]
        self.four = self.steps == 4
        if self.four:
            self.places = [lax.rem(self.place + k, 4) for k in (0, 3, 1, 2)]
        else:
            self.places = [jnp.int32(k) for k in range(self.steps)]

    def shift(self, x, by):
        n = self.steps
        return lax.ppermute(
            x, "dp", [(o[i], o[(i + by) % n]) for o in self.orders for i in range(n)]
        )

    def gather(self, x):
        if not self.four:
            whole = lax.all_gather(x, "dp", axis=0, axis_index_groups=self.orders)
            return [[whole[k]] for k in range(self.steps)]
        half = x.shape[0] // 2
        left, right = self.shift(x, 1), self.shift(x, -1)
        a, b = right[:half], left[half:]
        return [[x], [left], [right], [self.shift(a, -1), self.shift(b, 1)]]

    def reduce_stages(self, parts):
        if not self.four:
            yield []
            whole = jnp.stack([jnp.concatenate(p, axis=0) for p in parts])
            yield lax.psum_scatter(
                whole, "dp", scatter_dimension=0, axis_index_groups=self.orders
            ).astype(F32)
            return
        (own,), (left,), (right,), (far_a, far_b) = parts
        half = far_a.shape[0]
        a, b = yield [self.shift(far_a, 1), self.shift(far_b, -1)]
        right = jnp.concatenate(
            [(right[:half].astype(F32) + a.astype(F32)).astype(BF), right[half:]], axis=0
        )
        left = jnp.concatenate(
            [left[:half], (left[half:].astype(F32) + b.astype(F32)).astype(BF)], axis=0
        )
        yield own.astype(F32) + (
            self.shift(right, 1).astype(F32) + self.shift(left, -1).astype(F32)
        )

    def reduce(self, parts):
        stages = self.reduce_stages(parts)
        return stages.send(next(stages))


def sum_over_all(value):
    sizes = [lax.axis_size(name) for name in ("dp", "row", "col")]
    if sizes != [8, 2, 2]:
        return lax.psum(value, ("dp", "row", "col"))
    for name, size, bit in (("col", 2, 1), ("row", 2, 1), ("dp", 8, 1), ("dp", 8, 2), ("dp", 8, 4)):
        value = value + lax.ppermute(value, name, [(i, i ^ bit) for i in range(size)])
    return value


def write_kernel(spans, sizes, place_ref, *refs):
    pieces, outs = refs[: sum(sizes)], refs[sum(sizes) :]
    at = 0
    for k, size in enumerate(sizes):
        for i in range(size):
            rows = pieces[at].shape[0]
            start = pl.multiple_of(place_ref[k] * (rows * size) + i * rows, 16)
            for (a, b), out in zip(spans, outs):
                out[pl.ds(start, rows), :] = pieces[at][:, a:b].astype(F32)
            at += 1


def sum_over_dp(part, spans, ring, pairs):
    rows, width = part.shape
    chunk = rows // ring.steps

    def cut(place, at, size):
        return lax.dynamic_slice(part, (place * chunk + at, 0), (size, width))

    parts = [[cut(place, 0, chunk)] for place in ring.places]
    if ring.four:
        half = chunk // 2
        parts[3] = [cut(ring.places[3], 0, half), cut(ring.places[3], half, half)]
    stages = ring.reduce_stages(parts)
    total = stages.send((yield next(stages)))
    total = (yield [total])[0].astype(BF)
    came = (yield [lax.ppermute(total, "dp", pairs)])[0]
    total = (total.astype(F32) + came.astype(F32)).astype(BF)
    pieces = ring.gather(total)
    pieces[0] = yield pieces[0]
    sizes = [len(p) for p in pieces]
    yield pl.pallas_call(
        functools.partial(write_kernel, spans, sizes),
        out_shape=[jax.ShapeDtypeStruct((rows, b - a), F32) for a, b in spans],
        in_specs=[SMEM] + [VMEM] * sum(sizes),
        out_specs=[VMEM] * len(spans),
        compiler_params=pltpu.CompilerParams(vmem_limit_bytes=24 * MIB),
        name="write_grads",
    )(jnp.stack(ring.places).astype(jnp.int32), *[p for pair in pieces for p in pair])


def rms_scale(values):
    return lax.rsqrt(jnp.mean(values * values, axis=-1, keepdims=True) + EPS)


def norm_back(grad_normed, values, scale_rows, gain):
    weighted = grad_normed * gain
    grad_gain = jnp.sum(grad_normed * values * scale_rows, axis=0)
    inner = jnp.mean(weighted * values, axis=-1, keepdims=True)
    return (
        scale_rows * weighted - values * scale_rows * scale_rows * scale_rows * inner,
        grad_gain,
    )


def shards_program(
    tokens, attn_gain, query_weight, key_weight, value_weight, out_weight, mlp_gain, router_weight,
    gate_weight, up_weight, down_weight, output_grad, expert_ids, slot_rank, segment_ids, parent_ids,
):
    local_rows, width = tokens.shape
    half = local_rows // 2
    dp_size = lax.axis_size("dp")
    dp_index = lax.axis_index("dp")
    pairs = [(i, partner_of(i, dp_size)) for i in range(dp_size)]
    ring = Ring(dp_size, dp_index)
    shards, tree_gather, tree_reduce = tree_moves()
    count = len(shards)
    shard_ids = jnp.stack(shards).astype(jnp.int32)
    kv = key_weight.shape[1] // HD
    per_group = query_weight.shape[1] // key_weight.shape[1]
    q_width = query_weight.shape[1]
    k_width = key_weight.shape[1]
    experts_local = gate_weight.shape[0]
    unit = gate_weight.shape[2]
    experts = experts_local * dp_size
    capacity = 5 * local_rows * TOPK // (4 * experts)
    seg = local_rows * count // 20

    token_values = tokens.astype(F32)
    scale_attn = rms_scale(token_values)
    normed = (token_values * scale_attn * attn_gain).astype(BF)
    step = math.gcd(seg, local_rows)
    each = local_rows // step
    labels = jnp.stack([segment_ids[::step], parent_ids[::step]]).astype(BF)
    normed_packet = jnp.concatenate(
        [normed, jnp.pad(labels, ((0, 14), (0, width - each)))], axis=0
    )
    tree_normed = tree_gather(normed_packet)
    labels = jnp.concatenate([v[local_rows : local_rows + 2, :each] for v in tree_normed], axis=1)
    spots = jnp.concatenate([s * each + jnp.arange(each, dtype=jnp.int32) for s in shards])
    spots = spots.astype(jnp.int32)
    block_spot = spots * step // seg
    is_parent = (labels[0][None, :] == labels[1][:, None]) & (labels[1][:, None] > 0)
    parent_spot = jnp.max(jnp.where(is_parent, block_spot[None, :], 0), axis=1)
    natural = jnp.arange(20, dtype=jnp.int32) * (seg // step)
    parent_block = jnp.sum(
        jnp.where(spots[None, :] == natural[:, None], parent_spot[None, :], 0), axis=1
    ).astype(jnp.int32)

    flat_expert = expert_ids.reshape(-1)
    flat_rank = slot_rank.reshape(-1)
    earlier = (flat_expert[None, :] == flat_expert[:, None]) & (
        flat_rank[None, :] < flat_rank[:, None]
    )
    kept = (jnp.sum(earlier.astype(jnp.int32), axis=1) < capacity).reshape(local_rows, TOPK)
    marks = 1.0 + kept.T.astype(F32)
    columns = jnp.arange(experts, dtype=jnp.int32)
    code = jnp.sum(
        jnp.where(expert_ids.T[:, None, :] == columns[None, :, None], marks[:, None, :], 0.0), axis=0
    )
    extra = -(-experts // 16) * 16
    codes = [
        jnp.pad(code[:, at : at + half].astype(BF), ((0, extra - experts), (0, width - half)))
        for at in (0, half)
    ]
    all_output_grad = lax.all_gather(output_grad, "dp", axis=0, tiled=True)

    raw = [
        jnp.stack([gate_weight[n], up_weight[n], down_weight[n].T]) for n in range(experts_local)
    ]

    def blocks_of(value):
        blocks = tree_gather(value)
        return blocks if unit % 128 == 0 else [jnp.concatenate(blocks, axis=2)]

    weights = [blocks_of(raw[0])]
    qkv_weight = jnp.concatenate([query_weight, key_weight, value_weight], axis=1)
    qkv_blocks = [
        jnp.dot(block, qkv_weight, preferred_element_type=F32).astype(BF) for block in tree_normed
    ]
    qkv, heads = attend_forward(shard_ids, parent_block, qkv_blocks, kv, per_group, seg)
    heads, weights[0][-1 if count != 4 else 1] = tie(heads, weights[0][-1 if count != 4 else 1])
    def by_shard(rows, weight):
        result = jnp.dot(rows, weight, preferred_element_type=F32).astype(BF)
        return result.reshape(-1, local_rows, width)

    middle = (count + 1) // 2 * local_rows
    attn_near, attn_far = tree_reduce(
        by_shard(heads[:middle], out_weight), by_shard(heads[middle:], out_weight)
    )
    attn_far, *later = tie(attn_far, *raw[1:])
    weights += [blocks_of(v) for v in later]
    hidden = token_values + attn_near + attn_far.astype(F32)
    scale_mlp = rms_scale(hidden)
    mlp_in = (hidden * scale_mlp * mlp_gain).astype(BF)

    order = ring_order(dp_size)
    all_places = jnp.array([order.index(i) for i in range(dp_size)], jnp.int32)
    place = all_places[dp_index]
    walk = jnp.array(order, jnp.int32)
    steps = jnp.arange(dp_size, dtype=jnp.int32)
    at = jnp.stack(
        [
            jnp.full_like(steps, dp_index * experts_local),
            walk[(place - steps) % dp_size],
            walk[(place + steps) % dp_size],
        ],
        axis=1,
    ).astype(jnp.int32)
    x = [
        jnp.concatenate([mlp_in[start : start + half], c], axis=0)
        for start, c in zip((0, half), codes)
    ]
    kept = None
    backs, dots, came = [], [], []
    for k in range(dp_size):
        if k > 0:
            x = [ring_move(x[0], order, 1), ring_move(x[1], order, -1)]
        if k == 1:
            *x, all_output_grad = tie(*x, all_output_grad)
        if k == 2:
            *x, dots[0] = tie(*x, dots[0])
        if k > 2:
            *x, a, b, dots[k - 2] = tie(*x, *came[k - 2], dots[k - 2])
            came[k - 2] = (a, b)
        back, pair_dot, kept = expert_step(
            k, dp_size, at[k], x, all_output_grad, router_weight, weights, kept
        )
        backs.append(back)
        dots.append(pair_dot)
        came.append(None)
        if k > 0:
            if k > 1:
                back = [(n.astype(F32) + c.astype(F32)).astype(BF) for n, c in zip(back, came[k - 1])]
            came[k] = (ring_move(back[0], order, 1), ring_move(back[1], order, -1))
    mixes, all_rows, all_grads, *factors = kept
    grad_rows = jnp.concatenate(
        [n.astype(F32) + c.astype(F32) for n, c in zip(backs[0], came[-1])], axis=0
    )
    grad_rows, mixes = tie(grad_rows, mixes)
    mixture = lax.psum_scatter(mixes, "dp", scatter_dimension=0, tiled=True)

    all_dots = jnp.stack(dots)

    def pick(index):
        return jnp.sum(
            jnp.where((index[:, None] == steps[None, :])[:, :, None, None], all_dots[None], 0.0),
            axis=1,
        )

    send = jnp.where(
        jnp.arange(local_rows) < half,
        pick((place - all_places) % dp_size),
        pick((all_places - place) % dp_size),
    )
    grad_gates = lax.all_to_all(send, "dp", 0, 0, tiled=True).reshape(experts, local_rows).T

    code_here = code.T
    logits = jnp.dot(mlp_in, router_weight, preferred_element_type=F32)
    logits = jnp.where(code_here > 0.5, logits, NEG)
    chosen_exp = jnp.exp(logits - jnp.max(logits, axis=1, keepdims=True))
    gates = chosen_exp / jnp.sum(chosen_exp, axis=1, keepdims=True)
    weighted_sum = jnp.sum(gates * grad_gates, axis=1, keepdims=True)
    grad_logits = (gates * (grad_gates - weighted_sum)).astype(BF)
    router_part = jnp.dot(mlp_in.T, grad_logits, preferred_element_type=F32)
    grad_mlp_in = grad_rows + jnp.dot(grad_logits, router_weight.T, preferred_element_type=F32)
    grad_hidden_norm, mlp_gain_part = norm_back(grad_mlp_in, hidden, scale_mlp, mlp_gain)
    grad_hidden = output_grad.astype(F32) + grad_hidden_norm
    grad_attn = grad_hidden.astype(BF)

    grad_attn, *factors = tie(grad_attn, *factors)
    grad_blocks = tree_gather(grad_attn)
    expert_parts = [expert_grads(factors, all_rows, all_grads, count, 0)]
    grad_blocks[1], expert_parts[0][1] = tie(grad_blocks[1], expert_parts[0][1])
    expert_sums = [tree_reduce(*expert_parts[0])]
    grad_head_blocks = [
        jnp.dot(block, out_weight.T, preferred_element_type=F32).astype(BF) for block in grad_blocks
    ]
    out_part = jnp.dot(
        heads.T, jnp.concatenate(grad_blocks, axis=0), preferred_element_type=F32
    ).astype(BF)
    dqkv = attend_backward(
        shard_ids, parent_block, qkv, grad_head_blocks, kv, per_group, seg
    )
    out_stages = sum_over_dp(out_part, ((0, width),), ring, pairs)
    out_came = next(out_stages)
    near, across = expert_sums[0]
    dqkv, across, *tied = tie(dqkv, across, *factors, *out_came)
    expert_sums[0] = (near, across)
    factors, out_came = tied[:3], tied[3:]
    normed_rows = jnp.concatenate([v[:local_rows] for v in tree_normed], axis=0)
    qkv_part = jnp.dot(normed_rows.T, dqkv, preferred_element_type=F32).astype(BF)
    spread = qkv_weight.T
    spans = ((0, q_width), (q_width, q_width + k_width), (q_width + k_width, qkv_part.shape[1]))
    qkv_stages = sum_over_dp(qkv_part, spans, ring, pairs)
    qkv_came = next(qkv_stages)
    normed_near, normed_far = tree_reduce(
        by_shard(dqkv[:middle], spread), by_shard(dqkv[middle:], spread)
    )
    normed_far, mixture = tie(normed_far, mixture)
    output = (hidden + mixture.astype(F32)).astype(BF)
    grad_normed = normed_near + normed_far.astype(F32)
    grad_token_norm, attn_gain_part = norm_back(grad_normed, token_values, scale_attn, attn_gain)
    input_grad = grad_hidden + grad_token_norm

    out_came = out_stages.send(out_came)
    qkv_came = qkv_stages.send(qkv_came)
    *out_came, total, factors[0] = tie(*out_came, *qkv_came, factors[0])
    expert_parts += [
        expert_grads(factors, all_rows, all_grads, count, n) for n in range(1, experts_local)
    ]
    out_came = out_stages.send(out_came)
    (qkv_came,) = qkv_stages.send([total])
    qkv_came, expert_parts[-1][1] = tie(qkv_came, expert_parts[-1][1])
    expert_sums += [tree_reduce(*p) for p in expert_parts[1:]]
    (out_grad,) = out_stages.send(out_stages.send(out_came))
    (piece,) = qkv_stages.send([qkv_came])
    near, across = expert_sums[-1]
    piece, across = tie(piece, across)
    expert_sums[-1] = (near, across)
    query_grad, key_grad, value_grad = qkv_stages.send([piece])
    expert_grad = [
        jnp.stack([near[i] + across[i].astype(F32) for near, across in expert_sums])
        for i in range(3)
    ]
    small = jnp.concatenate(
        [router_part.T, mlp_gain_part.reshape(1, -1), attn_gain_part.reshape(1, -1)], axis=0
    )
    small = sum_over_all(small)
    return (
        output,
        input_grad,
        small[experts + 1],
        query_grad,
        key_grad,
        value_grad,
        out_grad,
        small[experts],
        small[:experts].T,
        expert_grad[0],
        expert_grad[1],
        jnp.swapaxes(expert_grad[2], 1, 2),
    )


def solution(mesh):
    every = ("dp", "row", "col")
    tree = ("row", "col")
    return jax.shard_map(
        shards_program,
        mesh=mesh,
        in_specs=(
            P(every, None),
            P(),
            P(None, tree),
            P(None, tree),
            P(None, tree),
            P(tree, None),
            P(),
            P(),
            P("dp", None, tree),
            P("dp", None, tree),
            P("dp", tree, None),
            P(every, None),
            P(every, None),
            P(every, None),
            P(every),
            P(every),
        ),
        out_specs=(
            P(every, None),
            P(every, None),
            P(),
            P(None, tree),
            P(None, tree),
            P(None, tree),
            P(tree, None),
            P(),
            P(),
            P("dp", None, tree),
            P("dp", None, tree),
            P("dp", tree, None),
        ),
        check_vma=False,
    )
```

```python
import functools
import math

import jax
import jax.numpy as jnp
from jax import lax
from jax.experimental import pallas as pl
from jax.experimental.pallas import tpu as pltpu
from jax.sharding import PartitionSpec as P

HD = 64
TOPK = 8
QT = 128
EPS = 1e-05
NEG = -1e30
MIB = 2**20
BF = jnp.bfloat16
F32 = jnp.float32
VMEM = pl.BlockSpec(memory_space=pltpu.VMEM)
SMEM = pl.BlockSpec(memory_space=pltpu.SMEM)
ANY = pl.BlockSpec(memory_space=pl.ANY)


def dot(a, b, ca, cb):
    return lax.dot_general(a, b, (((ca,), (cb,)), ((), ())), preferred_element_type=F32)


def tie(*values):
    return lax.optimization_barrier(values)


def stack_heads(block, count):
    return jnp.concatenate([block[:, h * HD : (h + 1) * HD] for h in range(count)], axis=0)


def causal_mask(per_group):
    key = lax.broadcasted_iota(jnp.int32, (QT, QT), 0)
    query = lax.broadcasted_iota(jnp.int32, (QT, QT), 1)
    return jnp.concatenate([key <= query] * per_group, axis=1)


def tile_masks(seg, parents, per_group):
    key = lax.broadcasted_iota(jnp.int32, (QT, QT), 0)
    query = lax.broadcasted_iota(jnp.int32, (QT, QT), 1)
    own = (key <= query) & (key // seg == query // seg)
    par = None
    for j, parent in enumerate(parents):
        hit = (key // seg == j) & (query // seg == j) & (parent > 0)
        par = hit if par is None else par | hit
    return (
        jnp.concatenate([own] * per_group, axis=1),
        jnp.concatenate([par] * per_group, axis=1),
    )


def softmax_parts(keys, masks, q):
    parts = []
    top = None
    for k, mask in zip(keys, masks):
        s = dot(k, q, 1, 1)
        if mask is not None:
            s = jnp.where(mask, s, NEG)
        parts.append(s)
        m = jnp.max(s, axis=0, keepdims=True)
        top = m if top is None else jnp.maximum(top, m)
    probs = []
    total = None
    for s in parts:
        e = jnp.exp(s - top)
        t = jnp.sum(e, axis=0, keepdims=True)
        total = t if total is None else total + t
        probs.append(e)
    inverse = 1.0 / total
    return [e * inverse for e in probs]


def each_tile(qkv_ref, parent_ref, kv, per_group, seg, work):
    rows = qkv_ref.shape[0]
    trunk = 8 * seg
    segs = QT // seg
    q_width = kv * per_group * HD
    causal = causal_mask(per_group)

    def columns(g):
        return q_width + g * HD, q_width + kv * HD + g * HD

    for i in range(trunk // QT):
        for g in range(kv):
            kc, vc = columns(g)
            spans = ([(0, i * QT)] if i > 0 else []) + [(i * QT, QT)]
            keys = [qkv_ref[a : a + n, kc : kc + HD] for a, n in spans]
            values = [qkv_ref[a : a + n, vc : vc + HD] for a, n in spans]
            masks = ([None] if i > 0 else []) + [causal]
            work(i * QT, g, keys, values, masks, [[s] for s in spans])

    def body(i, carry):
        first = pl.multiple_of(trunk + i * QT, QT)
        parents = [parent_ref[8 + i * segs + j] for j in range(segs)]
        starts = [pl.multiple_of(p * seg, seg) for p in parents]
        own, par = tile_masks(seg, parents, per_group)

        def take(c):
            blocks = [qkv_ref[pl.ds(s, seg), c : c + HD] for s in starts]
            return [
                qkv_ref[0:trunk, c : c + HD],
                qkv_ref[pl.ds(first, QT), c : c + HD],
                jnp.concatenate(blocks, axis=0) if segs > 1 else blocks[0],
            ]

        for g in range(kv):
            kc, vc = columns(g)
            places = [[(0, trunk)], [(first, QT)], [(s, seg) for s in starts]]
            work(first, g, take(kc), take(vc), [None, own, par], places)
        return carry

    lax.fori_loop(0, (rows - trunk) // QT, body, 0)


def attend_forward_kernel(kv, per_group, seg, blocks, shard_ref, parent_ref, *refs):
    ins, row_refs, refs = refs[:blocks], refs[blocks : 2 * blocks], refs[2 * blocks :]
    qkv_ref, out_ref, rows_ref, full_ref, row_sem = refs
    local = out_ref.shape[0] // blocks
    copies = [
        pltpu.make_async_copy(
            row_refs[j].at[pl.ds(0, local)], rows_ref.at[pl.ds(j * local, local)], row_sem.at[j]
        )
        for j in range(blocks)
    ]
    for copy in copies:
        copy.start()
    scale = BF(1.0 / math.sqrt(HD))
    for j in range(blocks):
        at = pl.multiple_of(shard_ref[j] * local, 64)
        qkv_ref[pl.ds(at, local), :] = ins[j][0:local, :]

    def work(first, g, keys, values, masks, places):
        block = qkv_ref[pl.ds(first, QT), g * per_group * HD : (g + 1) * per_group * HD]
        probs = softmax_parts(keys, masks, stack_heads(block, per_group) * scale)
        total = None
        for p, v in zip(probs, values):
            o = dot(v, p.astype(BF), 0, 0)
            total = o if total is None else total + o
        for h in range(per_group):
            c = (g * per_group + h) * HD
            full_ref[pl.ds(first, QT), c : c + HD] = total[:, h * QT : (h + 1) * QT].T.astype(BF)

    each_tile(qkv_ref, parent_ref, kv, per_group, seg, work)
    for j in range(blocks):
        at = pl.multiple_of(shard_ref[j] * local, 64)
        out_ref[j * local : (j + 1) * local, :] = full_ref[pl.ds(at, local), :]
    for copy in copies:
        copy.wait()


def attend_forward(shards, parent_block, qkv_blocks, row_blocks, kv, per_group, seg):
    blocks = len(qkv_blocks)
    wide = qkv_blocks[0].shape[1]
    rows = 20 * seg
    width = kv * per_group * HD
    cells = rows * 12 * seg * kv * per_group
    return pl.pallas_call(
        functools.partial(attend_forward_kernel, kv, per_group, seg, blocks),
        out_shape=[
            jax.ShapeDtypeStruct((rows, wide), BF),
            jax.ShapeDtypeStruct((rows, width), BF),
            jax.ShapeDtypeStruct((rows, row_blocks[0].shape[1]), BF),
        ],
        in_specs=[SMEM, SMEM] + [VMEM] * blocks + [ANY] * blocks,
        out_specs=[VMEM, VMEM, ANY],
        scratch_shapes=[pltpu.VMEM((rows, width), BF), pltpu.SemaphoreType.DMA((blocks,))],
        compiler_params=pltpu.CompilerParams(vmem_limit_bytes=40 * MIB),
        cost_estimate=pl.CostEstimate(
            flops=16 * HD * cells, bytes_accessed=4 * rows * wide, transcendentals=cells
        ),
        name="attend_forward",
    )(shards, parent_block, *qkv_blocks, *row_blocks)


def attend_backward_kernel(kv, per_group, seg, blocks, shard_ref, parent_ref, qkv_ref, *refs):
    ins, (out_ref, do_ref, full_ref, dk_ref, dv_ref) = refs[:blocks], refs[blocks:]
    local = ins[0].shape[0]
    q_width = kv * per_group * HD
    scale = 1.0 / math.sqrt(HD)
    for j in range(blocks):
        at = pl.multiple_of(shard_ref[j] * local, 64)
        do_ref[pl.ds(at, local), :] = ins[j][...]
    dk_ref[...] = jnp.zeros_like(dk_ref)
    dv_ref[...] = jnp.zeros_like(dv_ref)

    def work(first, g, keys, values, masks, places):
        span = slice(g * per_group * HD, (g + 1) * per_group * HD)
        q = stack_heads(qkv_ref[pl.ds(first, QT), span], per_group) * BF(scale)
        d = stack_heads(do_ref[pl.ds(first, QT), span], per_group)
        probs = softmax_parts(keys, masks, q)
        grads = [dot(v, d, 1, 1) for v in values]
        delta = None
        for p, grad in zip(probs, grads):
            t = jnp.sum(grad * p, axis=0, keepdims=True)
            delta = t if delta is None else delta + t
        dq = None
        for p, grad, k, place in zip(probs, grads, keys, places):
            ds = (p * (grad - delta)).astype(BF)
            dk = dot(ds, q, 1, 0)
            dv = dot(p.astype(BF), d, 1, 0)
            o = dot(k, ds, 0, 0)
            dq = o if dq is None else dq + o
            at = 0
            for start, size in place:
                dk_ref[pl.ds(start, size), g * HD : (g + 1) * HD] += dk[at : at + size]
                dv_ref[pl.ds(start, size), g * HD : (g + 1) * HD] += dv[at : at + size]
                at += size
        dq = dq * scale
        for h in range(per_group):
            c = (g * per_group + h) * HD
            full_ref[pl.ds(first, QT), c : c + HD] = dq[:, h * QT : (h + 1) * QT].T.astype(BF)

    each_tile(qkv_ref, parent_ref, kv, per_group, seg, work)
    full_ref[:, q_width : q_width + kv * HD] = dk_ref[...].astype(BF)
    full_ref[:, q_width + kv * HD : q_width + 2 * kv * HD] = dv_ref[...].astype(BF)
    for j in range(blocks):
        at = pl.multiple_of(shard_ref[j] * local, 64)
        out_ref[j * local : (j + 1) * local, :] = full_ref[pl.ds(at, local), :]


def attend_backward(shards, parent_block, qkv, grad_blocks, kv, per_group, seg):
    blocks = len(grad_blocks)
    rows, wide = qkv.shape
    width = kv * per_group * HD
    cells = rows * 12 * seg * kv * per_group
    return pl.pallas_call(
        functools.partial(attend_backward_kernel, kv, per_group, seg, blocks),
        out_shape=jax.ShapeDtypeStruct((rows, wide), BF),
        in_specs=[SMEM, SMEM, VMEM] + [VMEM] * blocks,
        out_specs=VMEM,
        scratch_shapes=[
            pltpu.VMEM((rows, width), BF),
            pltpu.VMEM((rows, wide), BF),
            pltpu.VMEM((rows, kv * HD), F32),
            pltpu.VMEM((rows, kv * HD), F32),
        ],
        compiler_params=pltpu.CompilerParams(vmem_limit_bytes=40 * MIB),
        cost_estimate=pl.CostEstimate(
            flops=40 * HD * cells, bytes_accessed=6 * rows * wide, transcendentals=cells
        ),
        name="attend_backward",
    )(shards, parent_block, qkv, *grad_blocks)


def expert_kernel(first, blocks, fresh, local, at_ref, xa_ref, xb_ref, packet_ref, router_ref, *refs):
    count = len(blocks)
    weight_refs, refs = refs[: sum(blocks)], refs[sum(blocks) :]
    if not fresh:
        refs = refs[5:]
    back_a_ref, back_b_ref, mix_a_ref, mix_b_ref, dot_ref, rows_ref, grad_rows_ref = refs[:7]
    kept_refs = refs[7:10]
    weights, held, g_held, x_held, code_held, weight_sem, held_sem, row_sem, g_sem = refs[10:]
    half = back_a_ref.shape[0]
    rows = 2 * half
    experts = router_ref.shape[1]
    extra = code_held.shape[1]
    x_came, codes_came, arrived = [], [], []
    for i, ref in enumerate((xa_ref, xb_ref)):
        spot = i * (half + extra)
        if not local:
            spot = pl.multiple_of(at_ref[1 + i] * (rows + 2 * extra) + spot, 16)
        span = pl.ds(i * half, half)
        x_came.append(pltpu.make_async_copy(ref, x_held.at[span], g_sem.at[i]))
        codes_came.append(
            pltpu.make_async_copy(
                packet_ref.at[pl.ds(spot + half, extra)], code_held.at[i], g_sem.at[2 + i]
            )
        )
        arrived.append(
            pltpu.make_async_copy(packet_ref.at[pl.ds(spot, half)], g_held.at[span], g_sem.at[4 + i])
        )
    for copy in x_came + codes_came + arrived:
        copy.start()
    loads = []
    for i in (2, 0, 1):
        for n in range(count):
            at = sum(blocks[:n])
            for j in range(blocks[n]):
                source = weight_refs[at + j].at[i]
                unit = source.shape[1]
                copy = pltpu.make_async_copy(
                    source,
                    weights[i].at[n, :, pl.ds(j * unit, unit)],
                    weight_sem.at[i * sum(blocks) + at + j],
                )
                loads.append((n, i, copy))
    for n in range(count):
        for m, _, copy in loads:
            if m == n:
                copy.start()

    def loaded(n, i):
        for m, k, copy in loads:
            if (m, k) == (n, i):
                copy.wait()

    for copy in x_came:
        copy.wait()
    stores = [pltpu.make_async_copy(x_held, rows_ref.at[pl.ds(first, rows)], row_sem.at[0])]
    stores[0].start()
    x = x_held[...]
    for copy in codes_came:
        copy.wait()
    code = jnp.concatenate(
        [code_held[i, 0:experts, 0:half].astype(F32).T for i in range(2)], axis=0
    )
    logits = dot(x, router_ref[...], 1, 0)
    logits = jnp.where(code > 0.5, logits, NEG)
    top = jnp.max(logits, axis=1, keepdims=True)
    e = jnp.exp(logits - top)
    kept = jnp.where(code > 1.5, 1.0, 0.0)
    gates = kept * e / jnp.sum(e, axis=1, keepdims=True)
    lane = lax.broadcasted_iota(jnp.int32, gates.shape, 1)
    for copy in arrived:
        copy.wait()
    copy = pltpu.make_async_copy(g_held, grad_rows_ref.at[pl.ds(first, rows)], row_sem.at[1])
    copy.start()
    stores.append(copy)
    g = g_held[...]
    mix = None
    back = None
    for n in range(count):
        mine = lane == at_ref[0] + n
        weight = jnp.sum(jnp.where(mine, gates, 0.0), axis=1, keepdims=True)
        keep = jnp.sum(jnp.where(mine, kept, 0.0), axis=1, keepdims=True)
        loaded(n, 2)
        grad = dot(g, weights[2][n], 1, 0)
        loaded(n, 0)
        gate_pre = dot(x, weights[0][n], 1, 0)
        loaded(n, 1)
        up_pre = dot(x, weights[1][n], 1, 0)
        sig = 1.0 / (1.0 + jnp.exp(-gate_pre))
        silu = gate_pre * sig
        act = (silu * up_pre).astype(BF).astype(F32)
        pair_dot = jnp.sum(act * grad, axis=1, keepdims=True) * keep
        dot_ref[n : n + 1, :] = pair_dot.T
        weighted = (act * weight).astype(BF)
        grad = grad * weight
        dgate = (grad * up_pre * sig * (1.0 + gate_pre * (1.0 - sig))).astype(BF)
        dup = (grad * silu).astype(BF)
        for i, value in enumerate((weighted, dgate, dup)):
            held[i][n] = value
            copy = pltpu.make_async_copy(
                held[i].at[n], kept_refs[i].at[n, pl.ds(first, rows)], held_sem.at[n * 3 + i]
            )
            copy.start()
            stores.append(copy)
        m = dot(weighted, weights[2][n], 1, 1)
        mix = m if mix is None else mix + m
        b = dot(dgate, weights[0][n], 1, 1) + dot(dup, weights[1][n], 1, 1)
        back = b if back is None else back + b
    mix = mix.astype(BF)
    mix_a_ref[...] = mix[:half]
    mix_b_ref[...] = mix[half:]
    back = back.astype(BF)
    back_a_ref[...] = back[:half]
    back_b_ref[...] = back[half:]
    for copy in stores:
        copy.wait()


def expert_step(k, steps, local, at, x, packets, router, weights, buffers):
    width = x[0].shape[1]
    extra = -(-router.shape[1] // 16) * 16
    half = x[0].shape[0]
    rows = 2 * half
    count = len(weights)
    hidden = sum(w.shape[2] for w in weights[0])
    half_shape = jax.ShapeDtypeStruct((half, width), BF)
    big_shapes = [jax.ShapeDtypeStruct((steps * rows, width), BF)] * 2
    big_shapes += [jax.ShapeDtypeStruct((count, steps * rows, hidden), BF)] * 3
    operands = [at, *x, packets, router, *[b for w in weights for b in w]]
    specs = [SMEM, ANY, ANY, ANY, VMEM] + [ANY] * (len(operands) - 5)
    aliases = {}
    if buffers is not None:
        aliases = {len(operands) + i: 5 + i for i in range(5)}
        operands += buffers
        specs += [ANY] * 5
    blocks = [len(w) for w in weights]
    out = pl.pallas_call(
        functools.partial(expert_kernel, k * rows, blocks, buffers is None, local),
        out_shape=[half_shape] * 4 + [jax.ShapeDtypeStruct((count, rows), F32)] + big_shapes,
        in_specs=specs,
        out_specs=[VMEM] * 5 + [ANY] * 5,
        input_output_aliases=aliases,
        scratch_shapes=[
            [pltpu.VMEM((count, width, hidden), BF)] * 3,
            [pltpu.VMEM((count, rows, hidden), BF)] * 3,
            pltpu.VMEM((rows, width), BF),
            pltpu.VMEM((rows, width), BF),
            pltpu.VMEM((2, extra, width), BF),
            pltpu.SemaphoreType.DMA((3 * sum(blocks),)),
            pltpu.SemaphoreType.DMA((count * 3,)),
            pltpu.SemaphoreType.DMA((2,)),
            pltpu.SemaphoreType.DMA((6,)),
        ],
        compiler_params=pltpu.CompilerParams(vmem_limit_bytes=40 * MIB),
        cost_estimate=pl.CostEstimate(
            flops=2 * rows * width * hidden * count * 6,
            bytes_accessed=6 * width * hidden * count + 10 * rows * width,
            transcendentals=rows * hidden * count,
        ),
        name="expert_step",
    )(*operands)
    return out[:2], out[2:4], out[4], out[5:]


def expert_grad_kernel(act_ref, dgate_ref, dup_ref, x_ref, g_ref, *outs):
    half, _, _, unit = outs[0].shape
    for i, (rows, ref) in enumerate(((x_ref, dgate_ref), (x_ref, dup_ref), (g_ref, act_ref))):
        grad = dot(rows[...], ref[0], 0, 0).astype(BF)
        for j in range(2 * half):
            outs[j // half][j % half, i] = grad[:, j * unit : (j + 1) * unit]


def expert_grads(kept, x, g, parts, expert):
    _, rows, hidden = kept[0].shape
    width = x.shape[1]
    unit = hidden // parts
    tile = 512 if width % 512 == 0 else width
    half = parts // 2
    return list(pl.pallas_call(
        expert_grad_kernel,
        grid=(width // tile,),
        out_shape=[jax.ShapeDtypeStruct((half, 3, width, unit), BF)] * 2,
        in_specs=[pl.BlockSpec((1, rows, hidden), lambda i: (expert, 0, 0))] * 3
        + [pl.BlockSpec((rows, tile), lambda i: (0, i))] * 2,
        out_specs=[pl.BlockSpec((half, 3, tile, unit), lambda i: (0, 0, i, 0))] * 2,
        compiler_params=pltpu.CompilerParams(vmem_limit_bytes=56 * MIB),
        cost_estimate=pl.CostEstimate(
            flops=6 * rows * width * hidden,
            bytes_accessed=12 * width * hidden,
            transcendentals=0,
        ),
        name="expert_grads",
    )(*kept, x, g))


def finish_kernel(terms, *refs):
    ins, outs = refs[: len(refs) - 3], refs[len(refs) - 3 :]
    for n in range(len(ins) // terms):
        refs = ins[n * terms : (n + 1) * terms]
        for i in range(3):
            total = refs[-1][i].astype(F32)
            for ref in refs[:-1]:
                total = total + ref[0, i].astype(F32)
            outs[i][n] = total.T if i == 2 else total


def finish_grads(sums):
    count = len(sums)
    _, width, unit = sums[0][1].shape
    terms = len(sums[0][0]) + 1
    first = pl.BlockSpec((1, 3, width, unit), lambda i: (0, 0, 0, 0))
    specs = [first] * (terms - 1) + [pl.BlockSpec((3, width, unit), lambda i: (0, 0, 0))]
    shapes = [(count, width, unit), (count, width, unit), (count, unit, width)]
    return pl.pallas_call(
        functools.partial(finish_kernel, terms),
        grid=(1,),
        out_shape=[jax.ShapeDtypeStruct(v, F32) for v in shapes],
        in_specs=specs * count,
        out_specs=[pl.BlockSpec(v, lambda i: (0, 0, 0)) for v in shapes],
        compiler_params=pltpu.CompilerParams(vmem_limit_bytes=48 * MIB),
        name="finish_grads",
    )(*[v for near, across in sums for v in (*near, across)])


def tree_moves():
    rows, cols = lax.axis_size("row"), lax.axis_size("col")
    if rows == 2 and cols == 2:
        swap = [(0, 1), (1, 0)]
        me = lax.axis_index("row") * 2 + lax.axis_index("col")

        def gather(x, again=None, finish=True):
            across = lax.ppermute(x if again is None else again, "row", swap)
            beside = lax.ppermute(x, "col", swap)
            blocks = [x, across, beside]
            return finish_gather(blocks) if finish else blocks

        def finish_gather(blocks):
            return blocks + [lax.ppermute(blocks[1], "col", swap)]

        def reduce_first(mine, other):
            return [mine, lax.ppermute(other, "col", swap)]

        def reduce_second(mine, came):
            far = (mine[1].astype(F32) + came[1].astype(F32)).astype(BF)
            return [mine, came], lax.ppermute(far, "row", swap)

        reduce = (reduce_first, reduce_second)

        return [me, me ^ 2, me ^ 1, me ^ 3], gather, finish_gather, reduce

    count = rows * cols
    both = ("row", "col")

    def gather(x, again=None, finish=True):
        whole = lax.all_gather(x if again is None else again, both, axis=0)
        return [whole[i] for i in range(count)]

    def reduce_second(mine, other):
        blocks = jnp.concatenate([mine, other], axis=0)
        total = lax.psum_scatter(blocks, both, scatter_dimension=0)
        return [total[None]], jnp.zeros_like(total)

    reduce = (lambda mine, other: [mine, other], reduce_second)

    return [jnp.int32(i) for i in range(count)], gather, list, reduce


def half_orders(count):
    ys = count // 4
    near = [y for y in range(ys)] + [ys + y for y in reversed(range(ys))]
    return [near, [partner_of(i, count) for i in near]]


def partner_of(index, count):
    ys = count // 4
    return (3 - index // ys) * ys + index % ys


def ring_order(count):
    ys = count // 4
    order = []
    for y in range(ys):
        zs = range(4) if y % 2 == 0 else reversed(range(4))
        order += [z * ys + y for z in zs]
    return order


def ring_move(x, order, by):
    n = len(order)
    return lax.ppermute(x, "dp", [(order[i], order[(i + by) % n]) for i in range(n)])


def add_halves(came, own, last):
    total = [c.astype(F32) + n.astype(F32) for c, n in zip(came, own)]
    if last:
        return [jnp.concatenate(total, axis=0)]
    return list(tie(*[t.astype(BF) for t in total]))


def walk_hops(parts, order):
    n = len(order)
    a, b = parts[1]
    for k in range(1, n):
        came = yield [ring_move(a, order, 1), ring_move(b, order, -1)]
        total = add_halves(came, parts[(k + 1) % n], k == n - 1)
        if k < n - 1:
            a, b = total
    yield total


class Ring:
    def __init__(self, count, dp_index):
        self.orders = half_orders(count)
        self.steps = len(self.orders[0])
        at = [[o.index(i) for o in self.orders if i in o][0] for i in range(count)]
        self.place = jnp.array(at, jnp.int32)[dp_index]
        self.four = self.steps == 4
        if self.four:
            self.places = [lax.rem(self.place + k, 4) for k in (0, 3, 1, 2)]
        else:
            self.places = [jnp.int32(k) for k in range(self.steps)]

    def shift(self, x, by):
        n = self.steps
        return lax.ppermute(
            x, "dp", [(o[i], o[(i + by) % n]) for o in self.orders for i in range(n)]
        )

    def gather(self, x):
        if not self.four:
            whole = lax.all_gather(x, "dp", axis=0, axis_index_groups=self.orders)
            return [[whole[k]] for k in range(self.steps)]
        return self.gather_second(x, self.gather_first(x))

    def gather_first(self, x):
        return [self.shift(x, 1), self.shift(x, -1)] if self.four else [x]

    def gather_second(self, x, came):
        if not self.four:
            return self.gather(x)
        half = x.shape[0] // 2
        left, right = came
        a, b = right[:half], left[half:]
        return [[x], [left], [right], [self.shift(a, -1), self.shift(b, 1)]]

    def reduce_stages(self, parts):
        if not self.four:
            yield []
            whole = jnp.stack([jnp.concatenate(p, axis=0) for p in parts])
            yield lax.psum_scatter(
                whole, "dp", scatter_dimension=0, axis_index_groups=self.orders
            ).astype(F32)
            return
        (own,), (left,), (right,), (far_a, far_b) = parts
        half = far_a.shape[0]
        a, b = yield [self.shift(far_a, 1), self.shift(far_b, -1)]
        right = jnp.concatenate(
            [(right[:half].astype(F32) + a.astype(F32)).astype(BF), right[half:]], axis=0
        )
        left = jnp.concatenate(
            [left[:half], (left[half:].astype(F32) + b.astype(F32)).astype(BF)], axis=0
        )
        yield own.astype(F32) + (
            self.shift(right, 1).astype(F32) + self.shift(left, -1).astype(F32)
        )

    def reduce(self, parts):
        stages = self.reduce_stages(parts)
        return stages.send(next(stages))


def small_sum(value, part):
    sizes = [lax.axis_size(name) for name in ("dp", "row", "col")]
    if sizes != [8, 2, 2]:
        return lax.psum(value, ("col", "row", "dp")[part])
    hops = [[("col", 2, 1), ("dp", 8, 1)], [("row", 2, 1)], [("dp", 8, 2), ("dp", 8, 4)]]
    for name, size, bit in hops[part]:
        value = value + lax.ppermute(value, name, [(i, i ^ bit) for i in range(size)])
    return value


def write_kernel(spans, sizes, turned, place_ref, *refs):
    pieces, outs = refs[: sum(sizes)], refs[sum(sizes) :]
    at = 0
    for k, size in enumerate(sizes):
        chunk = jnp.concatenate([ref[...] for ref in pieces[at : at + size]], axis=0).astype(F32)
        rows = chunk.shape[0]
        at += size
        for n, ((a, b), out) in enumerate(zip(spans, outs)):
            if n == turned:
                start = pl.multiple_of(place_ref[k] * rows, 128)
                out[:, pl.ds(start, rows)] = chunk[:, a:b].T
            else:
                start = pl.multiple_of(place_ref[k] * rows, 16)
                out[pl.ds(start, rows), :] = chunk[:, a:b]


def sum_over_dp(parts, spans, ring, pairs):
    rows = parts[0].shape[0]
    chunk = rows // ring.steps

    def cut(place, at, size):
        return jnp.concatenate(
            [lax.dynamic_slice(v, (place * chunk + at, 0), (size, v.shape[1])) for v in parts],
            axis=1,
        )

    terms = [[cut(place, 0, chunk)] for place in ring.places]
    if ring.four:
        half = chunk // 2
        terms[3] = [cut(ring.places[3], 0, half), cut(ring.places[3], half, half)]
    stages = ring.reduce_stages(terms)
    total = stages.send((yield next(stages)))
    total = (yield [total])[0].astype(BF)
    came = (yield [lax.ppermute(total, "dp", pairs)])[0]
    total = (total.astype(F32) + came.astype(F32)).astype(BF)
    pieces = ring.gather_second(total, (yield ring.gather_first(total)))
    pieces[-1] = yield pieces[-1]
    sizes = [len(p) for p in pieces]
    turned = len(spans) - 1 if chunk % 128 == 0 else None
    shapes = [
        jax.ShapeDtypeStruct((b - a, rows) if n == turned else (rows, b - a), F32)
        for n, (a, b) in enumerate(spans)
    ]
    sums = list(
        pl.pallas_call(
            functools.partial(write_kernel, spans, sizes, turned),
            out_shape=shapes,
            in_specs=[SMEM] + [VMEM] * sum(sizes),
            out_specs=[VMEM] * len(spans),
            compiler_params=pltpu.CompilerParams(vmem_limit_bytes=32 * MIB),
            name="write_grads",
        )(jnp.stack(ring.places).astype(jnp.int32), *[p for pair in pieces for p in pair])
    )
    if turned is None:
        sums[-1] = sums[-1].T
    yield sums


def rms_scale(values):
    return lax.rsqrt(jnp.mean(values * values, axis=-1, keepdims=True) + EPS)


def norm_back(grad_normed, values, scale_rows, gain):
    weighted = grad_normed * gain
    grad_gain = jnp.sum(grad_normed * values * scale_rows, axis=0)
    inner = jnp.mean(weighted * values, axis=-1, keepdims=True)
    return (
        scale_rows * weighted - values * scale_rows * scale_rows * scale_rows * inner,
        grad_gain,
    )


def shards_program(
    tokens, attn_gain, query_weight, key_weight, value_weight, out_weight, mlp_gain, router_weight,
    gate_weight, up_weight, down_weight, output_grad, expert_ids, slot_rank, segment_ids, parent_ids,
):
    local_rows, width = tokens.shape
    half = local_rows // 2
    dp_size = lax.axis_size("dp")
    dp_index = lax.axis_index("dp")
    pairs = [(i, partner_of(i, dp_size)) for i in range(dp_size)]
    ring = Ring(dp_size, dp_index)
    shards, tree_gather, tree_finish, (reduce_first, reduce_second) = tree_moves()

    def tree_reduce(mine, other):
        return reduce_second(*reduce_first(mine, other))

    count = len(shards)
    shard_ids = jnp.stack(shards).astype(jnp.int32)
    kv = key_weight.shape[1] // HD
    per_group = query_weight.shape[1] // key_weight.shape[1]
    q_width = query_weight.shape[1]
    k_width = key_weight.shape[1]
    experts_local = gate_weight.shape[0]
    unit = gate_weight.shape[2]
    experts = experts_local * dp_size
    capacity = 5 * local_rows * TOPK // (4 * experts)
    seg = local_rows * count // 20

    token_values = tokens.astype(F32)
    scale_attn = rms_scale(token_values)
    normed = (token_values * scale_attn * attn_gain).astype(BF)
    step = math.gcd(seg, local_rows)
    each = local_rows // step
    labels = jnp.stack([segment_ids[::step], parent_ids[::step]]).astype(BF)
    normed_packet = jnp.concatenate(
        [normed, jnp.pad(labels, ((0, 14), (0, width - each)))], axis=0
    )
    tree_normed = tree_gather(normed_packet)
    labels = jnp.concatenate([v[local_rows : local_rows + 2, :each] for v in tree_normed], axis=1)
    spots = jnp.concatenate([s * each + jnp.arange(each, dtype=jnp.int32) for s in shards])
    spots = spots.astype(jnp.int32)
    block_spot = spots * step // seg
    is_parent = (labels[0][None, :] == labels[1][:, None]) & (labels[1][:, None] > 0)
    parent_spot = jnp.max(jnp.where(is_parent, block_spot[None, :], 0), axis=1)
    natural = jnp.arange(20, dtype=jnp.int32) * (seg // step)
    parent_block = jnp.sum(
        jnp.where(spots[None, :] == natural[:, None], parent_spot[None, :], 0), axis=1
    ).astype(jnp.int32)

    columns = jnp.arange(experts, dtype=jnp.int32)
    unranked = local_rows * TOPK
    rank = jnp.min(
        jnp.where(
            expert_ids.T[:, None, :] == columns[None, :, None], slot_rank.T[:, None, :], unranked
        ),
        axis=0,
    )
    slot = jnp.sum((rank[:, :, None] < rank[:, None, :]).astype(jnp.int32), axis=1)
    code = jnp.where(rank == unranked, 0.0, jnp.where(slot < capacity, 2.0, 1.0))
    extra = -(-experts // 16) * 16
    packet = []
    for at in (0, half):
        lanes = ((0, extra - experts), (0, width - half))
        packet += [output_grad[at : at + half], jnp.pad(code[:, at : at + half].astype(BF), lanes)]
    packet = jnp.concatenate(packet, axis=0)
    packets = lax.all_gather(packet, "dp", axis=0, tiled=True)
    tree_normed[1], packet = tie(tree_normed[1], packet)

    raw = [
        jnp.stack([gate_weight[n], up_weight[n], down_weight[n].T]) for n in range(experts_local)
    ]

    def joined(blocks):
        return blocks if unit % 128 == 0 else [jnp.concatenate(blocks, axis=2)]

    weights = [tree_gather(raw[0])]
    qkv_weight = jnp.concatenate([query_weight, key_weight, value_weight], axis=1)
    qkv_blocks = [
        jnp.dot(block, qkv_weight, preferred_element_type=F32).astype(BF) for block in tree_normed
    ]
    qkv, heads, normed_rows = attend_forward(
        shard_ids, parent_block, qkv_blocks, tree_normed, kv, per_group, seg
    )
    heads, weights[0][1] = tie(heads, weights[0][1])
    def by_shard(rows, weight):
        result = jnp.dot(rows, weight, preferred_element_type=F32).astype(BF)
        return result.reshape(-1, local_rows, width)

    middle = (count + 1) // 2 * local_rows
    attn_near, attn_far = tree_reduce(
        *tie(by_shard(heads[:middle], out_weight), by_shard(heads[middle:], out_weight))
    )
    attn_far, *later = tie(attn_far, *raw[1:], *weights[0][2:])
    weights[0][2:] = later[len(raw) - 1 :]
    weights += [tree_gather(v, again, False) for v, again in zip(raw[1:], later)]
    hidden = token_values + attn_far.astype(F32) + sum(v[0].astype(F32) for v in attn_near)
    scale_mlp = rms_scale(hidden)
    mlp_in = (hidden * scale_mlp * mlp_gain).astype(BF)

    order = ring_order(dp_size)
    all_places = jnp.array([order.index(i) for i in range(dp_size)], jnp.int32)
    place = all_places[dp_index]
    walk = jnp.array(order, jnp.int32)
    steps = jnp.arange(dp_size, dtype=jnp.int32)
    at = jnp.stack(
        [
            jnp.full_like(steps, dp_index * experts_local),
            walk[(place - steps) % dp_size],
            walk[(place + steps) % dp_size],
        ],
        axis=1,
    ).astype(jnp.int32)
    x = [mlp_in[:half], mlp_in[half:]]
    kept = None
    backs, mixes, dots, came = [], [], [], []
    coming = [ring_move(x[0], order, 1), ring_move(x[1], order, -1)]
    *coming, weights[-1][1] = tie(*coming, weights[-1][1])
    weights[1:] = [tree_finish(blocks) for blocks in weights[1:]]
    weights = [joined(blocks) for blocks in weights]
    for k in range(dp_size):
        if k > 0:
            x = coming
            if k > 1:
                x = [ring_move(x[0], order, 1), ring_move(x[1], order, -1)]
            if k > 1:
                *x, dots[k - 2] = tie(*x, dots[k - 2])
            if k > 2:
                *x, came[k - 2][0], came[k - 2][1] = tie(*x, *came[k - 2])
            coming = x
        back, mix, pair_dot, kept = expert_step(
            k,
            dp_size,
            k == 0,
            at[k],
            x,
            packets if k > 0 else packet,
            router_weight,
            weights,
            kept,
        )
        backs.append(back)
        mixes.append(list(mix))
        dots.append(pair_dot)
        came.append(None)
        if k > 0:
            if k > 1:
                *came[k - 1], dots[k] = tie(*came[k - 1], dots[k])
                back = add_halves(came[k - 1], back, False)
            if k == dp_size - 1:
                *back, mixes[1][0], mixes[1][1] = tie(*back, *mixes[1])
            came[k] = [ring_move(back[0], order, 1), ring_move(back[1], order, -1)]
    all_rows, all_grads, *factors = kept
    mlp_in, code, dots[-1] = tie(mlp_in, code, dots[-1])
    (grad_rows,) = add_halves(came[-1], backs[0], True)
    hops = walk_hops(mixes, order)
    hop = next(hops)
    left = dp_size - 1

    def next_hop(*values):
        nonlocal hop, left
        if left == 0:
            return values
        *values, a, b = tie(*values, *hop)
        hop = hops.send([a, b])
        left -= 1
        return values


    all_dots = jnp.stack(dots)

    def pick(index):
        return jnp.sum(
            jnp.where((index[:, None] == steps[None, :])[:, :, None, None], all_dots[None], 0.0),
            axis=1,
        )

    send = jnp.where(
        jnp.arange(local_rows) < half,
        pick((place - all_places) % dp_size),
        pick((all_places - place) % dp_size),
    )
    grad_gates = lax.all_to_all(send, "dp", 0, 0, tiled=True).reshape(experts, local_rows).T

    code_here = code.T
    logits = jnp.dot(mlp_in, router_weight, preferred_element_type=F32)
    logits = jnp.where(code_here > 0.5, logits, NEG)
    chosen_exp = jnp.exp(logits - jnp.max(logits, axis=1, keepdims=True))
    gates = chosen_exp / jnp.sum(chosen_exp, axis=1, keepdims=True)
    weighted_sum = jnp.sum(gates * grad_gates, axis=1, keepdims=True)
    grad_logits = (gates * (grad_gates - weighted_sum)).astype(BF)
    router_part = jnp.dot(mlp_in.T, grad_logits, preferred_element_type=F32)
    grad_mlp_in = grad_rows + jnp.dot(grad_logits, router_weight.T, preferred_element_type=F32)
    grad_hidden_norm, mlp_gain_part = norm_back(grad_mlp_in, hidden, scale_mlp, mlp_gain)
    grad_hidden = output_grad.astype(F32) + grad_hidden_norm
    grad_attn = grad_hidden.astype(BF)

    grad_attn, *factors = next_hop(*tie(grad_attn, *factors))
    grad_blocks = tree_gather(grad_attn)
    expert_parts = [expert_grads(factors, all_rows, all_grads, count, 0)]
    grad_blocks[1], expert_parts[0][1] = next_hop(*tie(grad_blocks[1], expert_parts[0][1]))
    expert_sums = [tree_reduce(*expert_parts[0])]
    grad_head_blocks = [
        jnp.dot(block, out_weight.T, preferred_element_type=F32).astype(BF) for block in grad_blocks
    ]
    (grad_head_blocks[-1],) = next_hop(grad_head_blocks[-1])
    dqkv = attend_backward(
        shard_ids, parent_block, qkv, grad_head_blocks, kv, per_group, seg
    )
    near, across = expert_sums[0]
    dqkv, across, *factors = next_hop(*tie(dqkv, across, *factors))
    expert_sums[0] = (near, across)
    qkv_part = jnp.dot(normed_rows.T, dqkv, preferred_element_type=F32).astype(BF)
    out_rows = jnp.concatenate(grad_blocks, axis=0)
    out_part = jnp.dot(out_rows.T, heads, preferred_element_type=F32).astype(BF)
    spans = (
        (0, q_width),
        (q_width, q_width + k_width),
        (q_width + k_width, q_width + 2 * k_width),
        (q_width + 2 * k_width, 2 * q_width + 2 * k_width),
    )
    stages = sum_over_dp([qkv_part, out_part], spans, ring, pairs)
    came = next(stages)
    spread = qkv_weight.T
    normed_near, normed_far = tree_reduce(
        by_shard(dqkv[:middle], spread), by_shard(dqkv[middle:], spread)
    )

    *came, factors[0] = next_hop(*tie(*came, factors[0]))
    came = stages.send(came)
    expert_parts += [
        expert_grads(factors, all_rows, all_grads, count, n) for n in range(1, experts_local)
    ]
    *came, normed_far, expert_parts[-1][1] = next_hop(
        *tie(*came, normed_far, expert_parts[-1][1])
    )
    came = stages.send(came)
    grad_normed = normed_far.astype(F32) + sum(v[0].astype(F32) for v in normed_near)
    grad_token_norm, attn_gain_part = norm_back(grad_normed, token_values, scale_attn, attn_gain)
    input_grad = grad_hidden + grad_token_norm
    small = jnp.concatenate(
        [router_part.T, mlp_gain_part.reshape(1, -1), attn_gain_part.reshape(1, -1)], axis=0
    )
    small = small_sum(small, 0)
    expert_sums += [tree_reduce(*p) for p in expert_parts[1:]]
    near, across = expert_sums[-1]
    across, small, *came = next_hop(*tie(across, small, *came))
    expert_sums[-1] = (near, across)
    while left > 0:
        next_hop()
    output = (hidden + hop[0]).astype(BF)
    came = stages.send(came)
    small = small_sum(small, 1)
    near, across = expert_sums[-1]
    across, *came = tie(across, *came)
    expert_sums[-1] = (near, across)
    came = stages.send(came)
    small, *came = tie(small, *came)
    query_grad, key_grad, value_grad, out_grad = stages.send(came)
    small = small_sum(small, 2)
    expert_grad = finish_grads(expert_sums)
    return (
        output,
        input_grad,
        small[experts + 1],
        query_grad,
        key_grad,
        value_grad,
        out_grad,
        small[experts],
        small[:experts].T,
        expert_grad[0],
        expert_grad[1],
        expert_grad[2],
    )


def solution(mesh):
    every = ("dp", "row", "col")
    tree = ("row", "col")
    return jax.shard_map(
        shards_program,
        mesh=mesh,
        in_specs=(
            P(every, None),
            P(),
            P(None, tree),
            P(None, tree),
            P(None, tree),
            P(tree, None),
            P(),
            P(),
            P("dp", None, tree),
            P("dp", None, tree),
            P("dp", tree, None),
            P(every, None),
            P(every, None),
            P(every, None),
            P(every),
            P(every),
        ),
        out_specs=(
            P(every, None),
            P(every, None),
            P(),
            P(None, tree),
            P(None, tree),
            P(None, tree),
            P(tree, None),
            P(),
            P(),
            P("dp", None, tree),
            P("dp", None, tree),
            P("dp", tree, None),
        ),
        check_vma=False,
    )
```

```python
import functools
import math

import jax
import jax.numpy as jnp
from jax import lax
from jax.experimental import pallas as pl
from jax.experimental.pallas import tpu as pltpu
from jax.sharding import PartitionSpec as P

HD = 64
TOPK = 8
QT = 128
EPS = 1e-05
NEG = -1e30
MIB = 2**20
BF = jnp.bfloat16
F32 = jnp.float32
VMEM = pl.BlockSpec(memory_space=pltpu.VMEM)
SMEM = pl.BlockSpec(memory_space=pltpu.SMEM)
ANY = pl.BlockSpec(memory_space=pl.ANY)


def dot(a, b, ca, cb):
    return lax.dot_general(a, b, (((ca,), (cb,)), ((), ())), preferred_element_type=F32)


def tie(*values):
    return lax.optimization_barrier(values)


def stack_heads(block, count):
    return jnp.concatenate([block[:, h * HD : (h + 1) * HD] for h in range(count)], axis=0)


def causal_mask(per_group):
    key = lax.broadcasted_iota(jnp.int32, (QT, QT), 0)
    query = lax.broadcasted_iota(jnp.int32, (QT, QT), 1)
    return jnp.concatenate([key <= query] * per_group, axis=1)


def tile_masks(seg, parents, per_group):
    key = lax.broadcasted_iota(jnp.int32, (QT, QT), 0)
    query = lax.broadcasted_iota(jnp.int32, (QT, QT), 1)
    own = (key <= query) & (key // seg == query // seg)
    par = None
    for j, parent in enumerate(parents):
        hit = (key // seg == j) & (query // seg == j) & (parent > 0)
        par = hit if par is None else par | hit
    return (
        jnp.concatenate([own] * per_group, axis=1),
        jnp.concatenate([par] * per_group, axis=1),
    )


def softmax_parts(keys, masks, q):
    parts = []
    top = None
    for k, mask in zip(keys, masks):
        s = dot(k, q, 1, 1)
        if mask is not None:
            s = jnp.where(mask, s, NEG)
        parts.append(s)
        m = jnp.max(s, axis=0, keepdims=True)
        top = m if top is None else jnp.maximum(top, m)
    probs = []
    total = None
    for s in parts:
        e = jnp.exp(s - top)
        t = jnp.sum(e, axis=0, keepdims=True)
        total = t if total is None else total + t
        probs.append(e)
    inverse = 1.0 / total
    return [e * inverse for e in probs]


def each_tile(qkv_ref, parent_ref, kv, per_group, seg, work):
    rows = qkv_ref.shape[0]
    trunk = 8 * seg
    segs = QT // seg
    q_width = kv * per_group * HD
    causal = causal_mask(per_group)

    def columns(g):
        return q_width + g * HD, q_width + kv * HD + g * HD

    for i in range(trunk // QT):
        for g in range(kv):
            kc, vc = columns(g)
            spans = ([(0, i * QT)] if i > 0 else []) + [(i * QT, QT)]
            keys = [qkv_ref[a : a + n, kc : kc + HD] for a, n in spans]
            values = [qkv_ref[a : a + n, vc : vc + HD] for a, n in spans]
            masks = ([None] if i > 0 else []) + [causal]
            work(i * QT, g, keys, values, masks, [[s] for s in spans])

    def body(i, carry):
        first = pl.multiple_of(trunk + i * QT, QT)
        parents = [parent_ref[8 + i * segs + j] for j in range(segs)]
        starts = [pl.multiple_of(p * seg, seg) for p in parents]
        own, par = tile_masks(seg, parents, per_group)

        def take(c):
            blocks = [qkv_ref[pl.ds(s, seg), c : c + HD] for s in starts]
            return [
                qkv_ref[0:trunk, c : c + HD],
                qkv_ref[pl.ds(first, QT), c : c + HD],
                jnp.concatenate(blocks, axis=0) if segs > 1 else blocks[0],
            ]

        for g in range(kv):
            kc, vc = columns(g)
            places = [[(0, trunk)], [(first, QT)], [(s, seg) for s in starts]]
            work(first, g, take(kc), take(vc), [None, own, par], places)
        return carry

    lax.fori_loop(0, (rows - trunk) // QT, body, 0)


def attend_forward_kernel(kv, per_group, seg, blocks, shard_ref, parent_ref, *refs):
    ins, row_refs, refs = refs[:blocks], refs[blocks : 2 * blocks], refs[2 * blocks :]
    qkv_ref, out_ref, rows_ref, full_ref, row_sem = refs
    local = out_ref.shape[0] // blocks
    copies = [
        pltpu.make_async_copy(
            row_refs[j].at[pl.ds(0, local)], rows_ref.at[pl.ds(j * local, local)], row_sem.at[j]
        )
        for j in range(blocks)
    ]
    for copy in copies:
        copy.start()
    scale = BF(1.0 / math.sqrt(HD))
    for j in range(blocks):
        at = pl.multiple_of(shard_ref[j] * local, 64)
        qkv_ref[pl.ds(at, local), :] = ins[j][0:local, :]

    def work(first, g, keys, values, masks, places):
        block = qkv_ref[pl.ds(first, QT), g * per_group * HD : (g + 1) * per_group * HD]
        probs = softmax_parts(keys, masks, stack_heads(block, per_group) * scale)
        total = None
        for p, v in zip(probs, values):
            o = dot(v, p.astype(BF), 0, 0)
            total = o if total is None else total + o
        for h in range(per_group):
            c = (g * per_group + h) * HD
            full_ref[pl.ds(first, QT), c : c + HD] = total[:, h * QT : (h + 1) * QT].T.astype(BF)

    each_tile(qkv_ref, parent_ref, kv, per_group, seg, work)
    for j in range(blocks):
        at = pl.multiple_of(shard_ref[j] * local, 64)
        out_ref[j * local : (j + 1) * local, :] = full_ref[pl.ds(at, local), :]
    for copy in copies:
        copy.wait()


def attend_forward(shards, parent_block, qkv_blocks, row_blocks, kv, per_group, seg):
    blocks = len(qkv_blocks)
    wide = qkv_blocks[0].shape[1]
    rows = 20 * seg
    width = kv * per_group * HD
    cells = rows * 12 * seg * kv * per_group
    return pl.pallas_call(
        functools.partial(attend_forward_kernel, kv, per_group, seg, blocks),
        out_shape=[
            jax.ShapeDtypeStruct((rows, wide), BF),
            jax.ShapeDtypeStruct((rows, width), BF),
            jax.ShapeDtypeStruct((rows, row_blocks[0].shape[1]), BF),
        ],
        in_specs=[SMEM, SMEM] + [VMEM] * blocks + [ANY] * blocks,
        out_specs=[VMEM, VMEM, ANY],
        scratch_shapes=[pltpu.VMEM((rows, width), BF), pltpu.SemaphoreType.DMA((blocks,))],
        compiler_params=pltpu.CompilerParams(vmem_limit_bytes=40 * MIB),
        cost_estimate=pl.CostEstimate(
            flops=16 * HD * cells, bytes_accessed=4 * rows * wide, transcendentals=cells
        ),
        name="attend_forward",
    )(shards, parent_block, *qkv_blocks, *row_blocks)


def attend_backward_kernel(kv, per_group, seg, blocks, shard_ref, parent_ref, qkv_ref, *refs):
    ins, (out_ref, do_ref, full_ref, dk_ref, dv_ref) = refs[:blocks], refs[blocks:]
    local = ins[0].shape[0]
    q_width = kv * per_group * HD
    scale = 1.0 / math.sqrt(HD)
    for j in range(blocks):
        at = pl.multiple_of(shard_ref[j] * local, 64)
        do_ref[pl.ds(at, local), :] = ins[j][...]
    dk_ref[...] = jnp.zeros_like(dk_ref)
    dv_ref[...] = jnp.zeros_like(dv_ref)

    def work(first, g, keys, values, masks, places):
        span = slice(g * per_group * HD, (g + 1) * per_group * HD)
        q = stack_heads(qkv_ref[pl.ds(first, QT), span], per_group) * BF(scale)
        d = stack_heads(do_ref[pl.ds(first, QT), span], per_group)
        probs = softmax_parts(keys, masks, q)
        grads = [dot(v, d, 1, 1) for v in values]
        delta = None
        for p, grad in zip(probs, grads):
            t = jnp.sum(grad * p, axis=0, keepdims=True)
            delta = t if delta is None else delta + t
        dq = None
        for p, grad, k, place in zip(probs, grads, keys, places):
            ds = (p * (grad - delta)).astype(BF)
            dk = dot(ds, q, 1, 0)
            dv = dot(p.astype(BF), d, 1, 0)
            o = dot(k, ds, 0, 0)
            dq = o if dq is None else dq + o
            at = 0
            for start, size in place:
                dk_ref[pl.ds(start, size), g * HD : (g + 1) * HD] += dk[at : at + size]
                dv_ref[pl.ds(start, size), g * HD : (g + 1) * HD] += dv[at : at + size]
                at += size
        dq = dq * scale
        for h in range(per_group):
            c = (g * per_group + h) * HD
            full_ref[pl.ds(first, QT), c : c + HD] = dq[:, h * QT : (h + 1) * QT].T.astype(BF)

    each_tile(qkv_ref, parent_ref, kv, per_group, seg, work)
    full_ref[:, q_width : q_width + kv * HD] = dk_ref[...].astype(BF)
    full_ref[:, q_width + kv * HD : q_width + 2 * kv * HD] = dv_ref[...].astype(BF)
    for j in range(blocks):
        at = pl.multiple_of(shard_ref[j] * local, 64)
        out_ref[j * local : (j + 1) * local, :] = full_ref[pl.ds(at, local), :]


def attend_backward(shards, parent_block, qkv, grad_blocks, kv, per_group, seg):
    blocks = len(grad_blocks)
    rows, wide = qkv.shape
    width = kv * per_group * HD
    cells = rows * 12 * seg * kv * per_group
    return pl.pallas_call(
        functools.partial(attend_backward_kernel, kv, per_group, seg, blocks),
        out_shape=jax.ShapeDtypeStruct((rows, wide), BF),
        in_specs=[SMEM, SMEM, VMEM] + [VMEM] * blocks,
        out_specs=VMEM,
        scratch_shapes=[
            pltpu.VMEM((rows, width), BF),
            pltpu.VMEM((rows, wide), BF),
            pltpu.VMEM((rows, kv * HD), F32),
            pltpu.VMEM((rows, kv * HD), F32),
        ],
        compiler_params=pltpu.CompilerParams(vmem_limit_bytes=40 * MIB),
        cost_estimate=pl.CostEstimate(
            flops=40 * HD * cells, bytes_accessed=6 * rows * wide, transcendentals=cells
        ),
        name="attend_backward",
    )(shards, parent_block, qkv, *grad_blocks)


def expert_kernel(first, blocks, fresh, local, at_ref, xa_ref, xb_ref, packet_ref, router_ref, *refs):
    count = len(blocks)
    weight_refs, refs = refs[: sum(blocks)], refs[sum(blocks) :]
    if not fresh:
        refs = refs[5:]
    back_a_ref, back_b_ref, mix_a_ref, mix_b_ref, dot_ref, rows_ref, grad_rows_ref = refs[:7]
    kept_refs = refs[7:10]
    weights, held, g_held, x_held, code_held, weight_sem, held_sem, row_sem, g_sem = refs[10:]
    half = back_a_ref.shape[0]
    rows = 2 * half
    experts = router_ref.shape[1]
    extra = code_held.shape[1]
    x_came, codes_came, arrived = [], [], []
    for i, ref in enumerate((xa_ref, xb_ref)):
        spot = i * (half + extra)
        if not local:
            spot = pl.multiple_of(at_ref[1 + i] * (rows + 2 * extra) + spot, 16)
        span = pl.ds(i * half, half)
        x_came.append(pltpu.make_async_copy(ref, x_held.at[span], g_sem.at[i]))
        codes_came.append(
            pltpu.make_async_copy(
                packet_ref.at[pl.ds(spot + half, extra)], code_held.at[i], g_sem.at[2 + i]
            )
        )
        arrived.append(
            pltpu.make_async_copy(packet_ref.at[pl.ds(spot, half)], g_held.at[span], g_sem.at[4 + i])
        )
    for copy in x_came + codes_came + arrived:
        copy.start()
    loads = []
    for i in (2, 0, 1):
        for n in range(count):
            at = sum(blocks[:n])
            for j in range(blocks[n]):
                source = weight_refs[at + j].at[i]
                unit = source.shape[1]
                copy = pltpu.make_async_copy(
                    source,
                    weights[i].at[n, :, pl.ds(j * unit, unit)],
                    weight_sem.at[i * sum(blocks) + at + j],
                )
                loads.append((n, i, copy))
    for n in range(count):
        for m, _, copy in loads:
            if m == n:
                copy.start()

    def loaded(n, i):
        for m, k, copy in loads:
            if (m, k) == (n, i):
                copy.wait()

    for copy in x_came:
        copy.wait()
    stores = [pltpu.make_async_copy(x_held, rows_ref.at[pl.ds(first, rows)], row_sem.at[0])]
    stores[0].start()
    x = x_held[...]
    for copy in codes_came:
        copy.wait()
    code = jnp.concatenate(
        [code_held[i, 0:experts, 0:half].astype(F32).T for i in range(2)], axis=0
    )
    logits = dot(x, router_ref[...], 1, 0)
    logits = jnp.where(code > 0.5, logits, NEG)
    top = jnp.max(logits, axis=1, keepdims=True)
    e = jnp.exp(logits - top)
    kept = jnp.where(code > 1.5, 1.0, 0.0)
    gates = kept * e / jnp.sum(e, axis=1, keepdims=True)
    lane = lax.broadcasted_iota(jnp.int32, gates.shape, 1)
    for copy in arrived:
        copy.wait()
    copy = pltpu.make_async_copy(g_held, grad_rows_ref.at[pl.ds(first, rows)], row_sem.at[1])
    copy.start()
    stores.append(copy)
    g = g_held[...]
    mix = None
    back = None
    for n in range(count):
        mine = lane == at_ref[0] + n
        weight = jnp.sum(jnp.where(mine, gates, 0.0), axis=1, keepdims=True)
        keep = jnp.sum(jnp.where(mine, kept, 0.0), axis=1, keepdims=True)
        loaded(n, 2)
        grad = dot(g, weights[2][n], 1, 0)
        loaded(n, 0)
        gate_pre = dot(x, weights[0][n], 1, 0)
        loaded(n, 1)
        up_pre = dot(x, weights[1][n], 1, 0)
        sig = 1.0 / (1.0 + jnp.exp(-gate_pre))
        silu = gate_pre * sig
        act = (silu * up_pre).astype(BF).astype(F32)
        pair_dot = jnp.sum(act * grad, axis=1, keepdims=True) * keep
        dot_ref[n : n + 1, :] = pair_dot.T
        weighted = (act * weight).astype(BF)
        grad = grad * weight
        dgate = (grad * up_pre * sig * (1.0 + gate_pre * (1.0 - sig))).astype(BF)
        dup = (grad * silu).astype(BF)
        for i, value in enumerate((weighted, dgate, dup)):
            held[i][n] = value
            copy = pltpu.make_async_copy(
                held[i].at[n], kept_refs[i].at[n, pl.ds(first, rows)], held_sem.at[n * 3 + i]
            )
            copy.start()
            stores.append(copy)
        m = dot(weighted, weights[2][n], 1, 1)
        mix = m if mix is None else mix + m
        b = dot(dgate, weights[0][n], 1, 1) + dot(dup, weights[1][n], 1, 1)
        back = b if back is None else back + b
    mix = mix.astype(BF)
    mix_a_ref[...] = mix[:half]
    mix_b_ref[...] = mix[half:]
    back = back.astype(BF)
    back_a_ref[...] = back[:half]
    back_b_ref[...] = back[half:]
    for copy in stores:
        copy.wait()


def expert_step(k, steps, local, at, x, packets, router, weights, buffers):
    width = x[0].shape[1]
    extra = -(-router.shape[1] // 16) * 16
    half = x[0].shape[0]
    rows = 2 * half
    count = len(weights)
    hidden = sum(w.shape[2] for w in weights[0])
    half_shape = jax.ShapeDtypeStruct((half, width), BF)
    big_shapes = [jax.ShapeDtypeStruct((steps * rows, width), BF)] * 2
    big_shapes += [jax.ShapeDtypeStruct((count, steps * rows, hidden), BF)] * 3
    operands = [at, *x, packets, router, *[b for w in weights for b in w]]
    specs = [SMEM, ANY, ANY, ANY, VMEM] + [ANY] * (len(operands) - 5)
    aliases = {}
    if buffers is not None:
        aliases = {len(operands) + i: 5 + i for i in range(5)}
        operands += buffers
        specs += [ANY] * 5
    blocks = [len(w) for w in weights]
    out = pl.pallas_call(
        functools.partial(expert_kernel, k * rows, blocks, buffers is None, local),
        out_shape=[half_shape] * 4 + [jax.ShapeDtypeStruct((count, rows), F32)] + big_shapes,
        in_specs=specs,
        out_specs=[VMEM] * 5 + [ANY] * 5,
        input_output_aliases=aliases,
        scratch_shapes=[
            [pltpu.VMEM((count, width, hidden), BF)] * 3,
            [pltpu.VMEM((count, rows, hidden), BF)] * 3,
            pltpu.VMEM((rows, width), BF),
            pltpu.VMEM((rows, width), BF),
            pltpu.VMEM((2, extra, width), BF),
            pltpu.SemaphoreType.DMA((3 * sum(blocks),)),
            pltpu.SemaphoreType.DMA((count * 3,)),
            pltpu.SemaphoreType.DMA((2,)),
            pltpu.SemaphoreType.DMA((6,)),
        ],
        compiler_params=pltpu.CompilerParams(vmem_limit_bytes=40 * MIB),
        cost_estimate=pl.CostEstimate(
            flops=2 * rows * width * hidden * count * 6,
            bytes_accessed=6 * width * hidden * count + 10 * rows * width,
            transcendentals=rows * hidden * count,
        ),
        name="expert_step",
    )(*operands)
    return out[:2], out[2:4], out[4], out[5:]


def expert_grad_kernel(act_ref, dgate_ref, dup_ref, x_ref, g_ref, *outs):
    half, _, _, unit = outs[0].shape
    for i, (rows, ref) in enumerate(((x_ref, dgate_ref), (x_ref, dup_ref), (g_ref, act_ref))):
        grad = dot(rows[...], ref[0], 0, 0).astype(BF)
        for j in range(2 * half):
            outs[j // half][j % half, i] = grad[:, j * unit : (j + 1) * unit]


def expert_grads(kept, x, g, parts, expert):
    _, rows, hidden = kept[0].shape
    width = x.shape[1]
    unit = hidden // parts
    tile = 512 if width % 512 == 0 else width
    half = parts // 2
    return list(pl.pallas_call(
        expert_grad_kernel,
        grid=(width // tile,),
        out_shape=[jax.ShapeDtypeStruct((half, 3, width, unit), BF)] * 2,
        in_specs=[pl.BlockSpec((1, rows, hidden), lambda i: (expert, 0, 0))] * 3
        + [pl.BlockSpec((rows, tile), lambda i: (0, i))] * 2,
        out_specs=[pl.BlockSpec((half, 3, tile, unit), lambda i: (0, 0, i, 0))] * 2,
        compiler_params=pltpu.CompilerParams(vmem_limit_bytes=56 * MIB),
        cost_estimate=pl.CostEstimate(
            flops=6 * rows * width * hidden,
            bytes_accessed=12 * width * hidden,
            transcendentals=0,
        ),
        name="expert_grads",
    )(*kept, x, g))


def finish_kernel(terms, *refs):
    ins, outs = refs[: len(refs) - 3], refs[len(refs) - 3 :]
    for n in range(len(ins) // terms):
        refs = ins[n * terms : (n + 1) * terms]
        for i in range(3):
            total = refs[-1][i].astype(F32)
            for ref in refs[:-1]:
                total = total + ref[0, i].astype(F32)
            outs[i][n] = total.T if i == 2 else total


def finish_grads(sums):
    count = len(sums)
    _, width, unit = sums[0][1].shape
    terms = len(sums[0][0]) + 1
    first = pl.BlockSpec((1, 3, width, unit), lambda i: (0, 0, 0, 0))
    specs = [first] * (terms - 1) + [pl.BlockSpec((3, width, unit), lambda i: (0, 0, 0))]
    shapes = [(count, width, unit), (count, width, unit), (count, unit, width)]
    return list(
        pl.pallas_call(
            functools.partial(finish_kernel, terms),
            grid=(1,),
            out_shape=[jax.ShapeDtypeStruct(v, F32) for v in shapes],
            in_specs=specs * count,
            out_specs=[pl.BlockSpec(v, lambda i: (0, 0, 0)) for v in shapes],
            compiler_params=pltpu.CompilerParams(vmem_limit_bytes=48 * MIB),
            name="finish_grads",
        )(*[v for near, across in sums for v in (*near, across)])
    )


def tree_moves():
    rows, cols = lax.axis_size("row"), lax.axis_size("col")
    if rows == 2 and cols == 2:
        swap = [(0, 1), (1, 0)]
        me = lax.axis_index("row") * 2 + lax.axis_index("col")

        def gather(x, again=None, finish=True):
            across = lax.ppermute(x if again is None else again, "row", swap)
            beside = lax.ppermute(x, "col", swap)
            blocks = [x, across, beside]
            return finish_gather(blocks) if finish else blocks

        def finish_gather(blocks):
            return blocks + [lax.ppermute(blocks[1], "col", swap)]

        def reduce_first(mine, other):
            return [mine, lax.ppermute(other, "col", swap)]

        def reduce_second(mine, came):
            far = (mine[1].astype(F32) + came[1].astype(F32)).astype(BF)
            return [mine, came], lax.ppermute(far, "row", swap)

        reduce = (reduce_first, reduce_second)

        return [me, me ^ 2, me ^ 1, me ^ 3], gather, finish_gather, reduce

    count = rows * cols
    both = ("row", "col")

    def gather(x, again=None, finish=True):
        whole = lax.all_gather(x if again is None else again, both, axis=0)
        return [whole[i] for i in range(count)]

    def reduce_second(mine, other):
        blocks = jnp.concatenate([mine, other], axis=0)
        total = lax.psum_scatter(blocks, both, scatter_dimension=0)
        return [total[None]], jnp.zeros_like(total)

    reduce = (lambda mine, other: [mine, other], reduce_second)

    return [jnp.int32(i) for i in range(count)], gather, list, reduce


def half_orders(count):
    ys = count // 4
    near = [y for y in range(ys)] + [ys + y for y in reversed(range(ys))]
    return [near, [partner_of(i, count) for i in near]]


def partner_of(index, count):
    ys = count // 4
    return (3 - index // ys) * ys + index % ys


def ring_order(count):
    ys = count // 4
    order = []
    for y in range(ys):
        zs = range(4) if y % 2 == 0 else reversed(range(4))
        order += [z * ys + y for z in zs]
    return order


def ring_move(x, order, by):
    n = len(order)
    return lax.ppermute(x, "dp", [(order[i], order[(i + by) % n]) for i in range(n)])


def add_halves(came, own, last):
    total = [c.astype(F32) + n.astype(F32) for c, n in zip(came, own)]
    if last:
        return [jnp.concatenate(total, axis=0)]
    return list(tie(*[t.astype(BF) for t in total]))


def walk_hops(parts, order):
    n = len(order)
    a, b = parts[1]
    for k in range(1, n):
        came = yield [ring_move(a, order, 1), ring_move(b, order, -1)]
        total = add_halves(came, parts[(k + 1) % n], k == n - 1)
        if k < n - 1:
            a, b = total
    yield total


class Ring:
    def __init__(self, count, dp_index):
        self.orders = half_orders(count)
        self.steps = len(self.orders[0])
        at = [[o.index(i) for o in self.orders if i in o][0] for i in range(count)]
        self.place = jnp.array(at, jnp.int32)[dp_index]
        self.four = self.steps == 4
        if self.four:
            self.places = [lax.rem(self.place + k, 4) for k in (0, 3, 1, 2)]
        else:
            self.places = [jnp.int32(k) for k in range(self.steps)]

    def shift(self, x, by):
        n = self.steps
        return lax.ppermute(
            x, "dp", [(o[i], o[(i + by) % n]) for o in self.orders for i in range(n)]
        )

    def gather(self, x):
        if not self.four:
            whole = lax.all_gather(x, "dp", axis=0, axis_index_groups=self.orders)
            return [[whole[k]] for k in range(self.steps)]
        return self.gather_second(x, self.gather_first(x))

    def gather_first(self, x):
        return [self.shift(x, 1), self.shift(x, -1)] if self.four else [x]

    def gather_second(self, x, came):
        if not self.four:
            return self.gather(x)
        half = x.shape[0] // 2
        left, right = came
        a, b = right[:half], left[half:]
        return [[x], [left], [right], [self.shift(a, -1), self.shift(b, 1)]]

    def reduce_stages(self, parts):
        if not self.four:
            yield []
            whole = jnp.stack([jnp.concatenate(p, axis=0) for p in parts])
            yield lax.psum_scatter(
                whole, "dp", scatter_dimension=0, axis_index_groups=self.orders
            ).astype(F32)
            return
        (own,), (left,), (right,), (far_a, far_b) = parts
        half = far_a.shape[0]
        a, b = yield [self.shift(far_a, 1), self.shift(far_b, -1)]
        right = jnp.concatenate(
            [(right[:half].astype(F32) + a.astype(F32)).astype(BF), right[half:]], axis=0
        )
        left = jnp.concatenate(
            [left[:half], (left[half:].astype(F32) + b.astype(F32)).astype(BF)], axis=0
        )
        yield own.astype(F32) + (
            self.shift(right, 1).astype(F32) + self.shift(left, -1).astype(F32)
        )

    def reduce(self, parts):
        stages = self.reduce_stages(parts)
        return stages.send(next(stages))


def small_sum(value, part):
    sizes = [lax.axis_size(name) for name in ("dp", "row", "col")]
    if sizes != [8, 2, 2]:
        return lax.psum(value, ("col", "row", "dp")[part]) if part < 3 else value
    hops = [[("col", 2, 1), ("dp", 8, 1)], [("row", 2, 1)], [("dp", 8, 2)], [("dp", 8, 4)]]
    for name, size, bit in hops[part]:
        value = value + lax.ppermute(value, name, [(i, i ^ bit) for i in range(size)])
    return value


def write_kernel(spans, sizes, turned, place_ref, *refs):
    pieces, outs = refs[: sum(sizes)], refs[sum(sizes) :]
    at = 0
    for k, size in enumerate(sizes):
        chunk = jnp.concatenate([ref[...] for ref in pieces[at : at + size]], axis=0).astype(F32)
        rows = chunk.shape[0]
        at += size
        for n, ((a, b), out) in enumerate(zip(spans, outs)):
            if n == turned:
                start = pl.multiple_of(place_ref[k] * rows, 128)
                out[:, pl.ds(start, rows)] = chunk[:, a:b].T
            else:
                start = pl.multiple_of(place_ref[k] * rows, 16)
                out[pl.ds(start, rows), :] = chunk[:, a:b]


def sum_over_dp(parts, spans, ring, pairs):
    rows = parts[0].shape[0]
    chunk = rows // ring.steps

    def cut(place, at, size):
        return jnp.concatenate(
            [lax.dynamic_slice(v, (place * chunk + at, 0), (size, v.shape[1])) for v in parts],
            axis=1,
        )

    terms = [[cut(place, 0, chunk)] for place in ring.places]
    if ring.four:
        half = chunk // 2
        terms[3] = [cut(ring.places[3], 0, half), cut(ring.places[3], half, half)]
    stages = ring.reduce_stages(terms)
    total = stages.send((yield next(stages)))
    total = (yield [total])[0].astype(BF)
    came = (yield [lax.ppermute(total, "dp", pairs)])[0]
    total = (total.astype(F32) + came.astype(F32)).astype(BF)
    pieces = ring.gather_second(total, (yield ring.gather_first(total)))
    pieces[-1] = yield pieces[-1]
    sizes = [len(p) for p in pieces]
    turned = len(spans) - 1 if chunk % 128 == 0 else None
    shapes = [
        jax.ShapeDtypeStruct((b - a, rows) if n == turned else (rows, b - a), F32)
        for n, (a, b) in enumerate(spans)
    ]
    sums = list(
        pl.pallas_call(
            functools.partial(write_kernel, spans, sizes, turned),
            out_shape=shapes,
            in_specs=[SMEM] + [VMEM] * sum(sizes),
            out_specs=[VMEM] * len(spans),
            compiler_params=pltpu.CompilerParams(vmem_limit_bytes=32 * MIB),
            name="write_grads",
        )(jnp.stack(ring.places).astype(jnp.int32), *[p for pair in pieces for p in pair])
    )
    if turned is None:
        sums[-1] = sums[-1].T
    yield sums


def rms_scale(values):
    return lax.rsqrt(jnp.mean(values * values, axis=-1, keepdims=True) + EPS)


def norm_back(grad_normed, values, scale_rows, gain):
    weighted = grad_normed * gain
    grad_gain = jnp.sum(grad_normed * values * scale_rows, axis=0)
    inner = jnp.mean(weighted * values, axis=-1, keepdims=True)
    return (
        scale_rows * weighted - values * scale_rows * scale_rows * scale_rows * inner,
        grad_gain,
    )


def shards_program(
    tokens, attn_gain, query_weight, key_weight, value_weight, out_weight, mlp_gain, router_weight,
    gate_weight, up_weight, down_weight, output_grad, expert_ids, slot_rank, segment_ids, parent_ids,
):
    local_rows, width = tokens.shape
    half = local_rows // 2
    dp_size = lax.axis_size("dp")
    dp_index = lax.axis_index("dp")
    pairs = [(i, partner_of(i, dp_size)) for i in range(dp_size)]
    ring = Ring(dp_size, dp_index)
    shards, tree_gather, tree_finish, (reduce_first, reduce_second) = tree_moves()

    def tree_reduce(mine, other):
        return reduce_second(*reduce_first(mine, other))

    count = len(shards)
    shard_ids = jnp.stack(shards).astype(jnp.int32)
    kv = key_weight.shape[1] // HD
    per_group = query_weight.shape[1] // key_weight.shape[1]
    q_width = query_weight.shape[1]
    k_width = key_weight.shape[1]
    experts_local = gate_weight.shape[0]
    unit = gate_weight.shape[2]
    experts = experts_local * dp_size
    capacity = 5 * local_rows * TOPK // (4 * experts)
    seg = local_rows * count // 20

    token_values = tokens.astype(F32)
    scale_attn = rms_scale(token_values)
    normed = (token_values * scale_attn * attn_gain).astype(BF)
    step = math.gcd(seg, local_rows)
    each = local_rows // step
    labels = jnp.stack([segment_ids[::step], parent_ids[::step]]).astype(BF)
    normed_packet = jnp.concatenate(
        [normed, jnp.pad(labels, ((0, 14), (0, width - each)))], axis=0
    )
    tree_normed = tree_gather(normed_packet)
    labels = jnp.concatenate([v[local_rows : local_rows + 2, :each] for v in tree_normed], axis=1)
    spots = jnp.concatenate([s * each + jnp.arange(each, dtype=jnp.int32) for s in shards])
    spots = spots.astype(jnp.int32)
    block_spot = spots * step // seg
    is_parent = (labels[0][None, :] == labels[1][:, None]) & (labels[1][:, None] > 0)
    parent_spot = jnp.max(jnp.where(is_parent, block_spot[None, :], 0), axis=1)
    natural = jnp.arange(20, dtype=jnp.int32) * (seg // step)
    parent_block = jnp.sum(
        jnp.where(spots[None, :] == natural[:, None], parent_spot[None, :], 0), axis=1
    ).astype(jnp.int32)

    columns = jnp.arange(experts, dtype=jnp.int32)
    unranked = local_rows * TOPK
    rank = jnp.min(
        jnp.where(
            expert_ids.T[:, None, :] == columns[None, :, None], slot_rank.T[:, None, :], unranked
        ),
        axis=0,
    )
    slot = jnp.sum((rank[:, :, None] < rank[:, None, :]).astype(jnp.int32), axis=1)
    code = jnp.where(rank == unranked, 0.0, jnp.where(slot < capacity, 2.0, 1.0))
    extra = -(-experts // 16) * 16
    packet = []
    for at in (0, half):
        lanes = ((0, extra - experts), (0, width - half))
        packet += [output_grad[at : at + half], jnp.pad(code[:, at : at + half].astype(BF), lanes)]
    packet = jnp.concatenate(packet, axis=0)
    packets = lax.all_gather(packet, "dp", axis=0, tiled=True)
    tree_normed[1], packet = tie(tree_normed[1], packet)

    raw = [
        jnp.stack([gate_weight[n], up_weight[n], down_weight[n].T]) for n in range(experts_local)
    ]

    def joined(blocks):
        return blocks if unit % 128 == 0 else [jnp.concatenate(blocks, axis=2)]

    weights = [tree_gather(raw[0])]
    qkv_weight = jnp.concatenate([query_weight, key_weight, value_weight], axis=1)
    qkv_blocks = [
        jnp.dot(block, qkv_weight, preferred_element_type=F32).astype(BF) for block in tree_normed
    ]
    qkv, heads, normed_rows = attend_forward(
        shard_ids, parent_block, qkv_blocks, tree_normed, kv, per_group, seg
    )
    heads, weights[0][1] = tie(heads, weights[0][1])
    def by_shard(rows, weight):
        result = jnp.dot(rows, weight, preferred_element_type=F32).astype(BF)
        return result.reshape(-1, local_rows, width)

    middle = (count + 1) // 2 * local_rows
    attn_near, attn_far = tree_reduce(
        *tie(by_shard(heads[:middle], out_weight), by_shard(heads[middle:], out_weight))
    )
    attn_far, *later = tie(attn_far, *raw[1:], *weights[0][2:])
    weights[0][2:] = later[len(raw) - 1 :]
    weights += [tree_gather(v, again, False) for v, again in zip(raw[1:], later)]
    hidden = token_values + attn_far.astype(F32) + sum(v[0].astype(F32) for v in attn_near)
    scale_mlp = rms_scale(hidden)
    mlp_in = (hidden * scale_mlp * mlp_gain).astype(BF)

    order = ring_order(dp_size)
    all_places = jnp.array([order.index(i) for i in range(dp_size)], jnp.int32)
    place = all_places[dp_index]
    walk = jnp.array(order, jnp.int32)
    steps = jnp.arange(dp_size, dtype=jnp.int32)
    at = jnp.stack(
        [
            jnp.full_like(steps, dp_index * experts_local),
            walk[(place - steps) % dp_size],
            walk[(place + steps) % dp_size],
        ],
        axis=1,
    ).astype(jnp.int32)
    x = [mlp_in[:half], mlp_in[half:]]
    kept = None
    backs, mixes, dots, came = [], [], [], []
    coming = [ring_move(x[0], order, 1), ring_move(x[1], order, -1)]
    weights[1:] = [tree_finish(blocks) for blocks in weights[1:]]
    weights = [joined(blocks) for blocks in weights]
    for k in range(dp_size):
        if k > 0:
            x = coming
            if k > 1:
                x = [ring_move(x[0], order, 1), ring_move(x[1], order, -1)]
            *x, dots[k - 1] = tie(*x, dots[k - 1])
            if k > 2:
                *x, came[k - 2][0], came[k - 2][1] = tie(*x, *came[k - 2])
            coming = x
        back, mix, pair_dot, kept = expert_step(
            k,
            dp_size,
            k == 0,
            at[k],
            x,
            packets if k > 0 else packet,
            router_weight,
            weights,
            kept,
        )
        backs.append(back)
        mixes.append(list(mix))
        dots.append(pair_dot)
        came.append(None)
        if k > 0:
            if k > 1:
                *came[k - 1], dots[k] = tie(*came[k - 1], dots[k])
                back = add_halves(came[k - 1], back, False)
            if k == dp_size - 1:
                *back, mixes[1][0], mixes[1][1] = tie(*back, *mixes[1])
            came[k] = [ring_move(back[0], order, 1), ring_move(back[1], order, -1)]
    all_rows, all_grads, *factors = kept
    mlp_in, code, dots[-1] = tie(mlp_in, code, dots[-1])
    (grad_rows,) = add_halves(came[-1], backs[0], True)
    hops = walk_hops(mixes, order)
    hop = next(hops)
    left = dp_size - 1

    def next_hop(*values):
        nonlocal hop, left
        if left == 0:
            return values
        *values, a, b = tie(*values, *hop)
        hop = hops.send([a, b])
        left -= 1
        return values


    all_dots = jnp.stack(dots)

    def pick(index):
        return jnp.sum(
            jnp.where((index[:, None] == steps[None, :])[:, :, None, None], all_dots[None], 0.0),
            axis=1,
        )

    send = jnp.where(
        jnp.arange(local_rows) < half,
        pick((place - all_places) % dp_size),
        pick((all_places - place) % dp_size),
    )
    grad_gates = lax.all_to_all(send, "dp", 0, 0, tiled=True).reshape(experts, local_rows).T

    code_here = code.T
    logits = jnp.dot(mlp_in, router_weight, preferred_element_type=F32)
    logits = jnp.where(code_here > 0.5, logits, NEG)
    chosen_exp = jnp.exp(logits - jnp.max(logits, axis=1, keepdims=True))
    gates = chosen_exp / jnp.sum(chosen_exp, axis=1, keepdims=True)
    weighted_sum = jnp.sum(gates * grad_gates, axis=1, keepdims=True)
    grad_logits = (gates * (grad_gates - weighted_sum)).astype(BF)
    router_part = jnp.dot(mlp_in.T, grad_logits, preferred_element_type=F32)
    grad_mlp_in = grad_rows + jnp.dot(grad_logits, router_weight.T, preferred_element_type=F32)
    grad_hidden_norm, mlp_gain_part = norm_back(grad_mlp_in, hidden, scale_mlp, mlp_gain)
    grad_hidden = output_grad.astype(F32) + grad_hidden_norm
    grad_attn = grad_hidden.astype(BF)

    grad_attn, *factors = next_hop(*tie(grad_attn, *factors))
    grad_blocks = tree_gather(grad_attn)
    expert_parts = [expert_grads(factors, all_rows, all_grads, count, 0)]
    grad_blocks[1], expert_parts[0][1] = next_hop(*tie(grad_blocks[1], expert_parts[0][1]))
    expert_sums = [tree_reduce(*expert_parts[0])]
    grad_head_blocks = [
        jnp.dot(block, out_weight.T, preferred_element_type=F32).astype(BF) for block in grad_blocks
    ]
    (grad_head_blocks[-1],) = next_hop(grad_head_blocks[-1])
    dqkv = attend_backward(
        shard_ids, parent_block, qkv, grad_head_blocks, kv, per_group, seg
    )
    near, across = expert_sums[0]
    dqkv, across, *factors = next_hop(*tie(dqkv, across, *factors))
    expert_sums[0] = (near, across)
    qkv_part = jnp.dot(normed_rows.T, dqkv, preferred_element_type=F32).astype(BF)
    out_rows = jnp.concatenate(grad_blocks, axis=0)
    out_part = jnp.dot(out_rows.T, heads, preferred_element_type=F32).astype(BF)
    spans = (
        (0, q_width),
        (q_width, q_width + k_width),
        (q_width + k_width, q_width + 2 * k_width),
        (q_width + 2 * k_width, 2 * q_width + 2 * k_width),
    )
    stages = sum_over_dp([qkv_part, out_part], spans, ring, pairs)
    came = next(stages)
    spread = qkv_weight.T
    normed_near, normed_far = tree_reduce(
        by_shard(dqkv[:middle], spread), by_shard(dqkv[middle:], spread)
    )

    *came, factors[0] = next_hop(*tie(*came, factors[0]))
    came = stages.send(came)
    expert_parts += [
        expert_grads(factors, all_rows, all_grads, count, n) for n in range(1, experts_local)
    ]
    *came, normed_far, expert_parts[-1][1] = next_hop(
        *tie(*came, normed_far, expert_parts[-1][1])
    )
    came = stages.send(came)
    grad_normed = normed_far.astype(F32) + sum(v[0].astype(F32) for v in normed_near)
    grad_token_norm, attn_gain_part = norm_back(grad_normed, token_values, scale_attn, attn_gain)
    input_grad = grad_hidden + grad_token_norm
    small = jnp.concatenate(
        [router_part.T, mlp_gain_part.reshape(1, -1), attn_gain_part.reshape(1, -1)], axis=0
    )
    small = small_sum(small, 0)
    expert_sums += [tree_reduce(*p) for p in expert_parts[1:]]
    near, across = expert_sums[-1]
    across, small, *came = next_hop(*tie(across, small, *came))
    expert_sums[-1] = (near, across)
    while left > 0:
        next_hop()
    output = (hidden + hop[0]).astype(BF)
    came = stages.send(came)
    small = small_sum(small, 1)
    near, across = expert_sums[-1]
    across, *came = tie(across, *came)
    expert_sums[-1] = (near, across)
    came = stages.send(came)
    expert_grad = finish_grads(expert_sums)
    small = small_sum(small, 2)
    small, expert_grad[0], *came = tie(small, expert_grad[0], *came)
    query_grad, key_grad, value_grad, out_grad = stages.send(came)
    small = small_sum(small, 3)
    return (
        output,
        input_grad,
        small[experts + 1],
        query_grad,
        key_grad,
        value_grad,
        out_grad,
        small[experts],
        small[:experts].T,
        expert_grad[0],
        expert_grad[1],
        expert_grad[2],
    )


def solution(mesh):
    every = ("dp", "row", "col")
    tree = ("row", "col")
    return jax.shard_map(
        shards_program,
        mesh=mesh,
        in_specs=(
            P(every, None),
            P(),
            P(None, tree),
            P(None, tree),
            P(None, tree),
            P(tree, None),
            P(),
            P(),
            P("dp", None, tree),
            P("dp", None, tree),
            P("dp", tree, None),
            P(every, None),
            P(every, None),
            P(every, None),
            P(every),
            P(every),
        ),
        out_specs=(
            P(every, None),
            P(every, None),
            P(),
            P(None, tree),
            P(None, tree),
            P(None, tree),
            P(tree, None),
            P(),
            P(),
            P("dp", None, tree),
            P("dp", None, tree),
            P("dp", tree, None),
        ),
        check_vma=False,
    )
```

```python
import functools
import math

import jax
import jax.numpy as jnp
from jax import lax
from jax.experimental import pallas as pl
from jax.experimental.pallas import tpu as pltpu
from jax.sharding import PartitionSpec as P

HD = 64
TOPK = 8
QT = 128
EPS = 1e-05
NEG = -1e30
MIB = 2**20
BF = jnp.bfloat16
F32 = jnp.float32
VMEM = pl.BlockSpec(memory_space=pltpu.VMEM)
SMEM = pl.BlockSpec(memory_space=pltpu.SMEM)
ANY = pl.BlockSpec(memory_space=pl.ANY)


def dot(a, b, ca, cb):
    return lax.dot_general(a, b, (((ca,), (cb,)), ((), ())), preferred_element_type=F32)


def tie(*values):
    return lax.optimization_barrier(values)


def stack_heads(block, count):
    return jnp.concatenate([block[:, h * HD : (h + 1) * HD] for h in range(count)], axis=0)


def causal_mask(per_group):
    key = lax.broadcasted_iota(jnp.int32, (QT, QT), 0)
    query = lax.broadcasted_iota(jnp.int32, (QT, QT), 1)
    return jnp.concatenate([key <= query] * per_group, axis=1)


def tile_masks(seg, parents, per_group):
    key = lax.broadcasted_iota(jnp.int32, (QT, QT), 0)
    query = lax.broadcasted_iota(jnp.int32, (QT, QT), 1)
    own = (key <= query) & (key // seg == query // seg)
    par = None
    for j, parent in enumerate(parents):
        hit = (key // seg == j) & (query // seg == j) & (parent > 0)
        par = hit if par is None else par | hit
    return (
        jnp.concatenate([own] * per_group, axis=1),
        jnp.concatenate([par] * per_group, axis=1),
    )


def softmax_parts(keys, masks, q):
    parts = []
    top = None
    for k, mask in zip(keys, masks):
        s = dot(k, q, 1, 1)
        if mask is not None:
            s = jnp.where(mask, s, NEG)
        parts.append(s)
        m = jnp.max(s, axis=0, keepdims=True)
        top = m if top is None else jnp.maximum(top, m)
    probs = []
    total = None
    for s in parts:
        e = jnp.exp(s - top)
        t = jnp.sum(e, axis=0, keepdims=True)
        total = t if total is None else total + t
        probs.append(e)
    inverse = 1.0 / total
    return [e * inverse for e in probs]


def each_tile(qkv_ref, parent_ref, kv, per_group, seg, work):
    rows = qkv_ref.shape[0]
    trunk = 8 * seg
    segs = QT // seg
    q_width = kv * per_group * HD
    causal = causal_mask(per_group)

    def columns(g):
        return q_width + g * HD, q_width + kv * HD + g * HD

    for i in range(trunk // QT):
        for g in range(kv):
            kc, vc = columns(g)
            spans = ([(0, i * QT)] if i > 0 else []) + [(i * QT, QT)]
            keys = [qkv_ref[a : a + n, kc : kc + HD] for a, n in spans]
            values = [qkv_ref[a : a + n, vc : vc + HD] for a, n in spans]
            masks = ([None] if i > 0 else []) + [causal]
            work(i * QT, g, keys, values, masks, [[s] for s in spans])

    def body(i, carry):
        first = pl.multiple_of(trunk + i * QT, QT)
        parents = [parent_ref[8 + i * segs + j] for j in range(segs)]
        starts = [pl.multiple_of(p * seg, seg) for p in parents]
        own, par = tile_masks(seg, parents, per_group)

        def take(c):
            blocks = [qkv_ref[pl.ds(s, seg), c : c + HD] for s in starts]
            return [
                qkv_ref[0:trunk, c : c + HD],
                qkv_ref[pl.ds(first, QT), c : c + HD],
                jnp.concatenate(blocks, axis=0) if segs > 1 else blocks[0],
            ]

        for g in range(kv):
            kc, vc = columns(g)
            places = [[(0, trunk)], [(first, QT)], [(s, seg) for s in starts]]
            work(first, g, take(kc), take(vc), [None, own, par], places)
        return carry

    lax.fori_loop(0, (rows - trunk) // QT, body, 0, unroll=6)


def attend_forward_kernel(kv, per_group, seg, blocks, shard_ref, parent_ref, *refs):
    ins, row_refs, refs = refs[:blocks], refs[blocks : 2 * blocks], refs[2 * blocks :]
    qkv_ref, out_ref, rows_ref, full_ref, row_sem = refs
    local = out_ref.shape[0] // blocks
    copies = [
        pltpu.make_async_copy(
            row_refs[j].at[pl.ds(0, local)], rows_ref.at[pl.ds(j * local, local)], row_sem.at[j]
        )
        for j in range(blocks)
    ]
    for copy in copies:
        copy.start()
    scale = BF(1.0 / math.sqrt(HD))
    for j in range(blocks):
        at = pl.multiple_of(shard_ref[j] * local, 64)
        qkv_ref[pl.ds(at, local), :] = ins[j][0:local, :]

    def work(first, g, keys, values, masks, places):
        block = qkv_ref[pl.ds(first, QT), g * per_group * HD : (g + 1) * per_group * HD]
        probs = softmax_parts(keys, masks, stack_heads(block, per_group) * scale)
        total = None
        for p, v in zip(probs, values):
            o = dot(v, p.astype(BF), 0, 0)
            total = o if total is None else total + o
        for h in range(per_group):
            c = (g * per_group + h) * HD
            full_ref[pl.ds(first, QT), c : c + HD] = total[:, h * QT : (h + 1) * QT].T.astype(BF)

    each_tile(qkv_ref, parent_ref, kv, per_group, seg, work)
    for j in range(blocks):
        at = pl.multiple_of(shard_ref[j] * local, 64)
        out_ref[j * local : (j + 1) * local, :] = full_ref[pl.ds(at, local), :]
    for copy in copies:
        copy.wait()


def attend_forward(shards, parent_block, qkv_blocks, row_blocks, kv, per_group, seg):
    blocks = len(qkv_blocks)
    wide = qkv_blocks[0].shape[1]
    rows = 20 * seg
    width = kv * per_group * HD
    cells = rows * 12 * seg * kv * per_group
    return pl.pallas_call(
        functools.partial(attend_forward_kernel, kv, per_group, seg, blocks),
        out_shape=[
            jax.ShapeDtypeStruct((rows, wide), BF),
            jax.ShapeDtypeStruct((rows, width), BF),
            jax.ShapeDtypeStruct((rows, row_blocks[0].shape[1]), BF),
        ],
        in_specs=[SMEM, SMEM] + [VMEM] * blocks + [ANY] * blocks,
        out_specs=[VMEM, VMEM, ANY],
        scratch_shapes=[pltpu.VMEM((rows, width), BF), pltpu.SemaphoreType.DMA((blocks,))],
        compiler_params=pltpu.CompilerParams(vmem_limit_bytes=40 * MIB),
        cost_estimate=pl.CostEstimate(
            flops=16 * HD * cells, bytes_accessed=4 * rows * wide, transcendentals=cells
        ),
        name="attend_forward",
    )(shards, parent_block, *qkv_blocks, *row_blocks)


def attend_backward_kernel(kv, per_group, seg, blocks, shard_ref, parent_ref, qkv_ref, *refs):
    ins, (out_ref, do_ref, full_ref, dk_ref, dv_ref) = refs[:blocks], refs[blocks:]
    local = ins[0].shape[0]
    q_width = kv * per_group * HD
    scale = 1.0 / math.sqrt(HD)
    for j in range(blocks):
        at = pl.multiple_of(shard_ref[j] * local, 64)
        do_ref[pl.ds(at, local), :] = ins[j][...]
    dk_ref[...] = jnp.zeros_like(dk_ref)
    dv_ref[...] = jnp.zeros_like(dv_ref)

    def work(first, g, keys, values, masks, places):
        span = slice(g * per_group * HD, (g + 1) * per_group * HD)
        q = stack_heads(qkv_ref[pl.ds(first, QT), span], per_group) * BF(scale)
        d = stack_heads(do_ref[pl.ds(first, QT), span], per_group)
        probs = softmax_parts(keys, masks, q)
        grads = [dot(v, d, 1, 1) for v in values]
        delta = None
        for p, grad in zip(probs, grads):
            t = jnp.sum(grad * p, axis=0, keepdims=True)
            delta = t if delta is None else delta + t
        dq = None
        for p, grad, k, place in zip(probs, grads, keys, places):
            ds = (p * (grad - delta)).astype(BF)
            dk = dot(ds, q, 1, 0)
            dv = dot(p.astype(BF), d, 1, 0)
            o = dot(k, ds, 0, 0)
            dq = o if dq is None else dq + o
            at = 0
            for start, size in place:
                dk_ref[pl.ds(start, size), g * HD : (g + 1) * HD] += dk[at : at + size]
                dv_ref[pl.ds(start, size), g * HD : (g + 1) * HD] += dv[at : at + size]
                at += size
        dq = dq * scale
        for h in range(per_group):
            c = (g * per_group + h) * HD
            full_ref[pl.ds(first, QT), c : c + HD] = dq[:, h * QT : (h + 1) * QT].T.astype(BF)

    each_tile(qkv_ref, parent_ref, kv, per_group, seg, work)
    full_ref[:, q_width : q_width + kv * HD] = dk_ref[...].astype(BF)
    full_ref[:, q_width + kv * HD : q_width + 2 * kv * HD] = dv_ref[...].astype(BF)
    for j in range(blocks):
        at = pl.multiple_of(shard_ref[j] * local, 64)
        out_ref[j * local : (j + 1) * local, :] = full_ref[pl.ds(at, local), :]


def attend_backward(shards, parent_block, qkv, grad_blocks, kv, per_group, seg):
    blocks = len(grad_blocks)
    rows, wide = qkv.shape
    width = kv * per_group * HD
    cells = rows * 12 * seg * kv * per_group
    return pl.pallas_call(
        functools.partial(attend_backward_kernel, kv, per_group, seg, blocks),
        out_shape=jax.ShapeDtypeStruct((rows, wide), BF),
        in_specs=[SMEM, SMEM, VMEM] + [VMEM] * blocks,
        out_specs=VMEM,
        scratch_shapes=[
            pltpu.VMEM((rows, width), BF),
            pltpu.VMEM((rows, wide), BF),
            pltpu.VMEM((rows, kv * HD), F32),
            pltpu.VMEM((rows, kv * HD), F32),
        ],
        compiler_params=pltpu.CompilerParams(vmem_limit_bytes=40 * MIB),
        cost_estimate=pl.CostEstimate(
            flops=40 * HD * cells, bytes_accessed=6 * rows * wide, transcendentals=cells
        ),
        name="attend_backward",
    )(shards, parent_block, qkv, *grad_blocks)


def expert_kernel(first, blocks, fresh, local, at_ref, xa_ref, xb_ref, packet_ref, router_ref, *refs):
    count = len(blocks)
    weight_refs, refs = refs[: sum(blocks)], refs[sum(blocks) :]
    if not fresh:
        refs = refs[5:]
    back_a_ref, back_b_ref, mix_a_ref, mix_b_ref, dot_ref, rows_ref, grad_rows_ref = refs[:7]
    kept_refs = refs[7:10]
    weights, held, g_held, x_held, code_held, weight_sem, held_sem, row_sem, g_sem = refs[10:]
    half = back_a_ref.shape[0]
    rows = 2 * half
    experts = router_ref.shape[1]
    extra = code_held.shape[1]
    x_came, codes_came, arrived = [], [], []
    for i, ref in enumerate((xa_ref, xb_ref)):
        spot = i * (half + extra)
        if not local:
            spot = pl.multiple_of(at_ref[1 + i] * (rows + 2 * extra) + spot, 16)
        span = pl.ds(i * half, half)
        x_came.append(pltpu.make_async_copy(ref, x_held.at[span], g_sem.at[i]))
        codes_came.append(
            pltpu.make_async_copy(
                packet_ref.at[pl.ds(spot + half, extra)], code_held.at[i], g_sem.at[2 + i]
            )
        )
        arrived.append(
            pltpu.make_async_copy(packet_ref.at[pl.ds(spot, half)], g_held.at[span], g_sem.at[4 + i])
        )
    for copy in x_came + codes_came + arrived:
        copy.start()
    loads = []
    for i in (2, 0, 1):
        for n in range(count):
            at = sum(blocks[:n])
            for j in range(blocks[n]):
                source = weight_refs[at + j].at[i]
                unit = source.shape[1]
                copy = pltpu.make_async_copy(
                    source,
                    weights[i].at[n, :, pl.ds(j * unit, unit)],
                    weight_sem.at[i * sum(blocks) + at + j],
                )
                loads.append((n, i, copy))
    for n in range(count):
        for m, _, copy in loads:
            if m == n:
                copy.start()

    def loaded(n, i):
        for m, k, copy in loads:
            if (m, k) == (n, i):
                copy.wait()

    for copy in x_came:
        copy.wait()
    stores = [pltpu.make_async_copy(x_held, rows_ref.at[pl.ds(first, rows)], row_sem.at[0])]
    stores[0].start()
    x = x_held[...]
    for copy in codes_came:
        copy.wait()
    code = jnp.concatenate(
        [code_held[i, 0:experts, 0:half].astype(F32).T for i in range(2)], axis=0
    )
    logits = dot(x, router_ref[...], 1, 0)
    logits = jnp.where(code > 0.5, logits, NEG)
    top = jnp.max(logits, axis=1, keepdims=True)
    e = jnp.exp(logits - top)
    kept = jnp.where(code > 1.5, 1.0, 0.0)
    gates = kept * e / jnp.sum(e, axis=1, keepdims=True)
    lane = lax.broadcasted_iota(jnp.int32, gates.shape, 1)
    for copy in arrived:
        copy.wait()
    copy = pltpu.make_async_copy(g_held, grad_rows_ref.at[pl.ds(first, rows)], row_sem.at[1])
    copy.start()
    stores.append(copy)
    g = g_held[...]
    mix = None
    back = None
    for n in range(count):
        mine = lane == at_ref[0] + n
        weight = jnp.sum(jnp.where(mine, gates, 0.0), axis=1, keepdims=True)
        keep = jnp.sum(jnp.where(mine, kept, 0.0), axis=1, keepdims=True)
        loaded(n, 2)
        grad = dot(g, weights[2][n], 1, 0)
        loaded(n, 0)
        gate_pre = dot(x, weights[0][n], 1, 0)
        loaded(n, 1)
        up_pre = dot(x, weights[1][n], 1, 0)
        sig = 1.0 / (1.0 + jnp.exp(-gate_pre))
        silu = gate_pre * sig
        act = (silu * up_pre).astype(BF).astype(F32)
        pair_dot = jnp.sum(act * grad, axis=1, keepdims=True) * keep
        dot_ref[n : n + 1, :] = pair_dot.T
        weighted = (act * weight).astype(BF)
        grad = grad * weight
        dgate = (grad * up_pre * sig * (1.0 + gate_pre * (1.0 - sig))).astype(BF)
        dup = (grad * silu).astype(BF)
        for i, value in enumerate((weighted, dgate, dup)):
            held[i][n] = value
            copy = pltpu.make_async_copy(
                held[i].at[n], kept_refs[i].at[n, pl.ds(first, rows)], held_sem.at[n * 3 + i]
            )
            copy.start()
            stores.append(copy)
        m = dot(weighted, weights[2][n], 1, 1)
        mix = m if mix is None else mix + m
        b = dot(dgate, weights[0][n], 1, 1) + dot(dup, weights[1][n], 1, 1)
        back = b if back is None else back + b
    mix = mix.astype(BF)
    mix_a_ref[...] = mix[:half]
    mix_b_ref[...] = mix[half:]
    back = back.astype(BF)
    back_a_ref[...] = back[:half]
    back_b_ref[...] = back[half:]
    for copy in stores:
        copy.wait()


def expert_step(k, steps, local, at, x, packets, router, weights, buffers):
    width = x[0].shape[1]
    extra = -(-router.shape[1] // 16) * 16
    half = x[0].shape[0]
    rows = 2 * half
    count = len(weights)
    hidden = sum(w.shape[2] for w in weights[0])
    half_shape = jax.ShapeDtypeStruct((half, width), BF)
    big_shapes = [jax.ShapeDtypeStruct((steps * rows, width), BF)] * 2
    big_shapes += [jax.ShapeDtypeStruct((count, steps * rows, hidden), BF)] * 3
    operands = [at, *x, packets, router, *[b for w in weights for b in w]]
    specs = [SMEM, ANY, ANY, ANY, VMEM] + [ANY] * (len(operands) - 5)
    aliases = {}
    if buffers is not None:
        aliases = {len(operands) + i: 5 + i for i in range(5)}
        operands += buffers
        specs += [ANY] * 5
    blocks = [len(w) for w in weights]
    out = pl.pallas_call(
        functools.partial(expert_kernel, k * rows, blocks, buffers is None, local),
        out_shape=[half_shape] * 4 + [jax.ShapeDtypeStruct((count, rows), F32)] + big_shapes,
        in_specs=specs,
        out_specs=[VMEM] * 5 + [ANY] * 5,
        input_output_aliases=aliases,
        scratch_shapes=[
            [pltpu.VMEM((count, width, hidden), BF)] * 3,
            [pltpu.VMEM((count, rows, hidden), BF)] * 3,
            pltpu.VMEM((rows, width), BF),
            pltpu.VMEM((rows, width), BF),
            pltpu.VMEM((2, extra, width), BF),
            pltpu.SemaphoreType.DMA((3 * sum(blocks),)),
            pltpu.SemaphoreType.DMA((count * 3,)),
            pltpu.SemaphoreType.DMA((2,)),
            pltpu.SemaphoreType.DMA((6,)),
        ],
        compiler_params=pltpu.CompilerParams(vmem_limit_bytes=40 * MIB),
        cost_estimate=pl.CostEstimate(
            flops=2 * rows * width * hidden * count * 6,
            bytes_accessed=6 * width * hidden * count + 10 * rows * width,
            transcendentals=rows * hidden * count,
        ),
        name="expert_step",
    )(*operands)
    return out[:2], out[2:4], out[4], out[5:]


def expert_grad_kernel(act_ref, dgate_ref, dup_ref, x_ref, g_ref, *outs):
    half, _, _, unit = outs[0].shape
    for i, (rows, ref) in enumerate(((x_ref, dgate_ref), (x_ref, dup_ref), (g_ref, act_ref))):
        grad = dot(rows[...], ref[0], 0, 0).astype(BF)
        for j in range(2 * half):
            outs[j // half][j % half, i] = grad[:, j * unit : (j + 1) * unit]


def expert_grads(kept, x, g, parts, expert):
    _, rows, hidden = kept[0].shape
    width = x.shape[1]
    unit = hidden // parts
    tile = 512 if width % 512 == 0 else width
    half = parts // 2
    return list(pl.pallas_call(
        expert_grad_kernel,
        grid=(width // tile,),
        out_shape=[jax.ShapeDtypeStruct((half, 3, width, unit), BF)] * 2,
        in_specs=[pl.BlockSpec((1, rows, hidden), lambda i: (expert, 0, 0))] * 3
        + [pl.BlockSpec((rows, tile), lambda i: (0, i))] * 2,
        out_specs=[pl.BlockSpec((half, 3, tile, unit), lambda i: (0, 0, i, 0))] * 2,
        compiler_params=pltpu.CompilerParams(vmem_limit_bytes=56 * MIB),
        cost_estimate=pl.CostEstimate(
            flops=6 * rows * width * hidden,
            bytes_accessed=12 * width * hidden,
            transcendentals=0,
        ),
        name="expert_grads",
    )(*kept, x, g))


def finish_kernel(terms, *refs):
    ins, outs = refs[: len(refs) - 3], refs[len(refs) - 3 :]
    for n in range(len(ins) // terms):
        refs = ins[n * terms : (n + 1) * terms]
        for i in range(3):
            total = refs[-1][i].astype(F32)
            for ref in refs[:-1]:
                total = total + ref[0, i].astype(F32)
            outs[i][n] = total.T if i == 2 else total


def finish_grads(sums):
    count = len(sums)
    _, width, unit = sums[0][1].shape
    terms = len(sums[0][0]) + 1
    first = pl.BlockSpec((1, 3, width, unit), lambda i: (0, 0, 0, 0))
    specs = [first] * (terms - 1) + [pl.BlockSpec((3, width, unit), lambda i: (0, 0, 0))]
    shapes = [(count, width, unit), (count, width, unit), (count, unit, width)]
    return list(
        pl.pallas_call(
            functools.partial(finish_kernel, terms),
            grid=(1,),
            out_shape=[jax.ShapeDtypeStruct(v, F32) for v in shapes],
            in_specs=specs * count,
            out_specs=[pl.BlockSpec(v, lambda i: (0, 0, 0)) for v in shapes],
            compiler_params=pltpu.CompilerParams(vmem_limit_bytes=48 * MIB),
            name="finish_grads",
        )(*[v for near, across in sums for v in (*near, across)])
    )


def tree_moves():
    rows, cols = lax.axis_size("row"), lax.axis_size("col")
    if rows == 2 and cols == 2:
        swap = [(0, 1), (1, 0)]
        me = lax.axis_index("row") * 2 + lax.axis_index("col")

        def gather(x, again=None, finish=True):
            across = lax.ppermute(x if again is None else again, "row", swap)
            beside = lax.ppermute(x, "col", swap)
            blocks = [x, across, beside]
            return finish_gather(blocks) if finish else blocks

        def finish_gather(blocks):
            return blocks + [lax.ppermute(blocks[1], "col", swap)]

        def reduce_first(mine, other):
            return [mine, lax.ppermute(other, "col", swap)]

        def reduce_second(mine, came):
            far = (mine[1].astype(F32) + came[1].astype(F32)).astype(BF)
            return [mine, came], lax.ppermute(far, "row", swap)

        reduce = (reduce_first, reduce_second)

        return [me, me ^ 2, me ^ 1, me ^ 3], gather, finish_gather, reduce

    count = rows * cols
    both = ("row", "col")

    def gather(x, again=None, finish=True):
        whole = lax.all_gather(x if again is None else again, both, axis=0)
        return [whole[i] for i in range(count)]

    def reduce_second(mine, other):
        blocks = jnp.concatenate([mine, other], axis=0)
        total = lax.psum_scatter(blocks, both, scatter_dimension=0)
        return [total[None]], jnp.zeros_like(total)

    reduce = (lambda mine, other: [mine, other], reduce_second)

    return [jnp.int32(i) for i in range(count)], gather, list, reduce


def half_orders(count):
    ys = count // 4
    near = [y for y in range(ys)] + [ys + y for y in reversed(range(ys))]
    return [near, [partner_of(i, count) for i in near]]


def partner_of(index, count):
    ys = count // 4
    return (3 - index // ys) * ys + index % ys


def ring_order(count):
    ys = count // 4
    order = []
    for y in range(ys):
        zs = range(4) if y % 2 == 0 else reversed(range(4))
        order += [z * ys + y for z in zs]
    return order


def ring_move(x, order, by):
    n = len(order)
    return lax.ppermute(x, "dp", [(order[i], order[(i + by) % n]) for i in range(n)])


def add_halves(came, own, last):
    total = [c.astype(F32) + n.astype(F32) for c, n in zip(came, own)]
    if last:
        return [jnp.concatenate(total, axis=0)]
    return list(tie(*[t.astype(BF) for t in total]))


def walk_hops(parts, order):
    n = len(order)
    a, b = parts[1]
    for k in range(1, n):
        came = yield [ring_move(a, order, 1), ring_move(b, order, -1)]
        total = add_halves(came, parts[(k + 1) % n], k == n - 1)
        if k < n - 1:
            a, b = total
    yield total


class Ring:
    def __init__(self, count, dp_index):
        self.orders = half_orders(count)
        self.steps = len(self.orders[0])
        at = [[o.index(i) for o in self.orders if i in o][0] for i in range(count)]
        self.place = jnp.array(at, jnp.int32)[dp_index]
        self.four = self.steps == 4
        if self.four:
            self.places = [lax.rem(self.place + k, 4) for k in (0, 3, 1, 2)]
        else:
            self.places = [jnp.int32(k) for k in range(self.steps)]

    def shift(self, x, by):
        n = self.steps
        return lax.ppermute(
            x, "dp", [(o[i], o[(i + by) % n]) for o in self.orders for i in range(n)]
        )

    def gather(self, x):
        if not self.four:
            whole = lax.all_gather(x, "dp", axis=0, axis_index_groups=self.orders)
            return [[whole[k]] for k in range(self.steps)]
        return self.gather_second(x, self.gather_first(x))

    def gather_first(self, x):
        return [self.shift(x, 1), self.shift(x, -1)] if self.four else [x]

    def gather_second(self, x, came):
        if not self.four:
            return self.gather(x)
        half = x.shape[0] // 2
        left, right = came
        a, b = right[:half], left[half:]
        return [[x], [left], [right], [self.shift(a, -1), self.shift(b, 1)]]

    def reduce_stages(self, parts):
        if not self.four:
            yield []
            whole = jnp.stack([jnp.concatenate(p, axis=0) for p in parts])
            yield lax.psum_scatter(
                whole, "dp", scatter_dimension=0, axis_index_groups=self.orders
            ).astype(F32)
            return
        (own,), (left,), (right,), (far_a, far_b) = parts
        half = far_a.shape[0]
        a, b = yield [self.shift(far_a, 1), self.shift(far_b, -1)]
        right = jnp.concatenate(
            [(right[:half].astype(F32) + a.astype(F32)).astype(BF), right[half:]], axis=0
        )
        left = jnp.concatenate(
            [left[:half], (left[half:].astype(F32) + b.astype(F32)).astype(BF)], axis=0
        )
        yield own.astype(F32) + (
            self.shift(right, 1).astype(F32) + self.shift(left, -1).astype(F32)
        )

    def reduce(self, parts):
        stages = self.reduce_stages(parts)
        return stages.send(next(stages))


def small_sum(value, part):
    sizes = [lax.axis_size(name) for name in ("dp", "row", "col")]
    if sizes != [8, 2, 2]:
        return lax.psum(value, ("col", "row", "dp")[part]) if part < 3 else value
    hops = [[("col", 2, 1), ("dp", 8, 1)], [("row", 2, 1)], [("dp", 8, 2)], [("dp", 8, 4)]]
    for name, size, bit in hops[part]:
        value = value + lax.ppermute(value, name, [(i, i ^ bit) for i in range(size)])
    return value


def write_kernel(spans, sizes, turned, place_ref, *refs):
    pieces, outs = refs[: sum(sizes)], refs[sum(sizes) :]
    at = 0
    for k, size in enumerate(sizes):
        chunk = jnp.concatenate([ref[...] for ref in pieces[at : at + size]], axis=0).astype(F32)
        rows = chunk.shape[0]
        at += size
        for n, ((a, b), out) in enumerate(zip(spans, outs)):
            if n == turned:
                start = pl.multiple_of(place_ref[k] * rows, 128)
                out[:, pl.ds(start, rows)] = chunk[:, a:b].T
            else:
                start = pl.multiple_of(place_ref[k] * rows, 16)
                out[pl.ds(start, rows), :] = chunk[:, a:b]


def sum_over_dp(parts, spans, ring, pairs):
    rows = parts[0].shape[0]
    chunk = rows // ring.steps

    def cut(place, at, size):
        return jnp.concatenate(
            [lax.dynamic_slice(v, (place * chunk + at, 0), (size, v.shape[1])) for v in parts],
            axis=1,
        )

    terms = [[cut(place, 0, chunk)] for place in ring.places]
    if ring.four:
        half = chunk // 2
        terms[3] = [cut(ring.places[3], 0, half), cut(ring.places[3], half, half)]
    stages = ring.reduce_stages(terms)
    total = stages.send((yield next(stages)))
    total = (yield [total])[0].astype(BF)
    came = (yield [lax.ppermute(total, "dp", pairs)])[0]
    total = (total.astype(F32) + came.astype(F32)).astype(BF)
    pieces = ring.gather_second(total, (yield ring.gather_first(total)))
    pieces[-1] = yield pieces[-1]
    sizes = [len(p) for p in pieces]
    turned = len(spans) - 1 if chunk % 128 == 0 else None
    shapes = [
        jax.ShapeDtypeStruct((b - a, rows) if n == turned else (rows, b - a), F32)
        for n, (a, b) in enumerate(spans)
    ]
    sums = list(
        pl.pallas_call(
            functools.partial(write_kernel, spans, sizes, turned),
            out_shape=shapes,
            in_specs=[SMEM] + [VMEM] * sum(sizes),
            out_specs=[VMEM] * len(spans),
            compiler_params=pltpu.CompilerParams(vmem_limit_bytes=32 * MIB),
            name="write_grads",
        )(jnp.stack(ring.places).astype(jnp.int32), *[p for pair in pieces for p in pair])
    )
    if turned is None:
        sums[-1] = sums[-1].T
    yield sums


def rms_scale(values):
    return lax.rsqrt(jnp.mean(values * values, axis=-1, keepdims=True) + EPS)


def norm_back(grad_normed, values, scale_rows, gain):
    weighted = grad_normed * gain
    grad_gain = jnp.sum(grad_normed * values * scale_rows, axis=0)
    inner = jnp.mean(weighted * values, axis=-1, keepdims=True)
    return (
        scale_rows * weighted - values * scale_rows * scale_rows * scale_rows * inner,
        grad_gain,
    )


def shards_program(
    tokens, attn_gain, query_weight, key_weight, value_weight, out_weight, mlp_gain, router_weight,
    gate_weight, up_weight, down_weight, output_grad, expert_ids, slot_rank, segment_ids, parent_ids,
):
    local_rows, width = tokens.shape
    half = local_rows // 2
    dp_size = lax.axis_size("dp")
    dp_index = lax.axis_index("dp")
    pairs = [(i, partner_of(i, dp_size)) for i in range(dp_size)]
    ring = Ring(dp_size, dp_index)
    shards, tree_gather, tree_finish, (reduce_first, reduce_second) = tree_moves()

    def tree_reduce(mine, other):
        return reduce_second(*reduce_first(mine, other))

    count = len(shards)
    shard_ids = jnp.stack(shards).astype(jnp.int32)
    kv = key_weight.shape[1] // HD
    per_group = query_weight.shape[1] // key_weight.shape[1]
    q_width = query_weight.shape[1]
    k_width = key_weight.shape[1]
    experts_local = gate_weight.shape[0]
    unit = gate_weight.shape[2]
    experts = experts_local * dp_size
    capacity = 5 * local_rows * TOPK // (4 * experts)
    seg = local_rows * count // 20

    token_values = tokens.astype(F32)
    scale_attn = rms_scale(token_values)
    normed = (token_values * scale_attn * attn_gain).astype(BF)
    step = math.gcd(seg, local_rows)
    each = local_rows // step
    labels = jnp.stack([segment_ids[::step], parent_ids[::step]]).astype(BF)
    normed_packet = jnp.concatenate(
        [normed, jnp.pad(labels, ((0, 14), (0, width - each)))], axis=0
    )
    tree_normed = tree_gather(normed_packet)
    labels = jnp.concatenate([v[local_rows : local_rows + 2, :each] for v in tree_normed], axis=1)
    spots = jnp.concatenate([s * each + jnp.arange(each, dtype=jnp.int32) for s in shards])
    spots = spots.astype(jnp.int32)
    block_spot = spots * step // seg
    is_parent = (labels[0][None, :] == labels[1][:, None]) & (labels[1][:, None] > 0)
    parent_spot = jnp.max(jnp.where(is_parent, block_spot[None, :], 0), axis=1)
    natural = jnp.arange(20, dtype=jnp.int32) * (seg // step)
    parent_block = jnp.sum(
        jnp.where(spots[None, :] == natural[:, None], parent_spot[None, :], 0), axis=1
    ).astype(jnp.int32)

    columns = jnp.arange(experts, dtype=jnp.int32)
    unranked = local_rows * TOPK
    rank = jnp.min(
        jnp.where(
            expert_ids.T[:, None, :] == columns[None, :, None], slot_rank.T[:, None, :], unranked
        ),
        axis=0,
    )
    slot = jnp.sum((rank[:, :, None] < rank[:, None, :]).astype(jnp.int32), axis=1)
    code = jnp.where(rank == unranked, 0.0, jnp.where(slot < capacity, 2.0, 1.0))
    extra = -(-experts // 16) * 16
    packet = []
    for at in (0, half):
        lanes = ((0, extra - experts), (0, width - half))
        packet += [output_grad[at : at + half], jnp.pad(code[:, at : at + half].astype(BF), lanes)]
    packet = jnp.concatenate(packet, axis=0)
    packets = lax.all_gather(packet, "dp", axis=0, tiled=True)
    tree_normed[1], packet = tie(tree_normed[1], packet)

    raw = [
        jnp.stack([gate_weight[n], up_weight[n], down_weight[n].T]) for n in range(experts_local)
    ]

    def joined(blocks):
        return blocks if unit % 128 == 0 else [jnp.concatenate(blocks, axis=2)]

    weights = [tree_gather(raw[0])]
    qkv_weight = jnp.concatenate([query_weight, key_weight, value_weight], axis=1)
    qkv_blocks = [
        jnp.dot(block, qkv_weight, preferred_element_type=F32).astype(BF) for block in tree_normed
    ]
    qkv, heads, normed_rows = attend_forward(
        shard_ids, parent_block, qkv_blocks, tree_normed, kv, per_group, seg
    )
    heads, weights[0][1] = tie(heads, weights[0][1])
    def by_shard(rows, weight):
        result = jnp.dot(rows, weight, preferred_element_type=F32).astype(BF)
        return result.reshape(-1, local_rows, width)

    middle = (count + 1) // 2 * local_rows
    attn_near, attn_far = tree_reduce(
        *tie(by_shard(heads[:middle], out_weight), by_shard(heads[middle:], out_weight))
    )
    attn_far, *later = tie(attn_far, *raw[1:], *weights[0][2:])
    weights[0][2:] = later[len(raw) - 1 :]
    weights += [tree_gather(v, again, False) for v, again in zip(raw[1:], later)]
    hidden = token_values + attn_far.astype(F32) + sum(v[0].astype(F32) for v in attn_near)
    scale_mlp = rms_scale(hidden)
    mlp_in = (hidden * scale_mlp * mlp_gain).astype(BF)

    order = ring_order(dp_size)
    all_places = jnp.array([order.index(i) for i in range(dp_size)], jnp.int32)
    place = all_places[dp_index]
    walk = jnp.array(order, jnp.int32)
    steps = jnp.arange(dp_size, dtype=jnp.int32)
    at = jnp.stack(
        [
            jnp.full_like(steps, dp_index * experts_local),
            walk[(place - steps) % dp_size],
            walk[(place + steps) % dp_size],
        ],
        axis=1,
    ).astype(jnp.int32)
    x = [mlp_in[:half], mlp_in[half:]]
    kept = None
    backs, mixes, dots, came = [], [], [], []
    coming = [ring_move(x[0], order, 1), ring_move(x[1], order, -1)]
    weights[1:] = [tree_finish(blocks) for blocks in weights[1:]]
    weights = [joined(blocks) for blocks in weights]
    for k in range(dp_size):
        if k > 0:
            x = coming
            if k > 1:
                x = [ring_move(x[0], order, 1), ring_move(x[1], order, -1)]
            *x, dots[k - 1] = tie(*x, dots[k - 1])
            if k > 2:
                *x, came[k - 2][0], came[k - 2][1] = tie(*x, *came[k - 2])
            coming = x
        back, mix, pair_dot, kept = expert_step(
            k,
            dp_size,
            k == 0,
            at[k],
            x,
            packets if k > 0 else packet,
            router_weight,
            weights,
            kept,
        )
        backs.append(back)
        mixes.append(list(mix))
        dots.append(pair_dot)
        came.append(None)
        if k > 0:
            if k > 1:
                *came[k - 1], dots[k] = tie(*came[k - 1], dots[k])
                back = add_halves(came[k - 1], back, False)
            if k == dp_size - 1:
                *back, mixes[1][0], mixes[1][1] = tie(*back, *mixes[1])
            came[k] = [ring_move(back[0], order, 1), ring_move(back[1], order, -1)]
    all_rows, all_grads, *factors = kept
    mlp_in, code, dots[-1] = tie(mlp_in, code, dots[-1])
    (grad_rows,) = add_halves(came[-1], backs[0], True)
    hops = walk_hops(mixes, order)
    hop = next(hops)
    left = dp_size - 1

    def next_hop(*values):
        nonlocal hop, left
        if left == 0:
            return values
        *values, a, b = tie(*values, *hop)
        hop = hops.send([a, b])
        left -= 1
        return values


    all_dots = jnp.stack(dots)

    def pick(index):
        return jnp.sum(
            jnp.where((index[:, None] == steps[None, :])[:, :, None, None], all_dots[None], 0.0),
            axis=1,
        )

    send = jnp.where(
        jnp.arange(local_rows) < half,
        pick((place - all_places) % dp_size),
        pick((all_places - place) % dp_size),
    )
    grad_gates = lax.all_to_all(send, "dp", 0, 0, tiled=True).reshape(experts, local_rows).T

    code_here = code.T
    logits = jnp.dot(mlp_in, router_weight, preferred_element_type=F32)
    logits = jnp.where(code_here > 0.5, logits, NEG)
    chosen_exp = jnp.exp(logits - jnp.max(logits, axis=1, keepdims=True))
    gates = chosen_exp / jnp.sum(chosen_exp, axis=1, keepdims=True)
    weighted_sum = jnp.sum(gates * grad_gates, axis=1, keepdims=True)
    grad_logits = (gates * (grad_gates - weighted_sum)).astype(BF)
    router_part = jnp.dot(mlp_in.T, grad_logits, preferred_element_type=F32)
    grad_mlp_in = grad_rows + jnp.dot(grad_logits, router_weight.T, preferred_element_type=F32)
    grad_hidden_norm, mlp_gain_part = norm_back(grad_mlp_in, hidden, scale_mlp, mlp_gain)
    grad_hidden = output_grad.astype(F32) + grad_hidden_norm
    grad_attn = grad_hidden.astype(BF)

    grad_attn, *factors = next_hop(*tie(grad_attn, *factors))
    grad_blocks = tree_gather(grad_attn)
    expert_parts = [expert_grads(factors, all_rows, all_grads, count, 0)]
    grad_blocks[1], expert_parts[0][1] = next_hop(*tie(grad_blocks[1], expert_parts[0][1]))
    expert_sums = [tree_reduce(*expert_parts[0])]
    grad_head_blocks = [
        jnp.dot(block, out_weight.T, preferred_element_type=F32).astype(BF) for block in grad_blocks
    ]
    (grad_head_blocks[-1],) = next_hop(grad_head_blocks[-1])
    dqkv = attend_backward(
        shard_ids, parent_block, qkv, grad_head_blocks, kv, per_group, seg
    )
    near, across = expert_sums[0]
    dqkv, across, *factors = next_hop(*tie(dqkv, across, *factors))
    expert_sums[0] = (near, across)
    qkv_part = jnp.dot(normed_rows.T, dqkv, preferred_element_type=F32).astype(BF)
    out_rows = jnp.concatenate(grad_blocks, axis=0)
    out_part = jnp.dot(out_rows.T, heads, preferred_element_type=F32).astype(BF)
    spans = (
        (0, q_width),
        (q_width, q_width + k_width),
        (q_width + k_width, q_width + 2 * k_width),
        (q_width + 2 * k_width, 2 * q_width + 2 * k_width),
    )
    stages = sum_over_dp([qkv_part, out_part], spans, ring, pairs)
    came = next(stages)
    spread = qkv_weight.T
    normed_near, normed_far = tree_reduce(
        by_shard(dqkv[:middle], spread), by_shard(dqkv[middle:], spread)
    )

    *came, factors[0] = next_hop(*tie(*came, factors[0]))
    came = stages.send(came)
    expert_parts += [
        expert_grads(factors, all_rows, all_grads, count, n) for n in range(1, experts_local)
    ]
    *came, normed_far, expert_parts[-1][1] = next_hop(
        *tie(*came, normed_far, expert_parts[-1][1])
    )
    came = stages.send(came)
    grad_normed = normed_far.astype(F32) + sum(v[0].astype(F32) for v in normed_near)
    grad_token_norm, attn_gain_part = norm_back(grad_normed, token_values, scale_attn, attn_gain)
    input_grad = grad_hidden + grad_token_norm
    small = jnp.concatenate(
        [router_part.T, mlp_gain_part.reshape(1, -1), attn_gain_part.reshape(1, -1)], axis=0
    )
    small = small_sum(small, 0)
    expert_sums += [tree_reduce(*p) for p in expert_parts[1:]]
    near, across = expert_sums[-1]
    across, small, *came = next_hop(*tie(across, small, *came))
    expert_sums[-1] = (near, across)
    while left > 0:
        next_hop()
    output = (hidden + hop[0]).astype(BF)
    came = stages.send(came)
    small = small_sum(small, 1)
    near, across = expert_sums[-1]
    across, *came = tie(across, *came)
    expert_sums[-1] = (near, across)
    came = stages.send(came)
    expert_grad = finish_grads(expert_sums)
    small = small_sum(small, 2)
    small, expert_grad[0], *came = tie(small, expert_grad[0], *came)
    query_grad, key_grad, value_grad, out_grad = stages.send(came)
    small = small_sum(small, 3)
    return (
        output,
        input_grad,
        small[experts + 1],
        query_grad,
        key_grad,
        value_grad,
        out_grad,
        small[experts],
        small[:experts].T,
        expert_grad[0],
        expert_grad[1],
        expert_grad[2],
    )


def solution(mesh):
    every = ("dp", "row", "col")
    tree = ("row", "col")
    return jax.shard_map(
        shards_program,
        mesh=mesh,
        in_specs=(
            P(every, None),
            P(),
            P(None, tree),
            P(None, tree),
            P(None, tree),
            P(tree, None),
            P(),
            P(),
            P("dp", None, tree),
            P("dp", None, tree),
            P("dp", tree, None),
            P(every, None),
            P(every, None),
            P(every, None),
            P(every),
            P(every),
        ),
        out_specs=(
            P(every, None),
            P(every, None),
            P(),
            P(None, tree),
            P(None, tree),
            P(None, tree),
            P(tree, None),
            P(),
            P(),
            P("dp", None, tree),
            P("dp", None, tree),
            P("dp", tree, None),
        ),
        check_vma=False,
    )
```
